128 devices in a mesh: tile: 8 (over x, core), scan: 16 (over y, z).
Axes of the slice: x: 4, y: 4, z: 4, core: 2. Of those that a mesh axis runs over, the one named last changes fastest.
Arguments:
- specimen: float32 [2, 2048, 4096], P(None, 'tile', 'scan'), may hold values from -6 to 6
- sampler_noise: float32 [2, 2048, 4096], P(None, 'tile', 'scan'), may hold values from -6 to 6
- probe_field: float32 [2, 256, 256], replicated, may hold values from -6 to 6
- amplitudes: bfloat16 [8, 16, 16, 2, 256, 256], P('tile', 'scan'), may hold values from 0.5 to 4
- corner_rows: int32 [8, 16, 16, 2], P('tile', 'scan'), may hold values from 0 to 256
- corner_cols: int32 [8, 16, 16, 2], P('tile', 'scan'), may hold values from 0 to 256
- slot_counts: int32 [8, 16, 16], P('tile', 'scan'), may hold values from 0 to 2, as said below
- first_weight: bfloat16 [128, 18], replicated, may hold values from -1.5 to 1.5
- first_bias: float32 [128], replicated, may hold values from -3 to 3
- second_weight: bfloat16 [18, 128], replicated, may hold values from -0.1875 to 0.1875
- second_bias: float32 [2], replicated, may hold values from -3 to 3
Outputs:
- updated: float32 [2, 2048, 4096], P(None, 'tile', 'scan')
The draws below stay inside these ranges and needn't reach their ends.
Inputs may be any that keep to these rules, and one draw needn't show every extreme that they name: slot_counts[t,s,s] = 2 for every band t and block column s; slots c < slot_counts[t,s,h] are the live ones.
All inputs are finite; a program needn't handle non-finite values.
Results may differ from the reference program's by a relative error of at most 0.011.
Values may be sent and summed in bfloat16 or wider, within the bound.
A program may use at most 128 MiB of HBM per device.

```python
import math
import jax
import jax.numpy as jnp
from jax import lax

PATCH = 256
HIDDEN_SIZE = 128
RB = 256
CB = 256
CAP = 2
BANDS = 8
PEERS = 16
NR = 2048
NC = 4096


def draw_slot_counts(key, part):
    key = jax.random.fold_in(key, 11)
    heat_key, load_key = jax.random.split(key)
    heated = jax.random.randint(heat_key, (BANDS, PEERS, 1), 0, 4) == 0
    light = jax.random.randint(load_key, (BANDS, PEERS, PEERS), 0, CAP)
    loads = jnp.where(heated, CAP, light)
    same_block = jnp.arange(PEERS)[:, None] == jnp.arange(PEERS)[None, :]
    return jnp.where(same_block[None], CAP, loads).astype(jnp.int32)


def place_ends(values, rng, smallest, high):
    spot = [jax.random.randint(jax.random.fold_in(rng, axis), (), 0, length) for axis, length in enumerate(values.shape)]
    longest = values.shape.index(max(values.shape))
    neighbour = spot[:longest] + [(spot[longest] + 1) % values.shape[longest]] + spot[longest + 1:]
    return values.at[tuple(spot)].set(smallest).at[tuple(neighbour)].set(high)


def steps_of(rng, dims, cuts, smallest, largest):
    def one(dim, shards_of):
        heights = jax.random.uniform(jax.random.fold_in(jax.random.fold_in(rng, 6), dim), (shards_of,), jnp.float32, smallest / len(cuts), largest / len(cuts))
        return jnp.repeat(jnp.exp(heights), dims[dim] // shards_of).reshape((-1,) + (1,) * (len(dims) - dim - 1))

    level = one(*cuts[0])
    for cut in cuts[1:]:
        level = level * one(*cut)
    return level


def centred(key, extent, deviation, bound, cuts=(), kind=jnp.bfloat16):
    factor_of = steps_of(key, extent, cuts, -0.22, 0.18) if cuts else 1.0
    drawn = jax.random.normal(key, extent, jnp.float32) * deviation * factor_of
    return jnp.minimum(jnp.maximum(drawn, -bound), bound).astype(kind)


def setup_inputs(seed: int = 0) -> dict:
    key_of = jax.random.split(jax.random.key(seed), 12)
    return {
        "specimen": centred(key_of[0], (2, NR, NC), 1.0, 6.0, ((1, 8), (2, 16)), jnp.float32),
        "sampler_noise": centred(key_of[1], (2, NR, NC), 1.0, 6.0, ((1, 8), (2, 16)), jnp.float32),
        "probe_field": centred(key_of[2], (2, PATCH, PATCH), 1.0, 6.0, (), jnp.float32),
        "amplitudes": jnp.clip(jnp.exp(math.log(4.0) - 2.0794415 * jax.random.uniform(key_of[3], (BANDS, PEERS, PEERS, CAP, PATCH, PATCH), jnp.float32) ** steps_of(key_of[3], (BANDS, PEERS, PEERS, CAP, PATCH, PATCH), ((0, 8), (1, 16)), -0.2, 0.2)), 0.5, 4.0).astype(jnp.bfloat16),
        "corner_rows": place_ends(jax.random.randint(key_of[4], (BANDS, PEERS, PEERS, CAP), 0, RB + 1), jax.random.fold_in(key_of[4], 1), 0, RB).astype(jnp.int32),
        "corner_cols": place_ends(jax.random.randint(key_of[5], (BANDS, PEERS, PEERS, CAP), 0, CB + 1), jax.random.fold_in(key_of[5], 1), 0, CB).astype(jnp.int32),
        "slot_counts": draw_slot_counts(jax.random.fold_in(key_of[11], 71), 0),
        "first_weight": centred(key_of[7], (HIDDEN_SIZE, 18), 18 ** -0.5, 1.5),
        "first_bias": centred(key_of[8], (HIDDEN_SIZE,), 0.5, 3.0, (), jnp.float32),
        "second_weight": centred(key_of[9], (18, HIDDEN_SIZE), (9 * HIDDEN_SIZE) ** -0.5, 0.1875),
        "second_bias": centred(key_of[10], (2,), 0.5, 3.0, (), jnp.float32),
    }


step_size = 0.25
noise_scale = 0.5
amplitude_floor = 1.0

def dft_tables(width):
    index = jnp.arange(width, dtype=jnp.int32)
    phase = index[:, None] * index[None, :] % width
    angle = phase.astype(jnp.float32) * (2.0 * math.pi / width)
    norm = 1.0 / math.sqrt(width)
    return ((jnp.cos(angle) * norm).astype(jnp.bfloat16), (jnp.sin(angle) * norm).astype(jnp.bfloat16))

def transform(real_part, imag_part, cosine_table, sine_table, sign):
    width = cosine_table.shape[0]
    left = jnp.concatenate([cosine_table, sine_table], 0).astype(jnp.float32)
    left_real = jnp.einsum('jk,nkl->njl', left, real_part.astype(jnp.float32))
    left_imag = jnp.einsum('jk,nkl->njl', left, imag_part.astype(jnp.float32))
    mid_real = (left_real[:, :width] + sign * left_imag[:, width:]).astype(jnp.bfloat16)
    mid_imag = (left_imag[:, :width] - sign * left_real[:, width:]).astype(jnp.bfloat16)
    right = jnp.concatenate([cosine_table, sine_table], 1).astype(jnp.float32)
    right_real = jnp.einsum('njk,kl->njl', mid_real.astype(jnp.float32), right)
    right_imag = jnp.einsum('njk,kl->njl', mid_imag.astype(jnp.float32), right)
    return (right_real[..., :width] + sign * right_imag[..., width:], right_imag[..., :width] - sign * right_real[..., width:])

def holder_gradients(patches, amps, probe_field, cosine_table, sine_table):
    probe_real, probe_imag = (probe_field[0], probe_field[1])
    patch_real = patches[:, 0].astype(jnp.float32)
    patch_imag = patches[:, 1].astype(jnp.float32)
    exit_real = (probe_real * patch_real - probe_imag * patch_imag).astype(jnp.bfloat16)
    exit_imag = (probe_real * patch_imag + probe_imag * patch_real).astype(jnp.bfloat16)
    far_real, far_imag = transform(exit_real, exit_imag, cosine_table, sine_table, 1.0)
    modulus = jnp.sqrt(far_real * far_real + far_imag * far_imag)
    keep = 1.0 - amps.astype(jnp.float32) / jnp.maximum(modulus, amplitude_floor)
    diff_real = (far_real * keep).astype(jnp.bfloat16)
    diff_imag = (far_imag * keep).astype(jnp.bfloat16)
    wave_real, wave_imag = transform(diff_real, diff_imag, cosine_table, sine_table, -1.0)
    grad_real = probe_real * wave_real + probe_imag * wave_imag
    grad_imag = probe_real * wave_imag - probe_imag * wave_real
    return jnp.stack([grad_real, grad_imag], 1).astype(jnp.bfloat16)

def cut_patches(source, rows, cols, width):

    def one(row, col):
        return lax.dynamic_slice(source, (jnp.int32(0), row, col), (source.shape[0], width, width))
    return jax.vmap(one)(rows, cols)

def add_patches(total, grads, rows, cols, live):

    def one_step(index, total):
        piece = grads[index].astype(jnp.float32) * live[index]
        start = (jnp.int32(0), rows[index], cols[index])
        current = lax.dynamic_slice(total, start, piece.shape)
        return lax.dynamic_update_slice(total, current + piece, start)
    return lax.fori_loop(0, grads.shape[0], one_step, total)

def tap_stack(source, rows, cols):
    pieces = [source[:, shift_row:shift_row + rows, shift_col:shift_col + cols] for shift_row in range(3) for shift_col in range(3)]
    return jnp.stack(pieces, 1).reshape(source.shape[0] * 9, rows, cols)

def hidden_units(taps, first_weight, first_bias):
    groups = (first_weight.reshape(4, -1, first_weight.shape[1]), first_bias.reshape(4, -1))

    def one_group(args):
        weight_part, bias_part = args
        pre = jnp.einsum('ok,kyx->oyx', weight_part.astype(jnp.float32), taps.astype(jnp.float32)) + bias_part[:, None, None]
        return jax.nn.silu(pre).astype(jnp.bfloat16)
    stacked = lax.map(one_group, groups)
    return stacked.reshape(first_weight.shape[0], taps.shape[1], taps.shape[2])

def prior_terms(hidden_ext, second_weight, rows, cols):
    mixed = jnp.einsum('ko,oyx->kyx', second_weight.astype(jnp.float32), hidden_ext.astype(jnp.float32))
    mixed = mixed.reshape(2, 9, rows + 2, cols + 2)
    total = jnp.zeros((2, rows, cols), jnp.float32)
    for shift_row in range(3):
        for shift_col in range(3):
            total = total + mixed[:, shift_row * 3 + shift_col, shift_row:shift_row + rows, shift_col:shift_col + cols]
    return total

def reference(specimen, sampler_noise, probe_field, amplitudes, corner_rows, corner_cols, slot_counts, first_weight, first_bias, second_weight, second_bias):
    half_patch = PATCH // 2
    cosine_table, sine_table = dft_tables(PATCH)
    widened = jnp.pad(specimen.astype(jnp.bfloat16), ((0, 0), (half_patch, half_patch), (half_patch, half_patch)))
    owners = BANDS * PEERS
    amp_owner = jnp.transpose(amplitudes, (0, 2, 1, 3, 4, 5)).reshape(owners, PEERS * CAP, PATCH, PATCH)
    rows_all = corner_rows.reshape(owners, PEERS * CAP)
    cols_all = corner_cols.reshape(owners, PEERS * CAP)
    live_all = (jnp.arange(CAP, dtype=jnp.int32)[None, None, None, :] < slot_counts[..., None]).astype(jnp.float32).reshape(owners, PEERS * CAP)

    def owner_step(total, inputs):
        owner_index, amps, rows, cols, live = inputs
        base_row = owner_index // PEERS * RB
        base_col = owner_index % PEERS * CB
        patch_rows = (base_row + rows).astype(jnp.int32)
        patch_cols = (base_col + cols).astype(jnp.int32)
        patches = cut_patches(widened, patch_rows, patch_cols, PATCH)
        grads = holder_gradients(patches, amps, probe_field, cosine_table, sine_table)
        return (add_patches(total, grads, patch_rows, patch_cols, live), None)
    start = jnp.zeros((2, NR + PATCH, NC + PATCH), jnp.float32)
    total, unused = lax.scan(owner_step, start, (jnp.arange(owners, dtype=jnp.int32), amp_owner, rows_all, cols_all, live_all))
    gradient = total[:, half_patch:half_patch + NR, half_patch:half_patch + NC]
    sampled = specimen - step_size * gradient + noise_scale * sampler_noise
    padded_input = jnp.pad(sampled.astype(jnp.bfloat16), ((0, 0), (2, 2), (2, 2)))
    col_pos = jnp.arange(NC + 2, dtype=jnp.int32) - 1
    col_ok = (col_pos >= 0) & (col_pos < NC)

    def row_block(block_index):
        source = lax.dynamic_slice(padded_input, (jnp.int32(0), block_index * RB, jnp.int32(0)), (2, RB + 4, NC + 4))
        hidden = hidden_units(tap_stack(source, RB + 2, NC + 2), first_weight, first_bias)
        row_pos = block_index * RB - 1 + jnp.arange(RB + 2, dtype=jnp.int32)
        inside = ((row_pos >= 0) & (row_pos < NR))[:, None] & col_ok[None, :]
        hidden = jnp.where(inside[None], hidden, jnp.zeros_like(hidden))
        return prior_terms(hidden, second_weight, RB, NC)
    blocks = lax.map(row_block, jnp.arange(BANDS, dtype=jnp.int32))
    prior_term = jnp.transpose(blocks, (1, 0, 2, 3)).reshape(2, NR, NC)
    return sampled - (prior_term + second_bias[:, None, None])
```

```python
import functools

import jax
import jax.numpy as jnp
import numpy as np
from jax import lax
from jax.experimental import pallas as pl
from jax.experimental.pallas import tpu as pltpu
from jax.sharding import PartitionSpec as P

MESH = pl.DeviceIdType.MESH
NW = 256
HALF = 128
EDGE = 16
WIDE = 384
CAP = 2

ORDER_16 = [(0, 3), (1, 0), (3, 2), (3, 1), (3, 3), (0, 2), (1, 3), (2, 0), (0, 1), (2, 1), (2, 3), (1, 2), (3, 0), (1, 1), (2, 2)]
SIDES = [(a, b) for a in (-1, 0, 1) for b in (-1, 0, 1) if (a, b) != (0, 0)]


def dft_matrices():
    index = np.arange(NW)
    angle = (index[:, None] * index[None, :] % NW) * (2.0 * np.pi / NW)
    cosine = (np.cos(angle) / 16.0).astype(jnp.bfloat16)
    sine = (np.sin(angle) / 16.0).astype(jnp.bfloat16)
    forward = np.concatenate([np.concatenate([cosine, sine], 1), np.concatenate([-sine, cosine], 1)], 0)
    return forward, np.ascontiguousarray(forward.T)


def span(step, low, mid, high):
    return {-1: low, 0: mid, 1: high}[step]


def patch_kernel(
    order, rows_y, tiles, peers,
    rows_ref, cols_ref, counts_ref, amps_ref, spec_ref, noise_ref, probe_ref, fwd_ref, inv_ref,
    out_ref, cells_ref,
    recv, frame, acc, rim, rim_in, probe2, rolled, wave_in, mid_ref, far_ref,
    amp_send, amp_recv, own_sem, halo_send, halo_recv, rim_send, rim_recv, ring_send, ring_recv,
):
    f32, bf16 = jnp.float32, jnp.bfloat16
    t = lax.axis_index("tile")
    s = lax.axis_index("scan")
    rows_z = peers // rows_y
    y, z = s // rows_z, lax.rem(s, rows_z)

    def peer(dy, dz):
        return lax.rem(y + dy + rows_y, rows_y) * rows_z + lax.rem(z + dz + rows_z, rows_z)

    def exists(dt, ds):
        ok_t = {-1: t > 0, 0: t >= 0, 1: t < tiles - 1}[dt]
        ok_s = {-1: s > 0, 0: s >= 0, 1: s < peers - 1}[ds]
        return jnp.logical_and(ok_t, ok_s)

    barrier = pltpu.get_barrier_semaphore()
    expected = jnp.int32(len(order))
    for dy, dz in order:
        pl.semaphore_signal(barrier, inc=1, device_id=(t, peer(-dy, -dz)), device_id_type=MESH)
    for dt, ds in SIDES:
        if dt != 0:
            here = exists(dt, ds)
            expected = expected + here.astype(jnp.int32)

            @pl.when(here)
            def _():
                pl.semaphore_signal(barrier, inc=1, device_id=(t + dt, s + ds), device_id_type=MESH)

    own = pltpu.make_async_copy(amps_ref.at[s], recv.at[0], own_sem)
    own.start()
    for part in range(2):
        frame[part, HALF : HALF + NW, HALF : HALF + NW] = spec_ref[part].astype(bf16)
    pl.semaphore_wait(barrier, expected)

    def halo_copy(k, dt, ds):
        src = (slice(None), slice(*span(dt, (128, 256), (128, 384), (256, 384))), slice(*span(ds, (128, 256), (128, 384), (256, 384))))
        dst = (slice(None), slice(*span(dt, (384, 512), (128, 384), (0, 128))), slice(*span(ds, (384, 512), (128, 384), (0, 128))))
        return pltpu.make_async_remote_copy(
            src_ref=frame.at[src], dst_ref=frame.at[dst], send_sem=halo_send.at[k], recv_sem=halo_recv.at[k],
            device_id=(t + dt, s + ds), device_id_type=MESH,
        )

    def amp_copy(k, dy, dz):
        d = peer(dy, dz)
        return pltpu.make_async_remote_copy(
            src_ref=amps_ref.at[d], dst_ref=recv.at[k], send_sem=amp_send.at[k], recv_sem=amp_recv.at[k],
            device_id=(t, d), device_id_type=MESH,
        )

    for k, (dt, ds) in enumerate(SIDES):
        @pl.when(exists(dt, ds))
        def _():
            halo_copy(k, dt, ds).start()
    for k, (dy, dz) in enumerate(order):
        amp_copy(k + 1, dy, dz).start()

    for part in range(2):
        acc[part] = jnp.zeros((2 * NW, 2 * NW), f32)
        acc[part, HALF : HALF + NW, HALF : HALF + NW] = spec_ref[part] + 0.5 * noise_ref[part]
        for half in range(2):
            columns = probe_ref[part, :, half * HALF : (half + 1) * HALF]
            probe2[part, half, :NW, :] = columns
            probe2[part, half, NW:, :] = columns

    for k, (dt, ds) in enumerate(SIDES):
        here = exists(-dt, -ds)

        @pl.when(here)
        def _():
            halo_copy(k, dt, ds).wait_recv()

        @pl.when(jnp.logical_not(here))
        def _():
            at_row, at_col = span(dt, (384, 512), (128, 384), (0, 128)), span(ds, (384, 512), (128, 384), (0, 128))
            for part in range(2):
                frame[part, slice(*at_row), slice(*at_col)] = jnp.zeros((at_row[1] - at_row[0], at_col[1] - at_col[0]), bf16)

    own.wait()

    def step(k, carry):
        dy, dz = jnp.int32(0), jnp.int32(0)
        for i, (a, b) in enumerate(order):
            dy = jnp.where(k == i + 1, a, dy)
            dz = jnp.where(k == i + 1, b, dz)
        h = peer(-dy, -dz)
        corner = [(rows_ref[h * CAP + c], cols_ref[h * CAP + c]) for c in range(CAP)]
        scale = [jnp.where(counts_ref[h] > c, f32(-0.25), f32(0.0)) for c in range(CAP)]
        CH = 32
        lane = lax.broadcasted_iota(jnp.int32, (CH, NW), 1)
        sub = lax.broadcasted_iota(jnp.int32, (CH, NW), 0)

        def exits(i, carry):
            base = pl.multiple_of(i * CH, CH)
            for c in range(CAP):
                r, q = corner[c]
                low_row = sub + base < r
                low_col = lane < q
                shift = lax.rem(q, NW)
                cell, prb = [], []
                for part in range(2):
                    tile = [[frame[part, pl.ds(base + a * NW, CH), b * NW : (b + 1) * NW].astype(f32) for b in range(2)] for a in range(2)]
                    cell.append(jnp.where(low_row, jnp.where(low_col, tile[1][1], tile[1][0]), jnp.where(low_col, tile[0][1], tile[0][0])))
                    turned = pltpu.roll(jnp.concatenate([probe2[part, half, pl.ds(base + NW - r, CH), :] for half in range(2)], 1), shift, 1)
                    rolled[c, part, pl.ds(base, CH), :] = turned
                    prb.append(turned)
                wave_in[pl.ds(base, CH), c * NW : (c + 1) * NW] = (prb[0] * cell[0] - prb[1] * cell[1]).astype(bf16)
                wave_in[pl.ds(base + NW, CH), c * NW : (c + 1) * NW] = (prb[0] * cell[1] + prb[1] * cell[0]).astype(bf16)
            return carry

        lax.fori_loop(0, NW // CH, exits, 0)

        def both(left_ref, right_ref):
            for c in range(CAP):
                mid = jnp.dot(left_ref[...], wave_in[:, c * NW : (c + 1) * NW], preferred_element_type=f32)
                for p in range(2):
                    mid_ref[c * NW : (c + 1) * NW, p * NW : (p + 1) * NW] = mid[p * NW : (p + 1) * NW].astype(bf16)
            for p in range(2):
                far_ref[:, p * NW : (p + 1) * NW] = jnp.dot(mid_ref[...], right_ref[:, p * NW : (p + 1) * NW], preferred_element_type=f32)

        both(fwd_ref, inv_ref)

        @pl.when(k > 0)
        def _():
            pltpu.make_async_remote_copy(
                src_ref=recv.at[k], dst_ref=recv.at[k], send_sem=amp_send.at[k], recv_sem=amp_recv.at[k],
                device_id=(t, peer(dy, dz)), device_id_type=MESH,
            ).wait_recv()

        def correct(i, carry):
            base = pl.multiple_of(i * CH, CH)
            for c in range(CAP):
                fr = far_ref[pl.ds(base + c * NW, CH), :NW]
                fi = far_ref[pl.ds(base + c * NW, CH), NW:]
                amp = recv[k, c, pl.ds(base, CH), :].astype(f32)
                keep = 1.0 - amp * lax.rsqrt(jnp.maximum(fr * fr + fi * fi, 1.0))
                wave_in[pl.ds(base, CH), c * NW : (c + 1) * NW] = (fr * keep).astype(bf16)
                wave_in[pl.ds(base + NW, CH), c * NW : (c + 1) * NW] = (fi * keep).astype(bf16)
            return carry

        lax.fori_loop(0, NW // CH, correct, 0)
        both(inv_ref, fwd_ref)

        def gather(i, carry):
            base = pl.multiple_of(i * CH, CH)
            grads = []
            for c in range(CAP):
                wr = far_ref[pl.ds(base + c * NW, CH), :NW]
                wi = far_ref[pl.ds(base + c * NW, CH), NW:]
                pr = rolled[c, 0, pl.ds(base, CH), :] * scale[c]
                pi = rolled[c, 1, pl.ds(base, CH), :] * scale[c]
                grads.append((pr * wr + pi * wi, pr * wi - pi * wr))
            for a in range(2):
                for b in range(2):
                    masks = []
                    for c in range(CAP):
                        r, q = corner[c]
                        row_ok = sub + base < r if a else sub + base >= r
                        col_ok = lane < q if b else lane >= q
                        masks.append(jnp.logical_and(row_ok, col_ok))
                    for part in range(2):
                        total = acc[part, pl.ds(base + a * NW, CH), b * NW : (b + 1) * NW]
                        for c in range(CAP):
                            total = total + jnp.where(masks[c], grads[c][part], 0.0)
                        acc[part, pl.ds(base + a * NW, CH), b * NW : (b + 1) * NW] = total
            return carry

        lax.fori_loop(0, NW // CH, gather, 0)
        return carry

    lax.fori_loop(0, len(order) + 1, step, 0)

    for part in range(2):
        for lo, hi in ((0, HALF), (HALF + NW, 2 * NW)):
            rim[part, lo:hi, :] = acc[part, lo:hi, :].astype(bf16)
            rim[part, HALF : HALF + NW, lo:hi] = acc[part, HALF : HALF + NW, lo:hi].astype(bf16)

    def rim_copy(k, dt, ds):
        where = (slice(None), slice(*span(dt, (0, 128), (128, 384), (384, 512))), slice(*span(ds, (0, 128), (128, 384), (384, 512))))
        return pltpu.make_async_remote_copy(
            src_ref=rim.at[where], dst_ref=rim_in.at[where], send_sem=rim_send.at[k], recv_sem=rim_recv.at[k],
            device_id=(t + dt, s + ds), device_id_type=MESH,
        )

    for k, (dt, ds) in enumerate(SIDES):
        @pl.when(exists(dt, ds))
        def _():
            rim_copy(k, dt, ds).start()
    for part in range(2):
        out_ref[part] = acc[part, HALF : HALF + NW, HALF : HALF + NW]
    for k, (dt, ds) in enumerate(SIDES):
        @pl.when(exists(-dt, -ds))
        def _():
            rim_copy(k, dt, ds).wait_recv()
            src_r, dst_r = span(dt, ((0, 128), (128, 256)), ((128, 384), (0, 256)), ((384, 512), (0, 128)))
            src_c, dst_c = span(ds, ((0, 128), (128, 256)), ((128, 384), (0, 256)), ((384, 512), (0, 128)))
            for part in range(2):
                out_ref[part, slice(*dst_r), slice(*dst_c)] += rim_in[part, slice(*src_r), slice(*src_c)].astype(f32)
    for part in range(2):
        cells_ref[part, EDGE : EDGE + NW, HALF : HALF + NW] = out_ref[part].astype(bf16)

    def ring_copy(k, dt, ds):
        src = (slice(None), slice(*span(dt, (16, 32), (16, 272), (256, 272))), slice(*span(ds, (128, 256), (128, 384), (256, 384))))
        dst = (slice(None), slice(*span(dt, (272, 288), (16, 272), (0, 16))), slice(*span(ds, (384, 512), (128, 384), (0, 128))))
        return pltpu.make_async_remote_copy(
            src_ref=cells_ref.at[src], dst_ref=cells_ref.at[dst], send_sem=ring_send.at[k], recv_sem=ring_recv.at[k],
            device_id=(t + dt, s + ds), device_id_type=MESH,
        )

    for k, (dt, ds) in enumerate(SIDES):
        @pl.when(exists(dt, ds))
        def _():
            ring_copy(k, dt, ds).start()
    for k, (dt, ds) in enumerate(SIDES):
        here = exists(-dt, -ds)

        @pl.when(here)
        def _():
            ring_copy(k, dt, ds).wait_recv()

        @pl.when(jnp.logical_not(here))
        def _():
            at_row, at_col = span(dt, (272, 288), (16, 272), (0, 16)), span(ds, (384, 512), (128, 384), (0, 128))
            for part in range(2):
                cells_ref[part, slice(*at_row), slice(*at_col)] = jnp.zeros((at_row[1] - at_row[0], at_col[1] - at_col[0]), bf16)

    for k, (dt, ds) in enumerate(SIDES):
        @pl.when(exists(dt, ds))
        def _():
            ring_copy(k, dt, ds).wait_send()
            halo_copy(k, dt, ds).wait_send()
            rim_copy(k, dt, ds).wait_send()
    for k, (dy, dz) in enumerate(order):
        amp_copy(k + 1, dy, dz).wait_send()


def sample(specimen, noise, probe, amps, rows, cols, counts):
    tiles, peers = lax.axis_size("tile"), lax.axis_size("scan")
    if peers == 16:
        order, rows_y = ORDER_16, 4
    else:
        order, rows_y = [(0, b) for b in range(1, peers)], 1
    forward, inverse = dft_matrices()
    f32, bf16 = jnp.float32, jnp.bfloat16
    smem = pl.BlockSpec(memory_space=pltpu.SMEM)
    vmem = pl.BlockSpec(memory_space=pltpu.VMEM)
    dma = pltpu.SemaphoreType.DMA
    return pl.pallas_call(
        functools.partial(patch_kernel, order, rows_y, tiles, peers),
        out_shape=(jax.ShapeDtypeStruct((2, NW, NW), f32), jax.ShapeDtypeStruct((2, NW + 2 * EDGE, 2 * NW), bf16)),
        in_specs=[smem, smem, smem, pl.BlockSpec(memory_space=pl.ANY), vmem, vmem, vmem, vmem, vmem],
        out_specs=(vmem, vmem),
        scratch_shapes=[
            pltpu.VMEM((peers, CAP, NW, NW), bf16),
            pltpu.VMEM((2, 2 * NW, 2 * NW), bf16),
            pltpu.VMEM((2, 2 * NW, 2 * NW), f32),
            pltpu.VMEM((2, 2 * NW, 2 * NW), bf16),
            pltpu.VMEM((2, 2 * NW, 2 * NW), bf16),
            pltpu.VMEM((2, 2, 2 * NW, HALF), f32),
            pltpu.VMEM((CAP, 2, NW, NW), f32),
            pltpu.VMEM((2 * NW, 2 * NW), bf16),
            pltpu.VMEM((2 * NW, 2 * NW), bf16),
            pltpu.VMEM((2 * NW, 2 * NW), f32),
            dma((peers,)), dma((peers,)), dma, dma((8,)), dma((8,)), dma((8,)), dma((8,)), dma((8,)), dma((8,)),
        ],
        compiler_params=pltpu.CompilerParams(collective_id=0, has_side_effects=True, vmem_limit_bytes=48 << 20),
        name="patches",
    )(rows, cols, counts, amps, specimen, noise, probe, jnp.asarray(forward), jnp.asarray(inverse))


def tap_selectors():
    first = np.zeros((18, 24), np.float32)
    second = np.zeros((24, 18), np.float32)
    for c in range(2):
        for dy in range(3):
            for dx in range(3):
                first[9 * c + 3 * dy + dx, 8 * dy + 3 * c + dx] = 0.5
                second[8 * dy + 3 * c + dx, 9 * c + 3 * dy + dx] = 1.0
    return first.astype(jnp.bfloat16), second.astype(jnp.bfloat16)


def prior_kernel(
    tiles, peers, cells_ref, sampled_ref, w1_ref, b1_ref, w2_ref, b2_ref, sel1_ref, sel2_ref, out_ref, taps, mixed_sum,
):
    f32, bf16 = jnp.float32, jnp.bfloat16
    t = lax.axis_index("tile")
    s = lax.axis_index("scan")
    rows = NW + 2 * EDGE
    square = lax.broadcasted_iota(jnp.int32, (128, 128), 0) == lax.broadcasted_iota(jnp.int32, (128, 128), 1)
    bias = jnp.sum(jnp.where(square, b1_ref[...], 0.0), axis=1, keepdims=True) * 0.5
    high = bias.astype(bf16).astype(f32)
    column = lax.broadcasted_iota(jnp.int32, (128, 24), 1)
    first = jnp.dot(w1_ref[...], sel1_ref[...], preferred_element_type=f32)
    first = (first + jnp.where(column == 6, high, 0.0) + jnp.where(column == 7, bias - high, 0.0)).astype(bf16)
    second = jnp.dot(sel2_ref[...], w2_ref[...], preferred_element_type=f32).astype(bf16)

    for c in range(2):
        plane = cells_ref[c].astype(f32)
        for dx in range(3):
            moved = pltpu.roll(plane, 2 * NW - (126 + dx), 1)
            for v in range(3):
                taps[v, pl.ds(3 * c + dx, rows, stride=8), :] = moved[:, v * 128 : (v + 1) * 128]
    for v in range(3):
        for k in (6, 7):
            taps[v, pl.ds(k, rows, stride=8), :] = jnp.ones((rows, 128), f32)

    lane = lax.broadcasted_iota(jnp.int32, (24, WIDE), 1)
    inside = jnp.logical_and(jnp.logical_or(lane > 0, s > 0), jnp.logical_or(lane < NW + 1, s < peers - 1))
    GROUP = 6

    def group(g, carry):
        older, old = carry
        for j in range(GROUP):
            index = g * GROUP + j
            start = pl.multiple_of((index + EDGE - 2) * 8, 8)
            window = jnp.concatenate([taps[v, pl.ds(start, 24), :] for v in range(3)], 1).astype(bf16)
            pre = jnp.dot(first, window, preferred_element_type=f32)
            hidden = (pre + pre * jnp.tanh(pre)).astype(bf16)
            here = jnp.logical_and(jnp.logical_or(index > 0, t > 0), jnp.logical_or(index < NW + 1, t < tiles - 1))
            mixed = jnp.where(jnp.logical_and(inside, here), jnp.dot(second, hidden, preferred_element_type=f32), 0.0)
            done = older + mixed[16:24]
            for v in range(3):
                mixed_sum[v, pl.ds(pl.multiple_of(index * 8, 8), 8), :] = done[:, v * 128 : (v + 1) * 128]
            older = old + mixed[8:16]
            old = mixed[0:8]
        return older, old

    zero = jnp.zeros((8, WIDE), f32)
    lax.fori_loop(0, (NW + 2) // GROUP, group, (zero, zero))
    for c in range(2):
        total = None
        for dx in range(3):
            part = jnp.concatenate([mixed_sum[v, pl.ds(16 + 3 * c + dx, NW, stride=8), :] for v in range(3)], 1)
            part = (pltpu.roll(part, WIDE - dx, 1) if dx else part)[:, :NW]
            total = part if total is None else total + part
        out_ref[c] = sampled_ref[c] - (total + b2_ref[c])


def subtract_prior(cells, sampled, first_weight, first_bias, second_weight, second_bias):
    tiles, peers = lax.axis_size("tile"), lax.axis_size("scan")
    f32 = jnp.float32
    smem = pl.BlockSpec(memory_space=pltpu.SMEM)
    vmem = pl.BlockSpec(memory_space=pltpu.VMEM)
    one, two = tap_selectors()
    return pl.pallas_call(
        functools.partial(prior_kernel, tiles, peers),
        out_shape=jax.ShapeDtypeStruct((2, NW, NW), f32),
        in_specs=[vmem, vmem, vmem, vmem, vmem, smem, vmem, vmem],
        out_specs=vmem,
        scratch_shapes=[
            pltpu.VMEM((3, 8 * (NW + 2 * EDGE), 128), f32),
            pltpu.VMEM((3, 8 * (NW + 2), 128), f32),
        ],
        compiler_params=pltpu.CompilerParams(vmem_limit_bytes=32 << 20),
        name="prior",
    )(cells, sampled, first_weight, first_bias.reshape(1, -1), second_weight, second_bias, jnp.asarray(one), jnp.asarray(two))


def shards(
    specimen, sampler_noise, probe_field, amplitudes, corner_rows, corner_cols, slot_counts,
    first_weight, first_bias, second_weight, second_bias,
):
    sampled, cells = sample(
        specimen, sampler_noise, probe_field, amplitudes[0, 0],
        corner_rows.reshape(-1), corner_cols.reshape(-1), slot_counts.reshape(-1),
    )
    return subtract_prior(cells, sampled, first_weight, first_bias, second_weight, second_bias)


def solution(mesh):
    return jax.shard_map(
        shards,
        mesh=mesh,
        in_specs=(
            P(None, "tile", "scan"),
            P(None, "tile", "scan"),
            P(),
            P("tile", "scan", None, None, None, None),
            P("tile", "scan", None, None),
            P("tile", "scan", None, None),
            P("tile", "scan", None),
            P(),
            P(),
            P(),
            P(),
        ),
        out_specs=P(None, "tile", "scan"),
        check_vma=False,
    )
```

```python
import functools

import jax
import jax.numpy as jnp
import numpy as np
from jax import lax
from jax.experimental import pallas as pl
from jax.experimental.pallas import tpu as pltpu
from jax.sharding import PartitionSpec as P

MESH = pl.DeviceIdType.MESH
NW = 256
HALF = 128
EDGE = 16
PRIOR_ROWS = 264
CAP = 2

ORDER_16 = [(3, 1), (2, 3), (1, 3), (3, 0), (3, 3), (0, 1), (1, 1), (0, 2), (2, 0), (3, 2), (1, 2), (0, 3), (2, 1), (2, 2), (1, 0)]
SIDES = [(a, b) for a in (-1, 0, 1) for b in (-1, 0, 1) if (a, b) != (0, 0)]


def dft_matrices():
    index = np.arange(NW)
    angle = (index[:, None] * index[None, :] % NW) * (2.0 * np.pi / NW)
    cosine = (np.cos(angle) / 16.0).astype(jnp.bfloat16)
    sine = (np.sin(angle) / 16.0).astype(jnp.bfloat16)
    forward = np.concatenate([np.concatenate([cosine, sine], 1), np.concatenate([-sine, cosine], 1)], 0)
    return forward, np.ascontiguousarray(forward.T)


def span(step, low, mid, high):
    return {-1: low, 0: mid, 1: high}[step]


def patch_kernel(
    order, rows_y, tiles, peers,
    rows_ref, cols_ref, counts_ref, amps_ref, spec_ref, noise_ref, probe_ref, fwd_ref, inv_ref,
    out_ref, cells_ref,
    recv, frame, acc, rim, rim_in, probe2, rolled, wave_in, mid_ref, far_ref, wave_ref,
    amp_send, amp_recv, own_sem, halo_send, halo_recv, rim_send, rim_recv, ring_send, ring_recv,
):
    f32, bf16 = jnp.float32, jnp.bfloat16
    t = lax.axis_index("tile")
    s = lax.axis_index("scan")
    rows_z = peers // rows_y
    y, z = s // rows_z, lax.rem(s, rows_z)

    mirror = 1 - 2 * lax.rem(t, 2)

    def peer(dy, dz):
        return lax.rem(y + mirror * dy + rows_y, rows_y) * rows_z + lax.rem(z + mirror * dz + rows_z, rows_z)

    def exists(dt, ds):
        ok_t = {-1: t > 0, 0: t >= 0, 1: t < tiles - 1}[dt]
        ok_s = {-1: s > 0, 0: s >= 0, 1: s < peers - 1}[ds]
        return jnp.logical_and(ok_t, ok_s)

    barrier = pltpu.get_barrier_semaphore()
    expected = jnp.int32(len(order))
    for dy, dz in order:
        pl.semaphore_signal(barrier, inc=1, device_id=(t, peer(-dy, -dz)), device_id_type=MESH)
    for dt, ds in SIDES:
        if dt != 0:
            here = exists(dt, ds)
            expected = expected + here.astype(jnp.int32)

            @pl.when(here)
            def _():
                pl.semaphore_signal(barrier, inc=1, device_id=(t + dt, s + ds), device_id_type=MESH)

    own = pltpu.make_async_copy(amps_ref.at[s], recv.at[0], own_sem)
    own.start()
    for part in range(2):
        frame[part, HALF : HALF + NW, HALF : HALF + NW] = spec_ref[part].astype(bf16)
    pl.semaphore_wait(barrier, expected)

    def halo_copy(k, dt, ds):
        src = (slice(None), slice(*span(dt, (128, 256), (128, 384), (256, 384))), slice(*span(ds, (128, 256), (128, 384), (256, 384))))
        dst = (slice(None), slice(*span(dt, (384, 512), (128, 384), (0, 128))), slice(*span(ds, (384, 512), (128, 384), (0, 128))))
        return pltpu.make_async_remote_copy(
            src_ref=frame.at[src], dst_ref=frame.at[dst], send_sem=halo_send.at[k], recv_sem=halo_recv.at[k],
            device_id=(t + dt, s + ds), device_id_type=MESH,
        )

    def amp_copy(k, dy, dz):
        d = peer(dy, dz)
        return pltpu.make_async_remote_copy(
            src_ref=amps_ref.at[d], dst_ref=recv.at[k], send_sem=amp_send.at[k], recv_sem=amp_recv.at[k],
            device_id=(t, d), device_id_type=MESH,
        )

    for k, (dt, ds) in enumerate(SIDES):
        @pl.when(exists(dt, ds))
        def _():
            halo_copy(k, dt, ds).start()

    for part in range(2):
        acc[part] = jnp.zeros((2 * NW, 2 * NW), f32)
        acc[part, HALF : HALF + NW, HALF : HALF + NW] = spec_ref[part] + 0.5 * noise_ref[part]
        for half in range(2):
            columns = probe_ref[part, :, half * HALF : (half + 1) * HALF]
            probe2[part, half, :NW, :] = columns
            probe2[part, half, NW:, :] = columns

    for k, (dt, ds) in enumerate(SIDES):
        here = exists(-dt, -ds)

        @pl.when(here)
        def _():
            halo_copy(k, dt, ds).wait_recv()

        @pl.when(jnp.logical_not(here))
        def _():
            at_row, at_col = span(dt, (384, 512), (128, 384), (0, 128)), span(ds, (384, 512), (128, 384), (0, 128))
            for part in range(2):
                frame[part, slice(*at_row), slice(*at_col)] = jnp.zeros((at_row[1] - at_row[0], at_col[1] - at_col[0]), bf16)

    CH = 32
    lane = lax.broadcasted_iota(jnp.int32, (CH, NW), 1)
    sub = lax.broadcasted_iota(jnp.int32, (CH, NW), 0)

    def steps_of(k):
        dy, dz = jnp.int32(0), jnp.int32(0)
        for i, (a, b) in enumerate(order):
            dy = jnp.where(k == i + 1, a, dy)
            dz = jnp.where(k == i + 1, b, dz)
        return dy, dz

    def corners(k):
        dy, dz = steps_of(k)
        h = peer(-dy, -dz)
        return h, [(rows_ref[h * CAP + c], cols_ref[h * CAP + c]) for c in range(CAP)]

    def both(left_ref, right_ref, result):
        for c in range(CAP):
            mid = jnp.dot(left_ref[...], wave_in[:, c * NW : (c + 1) * NW], preferred_element_type=f32)
            for p in range(2):
                mid_ref[c * NW : (c + 1) * NW, p * NW : (p + 1) * NW] = mid[p * NW : (p + 1) * NW].astype(bf16)
        for p in range(2):
            result[:, p * NW : (p + 1) * NW] = jnp.dot(mid_ref[...], right_ref[:, p * NW : (p + 1) * NW], preferred_element_type=f32)

    for k, (dy, dz) in enumerate(order):
        amp_copy(k + 1, dy, dz).start()

    def outward(k, carry):
        h, corner = corners(k)

        def exits(i, carry):
            base = pl.multiple_of(i * CH, CH)
            for c in range(CAP):
                r, q = corner[c]
                low_row = sub + base < r
                low_col = lane < q
                shift = lax.rem(q, NW)
                cell, prb = [], []
                for part in range(2):
                    tile = [[frame[part, pl.ds(base + a * NW, CH), b * NW : (b + 1) * NW].astype(f32) for b in range(2)] for a in range(2)]
                    cell.append(jnp.where(low_row, jnp.where(low_col, tile[1][1], tile[1][0]), jnp.where(low_col, tile[0][1], tile[0][0])))
                    turned = pltpu.roll(jnp.concatenate([probe2[part, half, pl.ds(base + NW - r, CH), :] for half in range(2)], 1), shift, 1)
                    rolled[k, c, part, pl.ds(base, CH), :] = turned
                    prb.append(turned)
                wave_in[pl.ds(base, CH), c * NW : (c + 1) * NW] = (prb[0] * cell[0] - prb[1] * cell[1]).astype(bf16)
                wave_in[pl.ds(base + NW, CH), c * NW : (c + 1) * NW] = (prb[0] * cell[1] + prb[1] * cell[0]).astype(bf16)
            return carry

        lax.fori_loop(0, NW // CH, exits, 0, unroll=True)
        both(fwd_ref, inv_ref, far_ref.at[k])
        return carry

    lax.fori_loop(0, len(order) + 1, outward, 0, unroll=2)
    own.wait()

    def inward(k, carry):
        h, corner = corners(k)
        dy, dz = steps_of(k)
        scale = [jnp.where(counts_ref[h] > c, f32(-0.25), f32(0.0)) for c in range(CAP)]

        @pl.when(k > 0)
        def _():
            pltpu.make_async_remote_copy(
                src_ref=recv.at[k], dst_ref=recv.at[k], send_sem=amp_send.at[k], recv_sem=amp_recv.at[k],
                device_id=(t, peer(dy, dz)), device_id_type=MESH,
            ).wait_recv()

        def correct(i, carry):
            base = pl.multiple_of(i * CH, CH)
            for c in range(CAP):
                fr = far_ref[k, pl.ds(base + c * NW, CH), :NW]
                fi = far_ref[k, pl.ds(base + c * NW, CH), NW:]
                amp = recv[k, c, pl.ds(base, CH), :].astype(f32)
                keep = 1.0 - amp * lax.rsqrt(jnp.maximum(fr * fr + fi * fi, 1.0))
                wave_in[pl.ds(base, CH), c * NW : (c + 1) * NW] = (fr * keep).astype(bf16)
                wave_in[pl.ds(base + NW, CH), c * NW : (c + 1) * NW] = (fi * keep).astype(bf16)
            return carry

        lax.fori_loop(0, NW // CH, correct, 0, unroll=True)
        both(inv_ref, fwd_ref, wave_ref)

        def gather(i, carry):
            base = pl.multiple_of(i * CH, CH)
            grads = []
            for c in range(CAP):
                wr = wave_ref[pl.ds(base + c * NW, CH), :NW]
                wi = wave_ref[pl.ds(base + c * NW, CH), NW:]
                pr = rolled[k, c, 0, pl.ds(base, CH), :] * scale[c]
                pi = rolled[k, c, 1, pl.ds(base, CH), :] * scale[c]
                grads.append((pr * wr + pi * wi, pr * wi - pi * wr))
            for a in range(2):
                for b in range(2):
                    masks = []
                    for c in range(CAP):
                        r, q = corner[c]
                        row_ok = sub + base < r if a else sub + base >= r
                        col_ok = lane < q if b else lane >= q
                        masks.append(jnp.logical_and(row_ok, col_ok))
                    for part in range(2):
                        total = acc[part, pl.ds(base + a * NW, CH), b * NW : (b + 1) * NW]
                        for c in range(CAP):
                            total = total + jnp.where(masks[c], grads[c][part], 0.0)
                        acc[part, pl.ds(base + a * NW, CH), b * NW : (b + 1) * NW] = total
            return carry

        lax.fori_loop(0, NW // CH, gather, 0, unroll=True)
        return carry

    lax.fori_loop(0, len(order) + 1, inward, 0, unroll=2)

    for part in range(2):
        for lo, hi in ((0, HALF), (HALF + NW, 2 * NW)):
            rim[part, lo:hi, :] = acc[part, lo:hi, :].astype(bf16)
            rim[part, HALF : HALF + NW, lo:hi] = acc[part, HALF : HALF + NW, lo:hi].astype(bf16)

    def rim_copy(k, dt, ds):
        where = (slice(None), slice(*span(dt, (0, 128), (128, 384), (384, 512))), slice(*span(ds, (0, 128), (128, 384), (384, 512))))
        return pltpu.make_async_remote_copy(
            src_ref=rim.at[where], dst_ref=rim_in.at[where], send_sem=rim_send.at[k], recv_sem=rim_recv.at[k],
            device_id=(t + dt, s + ds), device_id_type=MESH,
        )

    for k, (dt, ds) in enumerate(SIDES):
        @pl.when(exists(dt, ds))
        def _():
            rim_copy(k, dt, ds).start()
    for part in range(2):
        out_ref[part] = acc[part, HALF : HALF + NW, HALF : HALF + NW]
    for k, (dt, ds) in enumerate(SIDES):
        @pl.when(exists(-dt, -ds))
        def _():
            rim_copy(k, dt, ds).wait_recv()
            src_r, dst_r = span(dt, ((0, 128), (128, 256)), ((128, 384), (0, 256)), ((384, 512), (0, 128)))
            src_c, dst_c = span(ds, ((0, 128), (128, 256)), ((128, 384), (0, 256)), ((384, 512), (0, 128)))
            for part in range(2):
                out_ref[part, slice(*dst_r), slice(*dst_c)] += rim_in[part, slice(*src_r), slice(*src_c)].astype(f32)
    for part in range(2):
        cells_ref[part, EDGE : EDGE + NW, HALF : HALF + NW] = out_ref[part].astype(bf16)

    def ring_copy(k, dt, ds):
        src = (slice(None), slice(*span(dt, (16, 32), (16, 272), (256, 272))), slice(*span(ds, (128, 256), (128, 384), (256, 384))))
        dst = (slice(None), slice(*span(dt, (272, 288), (16, 272), (0, 16))), slice(*span(ds, (384, 512), (128, 384), (0, 128))))
        return pltpu.make_async_remote_copy(
            src_ref=cells_ref.at[src], dst_ref=cells_ref.at[dst], send_sem=ring_send.at[k], recv_sem=ring_recv.at[k],
            device_id=(t + dt, s + ds), device_id_type=MESH,
        )

    for k, (dt, ds) in enumerate(SIDES):
        @pl.when(exists(dt, ds))
        def _():
            ring_copy(k, dt, ds).start()
    for k, (dt, ds) in enumerate(SIDES):
        here = exists(-dt, -ds)

        @pl.when(here)
        def _():
            ring_copy(k, dt, ds).wait_recv()

        @pl.when(jnp.logical_not(here))
        def _():
            at_row, at_col = span(dt, (272, 288), (16, 272), (0, 16)), span(ds, (384, 512), (128, 384), (0, 128))
            for part in range(2):
                cells_ref[part, slice(*at_row), slice(*at_col)] = jnp.zeros((at_row[1] - at_row[0], at_col[1] - at_col[0]), bf16)

    for k, (dt, ds) in enumerate(SIDES):
        @pl.when(exists(dt, ds))
        def _():
            ring_copy(k, dt, ds).wait_send()
            halo_copy(k, dt, ds).wait_send()
            rim_copy(k, dt, ds).wait_send()
    for k, (dy, dz) in enumerate(order):
        amp_copy(k + 1, dy, dz).wait_send()


def sample(specimen, noise, probe, amps, rows, cols, counts):
    tiles, peers = lax.axis_size("tile"), lax.axis_size("scan")
    if peers == 16:
        order, rows_y = ORDER_16, 4
    else:
        order, rows_y = [(0, b) for b in range(1, peers)], 1
    forward, inverse = dft_matrices()
    f32, bf16 = jnp.float32, jnp.bfloat16
    smem = pl.BlockSpec(memory_space=pltpu.SMEM)
    vmem = pl.BlockSpec(memory_space=pltpu.VMEM)
    dma = pltpu.SemaphoreType.DMA
    return pl.pallas_call(
        functools.partial(patch_kernel, order, rows_y, tiles, peers),
        out_shape=(jax.ShapeDtypeStruct((2, NW, NW), f32), jax.ShapeDtypeStruct((2, NW + 2 * EDGE, 2 * NW), bf16)),
        in_specs=[smem, smem, smem, pl.BlockSpec(memory_space=pl.ANY), vmem, vmem, vmem, vmem, vmem],
        out_specs=(vmem, vmem),
        scratch_shapes=[
            pltpu.VMEM((peers, CAP, NW, NW), bf16),
            pltpu.VMEM((2, 2 * NW, 2 * NW), bf16),
            pltpu.VMEM((2, 2 * NW, 2 * NW), f32),
            pltpu.VMEM((2, 2 * NW, 2 * NW), bf16),
            pltpu.VMEM((2, 2 * NW, 2 * NW), bf16),
            pltpu.VMEM((2, 2, 2 * NW, HALF), f32),
            pltpu.VMEM((peers, CAP, 2, NW, NW), f32),
            pltpu.VMEM((2 * NW, 2 * NW), bf16),
            pltpu.VMEM((2 * NW, 2 * NW), bf16),
            pltpu.VMEM((peers, 2 * NW, 2 * NW), f32),
            pltpu.VMEM((2 * NW, 2 * NW), f32),
            dma((peers,)), dma((peers,)), dma, dma((8,)), dma((8,)), dma((8,)), dma((8,)), dma((8,)), dma((8,)),
        ],
        compiler_params=pltpu.CompilerParams(collective_id=0, has_side_effects=True, vmem_limit_bytes=60 << 20),
        name="patches",
    )(rows, cols, counts, amps, specimen, noise, probe, jnp.asarray(forward), jnp.asarray(inverse))


def tap_selectors():
    first = np.zeros((18, 24), np.float32)
    second = np.zeros((24, 18), np.float32)
    for c in range(2):
        for dy in range(3):
            for dx in range(3):
                first[9 * c + 3 * dy + dx, 8 * dy + 3 * c + dx] = 0.5
                second[8 * dy + 3 * c + dx, 9 * c + 3 * dy + dx] = 1.0
    return first.astype(jnp.bfloat16), second.astype(jnp.bfloat16)


def prior_kernel(
    tiles, peers, cells_ref, sampled_ref, w1_ref, b1_ref, w2_ref, b2_ref, sel1_ref, sel2_ref, out_ref, taps, mixed_sum,
):
    f32, bf16 = jnp.float32, jnp.bfloat16
    t = lax.axis_index("tile")
    s = lax.axis_index("scan")
    rows = NW + 2 * EDGE
    square = lax.broadcasted_iota(jnp.int32, (128, 128), 0) == lax.broadcasted_iota(jnp.int32, (128, 128), 1)
    bias = jnp.sum(jnp.where(square, b1_ref[...], 0.0), axis=1, keepdims=True) * 0.5
    high = bias.astype(bf16).astype(f32)
    column = lax.broadcasted_iota(jnp.int32, (128, 24), 1)
    first = jnp.dot(w1_ref[...], sel1_ref[...], preferred_element_type=f32)
    first = (first + jnp.where(column == 6, high, 0.0) + jnp.where(column == 7, bias - high, 0.0)).astype(bf16)
    second = jnp.dot(sel2_ref[...], w2_ref[...], preferred_element_type=f32).astype(bf16)

    for c in range(2):
        plane = cells_ref[c].astype(f32)
        for dx in range(3):
            moved = pltpu.roll(plane, 2 * NW - (126 + dx), 1)
            for v in range(3):
                taps[v, pl.ds(3 * c + dx, rows, stride=8), :] = moved[:, v * 128 : (v + 1) * 128]
    for v in range(3):
        for k in (6, 7):
            taps[v, pl.ds(k, rows, stride=8), :] = jnp.ones((rows, 128), f32)

    GROUP = 44
    lane = lax.broadcasted_iota(jnp.int32, (24, 128), 1)
    left_ok = jnp.logical_or(lane > 0, s > 0)
    extra_ok = jnp.logical_and(lane < 2, jnp.logical_or(lane < 1, s < peers - 1))

    def group(g, carry):
        older, old = carry
        windows, extra = [], None
        for j in range(GROUP):
            start = pl.multiple_of((g * GROUP + j + EDGE - 2) * 8, 8)
            windows += [taps[0, pl.ds(start, 24), :], taps[1, pl.ds(start, 24), :]]
            last = jnp.where(lane < 2, taps[2, pl.ds(start, 24), :], 0.0)
            last = pltpu.roll(last, 2 * j, 1) if j else last
            extra = last if extra is None else extra + last
        window = jnp.concatenate([v.astype(bf16) for v in windows + [extra]], 1)
        pre = jnp.dot(first, window, preferred_element_type=f32)
        hidden = (pre + pre * jnp.tanh(pre)).astype(bf16)
        mixed_all = jnp.dot(second, hidden, preferred_element_type=f32)
        tail = mixed_all[:, GROUP * 256 :]
        for j in range(GROUP):
            index = g * GROUP + j
            here = jnp.logical_and(jnp.logical_or(index > 0, t > 0), jnp.logical_or(index < NW + 1, t < tiles - 1))
            last = pltpu.roll(tail, 128 - 2 * j, 1) if j else tail
            mixed = [
                jnp.where(jnp.logical_and(left_ok, here), mixed_all[:, 256 * j : 256 * j + 128], 0.0),
                jnp.where(here, mixed_all[:, 256 * j + 128 : 256 * j + 256], 0.0),
                jnp.where(jnp.logical_and(extra_ok, here), last, 0.0),
            ]
            for v in range(3):
                mixed_sum[v, pl.ds(pl.multiple_of(index * 8, 8), 8), :] = older[v] + mixed[v][16:24]
            older = [old[v] + mixed[v][8:16] for v in range(3)]
            old = [mixed[v][0:8] for v in range(3)]
        return older, old

    zero = [jnp.zeros((8, 128), f32)] * 3
    lax.fori_loop(0, PRIOR_ROWS // GROUP, group, (zero, zero))
    for c in range(2):
        total = None
        for dx in range(3):
            part = jnp.concatenate([mixed_sum[v, pl.ds(16 + 3 * c + dx, NW, stride=8), :] for v in range(3)], 1)
            part = (pltpu.roll(part, 384 - dx, 1) if dx else part)[:, :NW]
            total = part if total is None else total + part
        out_ref[c] = sampled_ref[c] - (total + b2_ref[c])


def subtract_prior(cells, sampled, first_weight, first_bias, second_weight, second_bias):
    tiles, peers = lax.axis_size("tile"), lax.axis_size("scan")
    f32 = jnp.float32
    smem = pl.BlockSpec(memory_space=pltpu.SMEM)
    vmem = pl.BlockSpec(memory_space=pltpu.VMEM)
    one, two = tap_selectors()
    return pl.pallas_call(
        functools.partial(prior_kernel, tiles, peers),
        out_shape=jax.ShapeDtypeStruct((2, NW, NW), f32),
        in_specs=[vmem, vmem, vmem, vmem, vmem, smem, vmem, vmem],
        out_specs=vmem,
        scratch_shapes=[
            pltpu.VMEM((3, 8 * (NW + 2 * EDGE), 128), f32),
            pltpu.VMEM((3, 8 * PRIOR_ROWS, 128), f32),
        ],
        compiler_params=pltpu.CompilerParams(vmem_limit_bytes=32 << 20),
        name="prior",
    )(cells, sampled, first_weight, first_bias.reshape(1, -1), second_weight, second_bias, jnp.asarray(one), jnp.asarray(two))


def shards(
    specimen, sampler_noise, probe_field, amplitudes, corner_rows, corner_cols, slot_counts,
    first_weight, first_bias, second_weight, second_bias,
):
    sampled, cells = sample(
        specimen, sampler_noise, probe_field, amplitudes[0, 0],
        corner_rows.reshape(-1), corner_cols.reshape(-1), slot_counts.reshape(-1),
    )
    return subtract_prior(cells, sampled, first_weight, first_bias, second_weight, second_bias)


def solution(mesh):
    return jax.shard_map(
        shards,
        mesh=mesh,
        in_specs=(
            P(None, "tile", "scan"),
            P(None, "tile", "scan"),
            P(),
            P("tile", "scan", None, None, None, None),
            P("tile", "scan", None, None),
            P("tile", "scan", None, None),
            P("tile", "scan", None),
            P(),
            P(),
            P(),
            P(),
        ),
        out_specs=P(None, "tile", "scan"),
        check_vma=False,
    )
```

```python
import functools

import jax
import jax.numpy as jnp
import numpy as np
from jax import lax
from jax.experimental import pallas as pl
from jax.experimental.pallas import tpu as pltpu
from jax.sharding import PartitionSpec as P

MESH = pl.DeviceIdType.MESH
NW = 256
HALF = 128
EDGE = 16
PRIOR_ROWS = 264
CAP = 2

ORDER_16 = [(3, 1), (1, 3), (2, 3), (1, 1), (3, 0), (2, 0), (3, 3), (1, 2), (0, 1), (0, 3), (2, 1), (3, 2), (1, 0), (0, 2), (2, 2)]
ISSUE_16 = [0, 2, 1, 4, 6, 8, 3, 13, 5, 11, 7, 9, 10, 14, 12]
SIDES = [(a, b) for a in (-1, 0, 1) for b in (-1, 0, 1) if (a, b) != (0, 0)]


def dft_matrices():
    index = np.arange(NW)
    angle = (index[:, None] * index[None, :] % NW) * (2.0 * np.pi / NW)
    cosine = (np.cos(angle) / 16.0).astype(jnp.bfloat16)
    sine = (np.sin(angle) / 16.0).astype(jnp.bfloat16)
    forward = np.concatenate([np.concatenate([cosine, sine], 1), np.concatenate([-sine, cosine], 1)], 0)
    return forward, np.ascontiguousarray(forward.T)


def span(step, low, mid, high):
    return {-1: low, 0: mid, 1: high}[step]


def patch_kernel(
    order, issue, rows_y, tiles, peers,
    rows_ref, cols_ref, counts_ref, amps_ref, spec_ref, noise_ref, probe_ref, fwd_ref, inv_ref,
    out_ref, cells_ref,
    recv, frame, acc, rim, rim_in, probe2, rolled, wave_in, mid_ref, far_ref, wave_ref,
    amp_send, amp_recv, own_sem, halo_send, halo_recv, rim_send, rim_recv, ring_send, ring_recv,
):
    f32, bf16 = jnp.float32, jnp.bfloat16
    t = lax.axis_index("tile")
    s = lax.axis_index("scan")
    rows_z = peers // rows_y
    y, z = s // rows_z, lax.rem(s, rows_z)

    mirror = 1 - 2 * lax.rem(t, 2)

    def peer(dy, dz):
        return lax.rem(y + mirror * dy + rows_y, rows_y) * rows_z + lax.rem(z + mirror * dz + rows_z, rows_z)

    def exists(dt, ds):
        ok_t = {-1: t > 0, 0: t >= 0, 1: t < tiles - 1}[dt]
        ok_s = {-1: s > 0, 0: s >= 0, 1: s < peers - 1}[ds]
        return jnp.logical_and(ok_t, ok_s)

    barrier = pltpu.get_barrier_semaphore()
    expected = jnp.int32(len(order))
    for dy, dz in order:
        pl.semaphore_signal(barrier, inc=1, device_id=(t, peer(-dy, -dz)), device_id_type=MESH)
    for dt, ds in SIDES:
        if dt != 0:
            here = exists(dt, ds)
            expected = expected + here.astype(jnp.int32)

            @pl.when(here)
            def _():
                pl.semaphore_signal(barrier, inc=1, device_id=(t + dt, s + ds), device_id_type=MESH)

    own = pltpu.make_async_copy(amps_ref.at[s], recv.at[0], own_sem)
    own.start()
    for part in range(2):
        frame[part, HALF : HALF + NW, HALF : HALF + NW] = spec_ref[part].astype(bf16)
    pl.semaphore_wait(barrier, expected)

    def halo_copy(k, dt, ds):
        src = (slice(None), slice(*span(dt, (128, 256), (128, 384), (256, 384))), slice(*span(ds, (128, 256), (128, 384), (256, 384))))
        dst = (slice(None), slice(*span(dt, (384, 512), (128, 384), (0, 128))), slice(*span(ds, (384, 512), (128, 384), (0, 128))))
        return pltpu.make_async_remote_copy(
            src_ref=frame.at[src], dst_ref=frame.at[dst], send_sem=halo_send.at[k], recv_sem=halo_recv.at[k],
            device_id=(t + dt, s + ds), device_id_type=MESH,
        )

    def amp_copy(k, dy, dz):
        d = peer(dy, dz)
        return pltpu.make_async_remote_copy(
            src_ref=amps_ref.at[d], dst_ref=recv.at[k], send_sem=amp_send.at[k], recv_sem=amp_recv.at[k],
            device_id=(t, d), device_id_type=MESH,
        )

    for k, (dt, ds) in enumerate(SIDES):
        @pl.when(exists(dt, ds))
        def _():
            halo_copy(k, dt, ds).start()

    for part in range(2):
        acc[part] = jnp.zeros((2 * NW, 2 * NW), f32)
        acc[part, HALF : HALF + NW, HALF : HALF + NW] = spec_ref[part] + 0.5 * noise_ref[part]
        for half in range(2):
            columns = probe_ref[part, :, half * HALF : (half + 1) * HALF]
            probe2[part, half, :NW, :] = columns
            probe2[part, half, NW:, :] = columns

    for k, (dt, ds) in enumerate(SIDES):
        here = exists(-dt, -ds)

        @pl.when(here)
        def _():
            halo_copy(k, dt, ds).wait_recv()

        @pl.when(jnp.logical_not(here))
        def _():
            at_row, at_col = span(dt, (384, 512), (128, 384), (0, 128)), span(ds, (384, 512), (128, 384), (0, 128))
            for part in range(2):
                frame[part, slice(*at_row), slice(*at_col)] = jnp.zeros((at_row[1] - at_row[0], at_col[1] - at_col[0]), bf16)

    CH = 32
    lane = lax.broadcasted_iota(jnp.int32, (CH, NW), 1)
    sub = lax.broadcasted_iota(jnp.int32, (CH, NW), 0)

    def steps_of(k):
        dy, dz = jnp.int32(0), jnp.int32(0)
        for i, (a, b) in enumerate(order):
            dy = jnp.where(k == i + 1, a, dy)
            dz = jnp.where(k == i + 1, b, dz)
        return dy, dz

    def corners(k):
        dy, dz = steps_of(k)
        h = peer(-dy, -dz)
        return h, [(rows_ref[c, h], cols_ref[c, h]) for c in range(CAP)]

    def both(left_ref, right_ref, result):
        for c in range(CAP):
            mid = jnp.dot(left_ref[...], wave_in[:, c * NW : (c + 1) * NW], preferred_element_type=f32)
            for p in range(2):
                mid_ref[c * NW : (c + 1) * NW, p * NW : (p + 1) * NW] = mid[p * NW : (p + 1) * NW].astype(bf16)
        for p in range(2):
            result[:, p * NW : (p + 1) * NW] = jnp.dot(mid_ref[...], right_ref[:, p * NW : (p + 1) * NW], preferred_element_type=f32)

    for k in issue:
        amp_copy(k + 1, *order[k]).start()

    def outward(k, carry):
        h, corner = corners(k)

        def exits(i, carry):
            base = pl.multiple_of(i * CH, CH)
            for c in range(CAP):
                r, q = corner[c]
                low_row = sub + base < r
                low_col = lane < q
                shift = lax.rem(q, NW)
                cell, prb = [], []
                for part in range(2):
                    tile = [[frame[part, pl.ds(base + a * NW, CH), b * NW : (b + 1) * NW].astype(f32) for b in range(2)] for a in range(2)]
                    cell.append(jnp.where(low_row, jnp.where(low_col, tile[1][1], tile[1][0]), jnp.where(low_col, tile[0][1], tile[0][0])))
                    turned = pltpu.roll(jnp.concatenate([probe2[part, half, pl.ds(base + NW - r, CH), :] for half in range(2)], 1), shift, 1)
                    rolled[k, c, part, pl.ds(base, CH), :] = turned
                    prb.append(turned)
                wave_in[pl.ds(base, CH), c * NW : (c + 1) * NW] = (prb[0] * cell[0] - prb[1] * cell[1]).astype(bf16)
                wave_in[pl.ds(base + NW, CH), c * NW : (c + 1) * NW] = (prb[0] * cell[1] + prb[1] * cell[0]).astype(bf16)
            return carry

        lax.fori_loop(0, NW // CH, exits, 0, unroll=True)
        both(fwd_ref, inv_ref, far_ref.at[k])
        return carry

    lax.fori_loop(0, len(order) + 1, outward, 0, unroll=2)
    own.wait()

    def inward(k, carry):
        h, corner = corners(k)
        dy, dz = steps_of(k)
        scale = [jnp.where(counts_ref[h] > c, f32(-0.25), f32(0.0)) for c in range(CAP)]

        @pl.when(k > 0)
        def _():
            pltpu.make_async_remote_copy(
                src_ref=recv.at[k], dst_ref=recv.at[k], send_sem=amp_send.at[k], recv_sem=amp_recv.at[k],
                device_id=(t, peer(dy, dz)), device_id_type=MESH,
            ).wait_recv()

        def correct(i, carry):
            base = pl.multiple_of(i * CH, CH)
            for c in range(CAP):
                fr = far_ref[k, pl.ds(base + c * NW, CH), :NW]
                fi = far_ref[k, pl.ds(base + c * NW, CH), NW:]
                amp = recv[k, c, pl.ds(base, CH), :].astype(f32)
                keep = 1.0 - amp * lax.rsqrt(jnp.maximum(fr * fr + fi * fi, 1.0))
                wave_in[pl.ds(base, CH), c * NW : (c + 1) * NW] = (fr * keep).astype(bf16)
                wave_in[pl.ds(base + NW, CH), c * NW : (c + 1) * NW] = (fi * keep).astype(bf16)
            return carry

        lax.fori_loop(0, NW // CH, correct, 0, unroll=True)
        both(inv_ref, fwd_ref, wave_ref)

        def gather(i, carry):
            base = pl.multiple_of(i * CH, CH)
            grads = []
            for c in range(CAP):
                wr = wave_ref[pl.ds(base + c * NW, CH), :NW]
                wi = wave_ref[pl.ds(base + c * NW, CH), NW:]
                pr = rolled[k, c, 0, pl.ds(base, CH), :] * scale[c]
                pi = rolled[k, c, 1, pl.ds(base, CH), :] * scale[c]
                grads.append((pr * wr + pi * wi, pr * wi - pi * wr))
            for a in range(2):
                for b in range(2):
                    masks = []
                    for c in range(CAP):
                        r, q = corner[c]
                        row_ok = sub + base < r if a else sub + base >= r
                        col_ok = lane < q if b else lane >= q
                        masks.append(jnp.logical_and(row_ok, col_ok))
                    for part in range(2):
                        total = acc[part, pl.ds(base + a * NW, CH), b * NW : (b + 1) * NW]
                        for c in range(CAP):
                            total = total + jnp.where(masks[c], grads[c][part], 0.0)
                        acc[part, pl.ds(base + a * NW, CH), b * NW : (b + 1) * NW] = total
            return carry

        lax.fori_loop(0, NW // CH, gather, 0, unroll=True)
        return carry

    lax.fori_loop(0, len(order) + 1, inward, 0, unroll=2)

    for part in range(2):
        for lo, hi in ((0, HALF), (HALF + NW, 2 * NW)):
            rim[part, lo:hi, :] = acc[part, lo:hi, :].astype(bf16)
            rim[part, HALF : HALF + NW, lo:hi] = acc[part, HALF : HALF + NW, lo:hi].astype(bf16)

    def rim_copy(k, dt, ds):
        where = (slice(None), slice(*span(dt, (0, 128), (128, 384), (384, 512))), slice(*span(ds, (0, 128), (128, 384), (384, 512))))
        return pltpu.make_async_remote_copy(
            src_ref=rim.at[where], dst_ref=rim_in.at[where], send_sem=rim_send.at[k], recv_sem=rim_recv.at[k],
            device_id=(t + dt, s + ds), device_id_type=MESH,
        )

    for k, (dt, ds) in enumerate(SIDES):
        @pl.when(exists(dt, ds))
        def _():
            rim_copy(k, dt, ds).start()
    for part in range(2):
        out_ref[part] = acc[part, HALF : HALF + NW, HALF : HALF + NW]
    for k, (dt, ds) in enumerate(SIDES):
        @pl.when(exists(-dt, -ds))
        def _():
            rim_copy(k, dt, ds).wait_recv()
            src_r, dst_r = span(dt, ((0, 128), (128, 256)), ((128, 384), (0, 256)), ((384, 512), (0, 128)))
            src_c, dst_c = span(ds, ((0, 128), (128, 256)), ((128, 384), (0, 256)), ((384, 512), (0, 128)))
            for part in range(2):
                out_ref[part, slice(*dst_r), slice(*dst_c)] += rim_in[part, slice(*src_r), slice(*src_c)].astype(f32)
    for part in range(2):
        cells_ref[part, EDGE : EDGE + NW, HALF : HALF + NW] = out_ref[part].astype(bf16)

    def ring_copy(k, dt, ds):
        src = (slice(None), slice(*span(dt, (16, 32), (16, 272), (256, 272))), slice(*span(ds, (128, 256), (128, 384), (256, 384))))
        dst = (slice(None), slice(*span(dt, (272, 288), (16, 272), (0, 16))), slice(*span(ds, (384, 512), (128, 384), (0, 128))))
        return pltpu.make_async_remote_copy(
            src_ref=cells_ref.at[src], dst_ref=cells_ref.at[dst], send_sem=ring_send.at[k], recv_sem=ring_recv.at[k],
            device_id=(t + dt, s + ds), device_id_type=MESH,
        )

    for k, (dt, ds) in enumerate(SIDES):
        @pl.when(exists(dt, ds))
        def _():
            ring_copy(k, dt, ds).start()
    for k, (dt, ds) in enumerate(SIDES):
        here = exists(-dt, -ds)

        @pl.when(here)
        def _():
            ring_copy(k, dt, ds).wait_recv()

        @pl.when(jnp.logical_not(here))
        def _():
            at_row, at_col = span(dt, (272, 288), (16, 272), (0, 16)), span(ds, (384, 512), (128, 384), (0, 128))
            for part in range(2):
                cells_ref[part, slice(*at_row), slice(*at_col)] = jnp.zeros((at_row[1] - at_row[0], at_col[1] - at_col[0]), bf16)

    for k, (dt, ds) in enumerate(SIDES):
        @pl.when(exists(dt, ds))
        def _():
            ring_copy(k, dt, ds).wait_send()
            halo_copy(k, dt, ds).wait_send()
            rim_copy(k, dt, ds).wait_send()
    for k, (dy, dz) in enumerate(order):
        amp_copy(k + 1, dy, dz).wait_send()


def sample(specimen, noise, probe, amps, rows, cols, counts):
    tiles, peers = lax.axis_size("tile"), lax.axis_size("scan")
    if peers == 16:
        order, issue, rows_y = ORDER_16, ISSUE_16, 4
    else:
        order, issue, rows_y = [(0, b) for b in range(1, peers)], list(range(peers - 1)), 1
    forward, inverse = dft_matrices()
    f32, bf16 = jnp.float32, jnp.bfloat16
    smem = pl.BlockSpec(memory_space=pltpu.SMEM)
    vmem = pl.BlockSpec(memory_space=pltpu.VMEM)
    dma = pltpu.SemaphoreType.DMA
    return pl.pallas_call(
        functools.partial(patch_kernel, order, issue, rows_y, tiles, peers),
        out_shape=(jax.ShapeDtypeStruct((2, NW, NW), f32), jax.ShapeDtypeStruct((2, NW + 2 * EDGE, 2 * NW), bf16)),
        in_specs=[smem, smem, smem, pl.BlockSpec(memory_space=pl.ANY), vmem, vmem, vmem, vmem, vmem],
        out_specs=(vmem, vmem),
        scratch_shapes=[
            pltpu.VMEM((peers, CAP, NW, NW), bf16),
            pltpu.VMEM((2, 2 * NW, 2 * NW), bf16),
            pltpu.VMEM((2, 2 * NW, 2 * NW), f32),
            pltpu.VMEM((2, 2 * NW, 2 * NW), bf16),
            pltpu.VMEM((2, 2 * NW, 2 * NW), bf16),
            pltpu.VMEM((2, 2, 2 * NW, HALF), f32),
            pltpu.VMEM((peers, CAP, 2, NW, NW), f32),
            pltpu.VMEM((2 * NW, 2 * NW), bf16),
            pltpu.VMEM((2 * NW, 2 * NW), bf16),
            pltpu.VMEM((peers, 2 * NW, 2 * NW), f32),
            pltpu.VMEM((2 * NW, 2 * NW), f32),
            dma((peers,)), dma((peers,)), dma, dma((8,)), dma((8,)), dma((8,)), dma((8,)), dma((8,)), dma((8,)),
        ],
        compiler_params=pltpu.CompilerParams(collective_id=0, has_side_effects=True, vmem_limit_bytes=60 << 20),
        name="patches",
    )(rows, cols, counts, amps, specimen, noise, probe, jnp.asarray(forward), jnp.asarray(inverse))


def tap_selectors():
    first = np.zeros((18, 24), np.float32)
    second = np.zeros((24, 18), np.float32)
    for c in range(2):
        for dy in range(3):
            for dx in range(3):
                first[9 * c + 3 * dy + dx, 8 * dy + 3 * c + dx] = 0.5
                second[8 * dy + 3 * c + dx, 9 * c + 3 * dy + dx] = 1.0
    return first.astype(jnp.bfloat16), second.astype(jnp.bfloat16)


def prior_kernel(
    tiles, peers, cells_ref, sampled_ref, w1_ref, b1_ref, w2_ref, b2_ref, sel1_ref, sel2_ref, out_ref, taps, mixed_sum,
):
    f32, bf16 = jnp.float32, jnp.bfloat16
    t = lax.axis_index("tile")
    s = lax.axis_index("scan")
    rows = NW + 2 * EDGE
    square = lax.broadcasted_iota(jnp.int32, (128, 128), 0) == lax.broadcasted_iota(jnp.int32, (128, 128), 1)
    bias = jnp.sum(jnp.where(square, b1_ref[...], 0.0), axis=1, keepdims=True) * 0.5
    high = bias.astype(bf16).astype(f32)
    column = lax.broadcasted_iota(jnp.int32, (128, 24), 1)
    first = lax.dot_general(w1_ref[...], sel1_ref[...], (((0,), (0,)), ((), ())), preferred_element_type=f32)
    first = (first + jnp.where(column == 6, high, 0.0) + jnp.where(column == 7, bias - high, 0.0)).astype(bf16)
    second = jnp.dot(sel2_ref[...], w2_ref[...], preferred_element_type=f32).astype(bf16)

    for c in range(2):
        plane = cells_ref[c].astype(f32)
        for dx in range(3):
            moved = pltpu.roll(plane, 2 * NW - (126 + dx), 1)
            for v in range(3):
                taps[v, pl.ds(3 * c + dx, rows, stride=8), :] = moved[:, v * 128 : (v + 1) * 128]
    for v in range(3):
        for k in (6, 7):
            taps[v, pl.ds(k, rows, stride=8), :] = jnp.ones((rows, 128), f32)

    GROUP = 44
    lane = lax.broadcasted_iota(jnp.int32, (24, 128), 1)
    left_ok = jnp.logical_or(lane > 0, s > 0)
    extra_ok = jnp.logical_and(lane < 2, jnp.logical_or(lane < 1, s < peers - 1))

    def group(g, carry):
        older, old = carry
        windows, extra = [], None
        for j in range(GROUP):
            start = pl.multiple_of((g * GROUP + j + EDGE - 2) * 8, 8)
            windows += [taps[0, pl.ds(start, 24), :], taps[1, pl.ds(start, 24), :]]
            last = jnp.where(lane < 2, taps[2, pl.ds(start, 24), :], 0.0)
            last = pltpu.roll(last, 2 * j, 1) if j else last
            extra = last if extra is None else extra + last
        window = jnp.concatenate([v.astype(bf16) for v in windows + [extra]], 1)
        pre = jnp.dot(first, window, preferred_element_type=f32)
        hidden = (pre + pre * jnp.tanh(pre)).astype(bf16)
        mixed_all = jnp.dot(second, hidden, preferred_element_type=f32)
        tail = mixed_all[:, GROUP * 256 :]
        for j in range(GROUP):
            index = g * GROUP + j
            here = jnp.logical_and(jnp.logical_or(index > 0, t > 0), jnp.logical_or(index < NW + 1, t < tiles - 1))
            last = pltpu.roll(tail, 128 - 2 * j, 1) if j else tail
            mixed = [
                jnp.where(jnp.logical_and(left_ok, here), mixed_all[:, 256 * j : 256 * j + 128], 0.0),
                jnp.where(here, mixed_all[:, 256 * j + 128 : 256 * j + 256], 0.0),
                jnp.where(jnp.logical_and(extra_ok, here), last, 0.0),
            ]
            for v in range(3):
                mixed_sum[v, pl.ds(pl.multiple_of(index * 8, 8), 8), :] = older[v] + mixed[v][16:24]
            older = [old[v] + mixed[v][8:16] for v in range(3)]
            old = [mixed[v][0:8] for v in range(3)]
        return older, old

    zero = [jnp.zeros((8, 128), f32)] * 3
    lax.fori_loop(0, PRIOR_ROWS // GROUP, group, (zero, zero))
    for c in range(2):
        total = None
        for dx in range(3):
            part = jnp.concatenate([mixed_sum[v, pl.ds(16 + 3 * c + dx, NW, stride=8), :] for v in range(3)], 1)
            part = (pltpu.roll(part, 384 - dx, 1) if dx else part)[:, :NW]
            total = part if total is None else total + part
        out_ref[c] = sampled_ref[c] - (total + b2_ref[c])


def subtract_prior(cells, sampled, first_weight, first_bias, second_weight, second_bias):
    tiles, peers = lax.axis_size("tile"), lax.axis_size("scan")
    f32 = jnp.float32
    smem = pl.BlockSpec(memory_space=pltpu.SMEM)
    vmem = pl.BlockSpec(memory_space=pltpu.VMEM)
    one, two = tap_selectors()
    return pl.pallas_call(
        functools.partial(prior_kernel, tiles, peers),
        out_shape=jax.ShapeDtypeStruct((2, NW, NW), f32),
        in_specs=[vmem, vmem, vmem, vmem, vmem, smem, vmem, vmem],
        out_specs=vmem,
        scratch_shapes=[
            pltpu.VMEM((3, 8 * (NW + 2 * EDGE), 128), f32),
            pltpu.VMEM((3, 8 * PRIOR_ROWS, 128), f32),
        ],
        compiler_params=pltpu.CompilerParams(vmem_limit_bytes=32 << 20),
        name="prior",
    )(cells, sampled, first_weight.T, first_bias.reshape(1, -1), second_weight, second_bias, jnp.asarray(one), jnp.asarray(two))


def shards(
    specimen, sampler_noise, probe_field, amplitudes, corner_rows, corner_cols, slot_counts,
    first_weight, first_bias, second_weight, second_bias,
):
    sampled, cells = sample(
        specimen, sampler_noise, probe_field, amplitudes[0, 0],
        corner_rows[0, 0].T, corner_cols[0, 0].T, slot_counts[0, 0],
    )
    return subtract_prior(cells, sampled, first_weight, first_bias, second_weight, second_bias)


def solution(mesh):
    return jax.shard_map(
        shards,
        mesh=mesh,
        in_specs=(
            P(None, "tile", "scan"),
            P(None, "tile", "scan"),
            P(),
            P("tile", "scan", None, None, None, None),
            P("tile", "scan", None, None),
            P("tile", "scan", None, None),
            P("tile", "scan", None),
            P(),
            P(),
            P(),
            P(),
        ),
        out_specs=P(None, "tile", "scan"),
        check_vma=False,
    )
```

```python
import functools

import jax
import jax.numpy as jnp
import numpy as np
from jax import lax
from jax.experimental import pallas as pl
from jax.experimental.pallas import tpu as pltpu
from jax.sharding import PartitionSpec as P

MESH = pl.DeviceIdType.MESH
NW = 256
HALF = 128
EDGE = 16
GROUP = 24
PRIOR_ROWS = 264
CAP = 2

ORDER_16 = [(3, 1), (1, 3), (2, 3), (1, 1), (3, 0), (2, 0), (3, 3), (1, 2), (0, 1), (0, 3), (2, 1), (3, 2), (1, 0), (0, 2), (2, 2)]
ISSUE_16 = [0, 2, 1, 4, 6, 8, 3, 13, 5, 11, 7, 9, 10, 14, 12]
SIDES = [(a, b) for a in (-1, 0, 1) for b in (-1, 0, 1) if (a, b) != (0, 0)]


def dft_matrices():
    index = np.arange(NW)
    angle = (index[:, None] * index[None, :] % NW) * (2.0 * np.pi / NW)
    cosine = (np.cos(angle) / 16.0).astype(jnp.bfloat16)
    sine = (np.sin(angle) / 16.0).astype(jnp.bfloat16)
    forward = np.concatenate([np.concatenate([cosine, sine], 1), np.concatenate([-sine, cosine], 1)], 0)
    return forward, np.ascontiguousarray(forward.T)


def span(step, low, mid, high):
    return {-1: low, 0: mid, 1: high}[step]


def patch_kernel(
    order, issue, rows_y, tiles, peers,
    rows_ref, cols_ref, counts_ref, amps_ref, spec_ref, noise_ref, probe_ref, fwd_ref, inv_ref,
    w1_ref, b1_ref, w2_ref, b2_ref, sel1_ref, sel2_ref,
    out_ref,
    cells_ref, taps, mixed_sum, first_ref, first_edge, second_ref, second_edge,
    recv, frame, acc, rim, rim_in, probe2, rolled, wave_in, mid_ref, far_ref, wave_ref,
    amp_send, amp_recv, own_sem, halo_send, halo_recv, rim_send, rim_recv, ring_send, ring_recv,
):
    f32, bf16 = jnp.float32, jnp.bfloat16
    t = lax.axis_index("tile")
    s = lax.axis_index("scan")
    rows_z = peers // rows_y
    y, z = s // rows_z, lax.rem(s, rows_z)

    mirror = 1 - 2 * lax.rem(t, 2)

    def peer(dy, dz):
        return lax.rem(y + mirror * dy + rows_y, rows_y) * rows_z + lax.rem(z + mirror * dz + rows_z, rows_z)

    def exists(dt, ds):
        ok_t = {-1: t > 0, 0: t >= 0, 1: t < tiles - 1}[dt]
        ok_s = {-1: s > 0, 0: s >= 0, 1: s < peers - 1}[ds]
        return jnp.logical_and(ok_t, ok_s)

    barrier = pltpu.get_barrier_semaphore()
    expected = jnp.int32(len(order))
    for dy, dz in order:
        pl.semaphore_signal(barrier, inc=1, device_id=(t, peer(-dy, -dz)), device_id_type=MESH)
    for dt, ds in SIDES:
        if dt != 0:
            here = exists(dt, ds)
            expected = expected + here.astype(jnp.int32)

            @pl.when(here)
            def _():
                pl.semaphore_signal(barrier, inc=1, device_id=(t + dt, s + ds), device_id_type=MESH)

    own = pltpu.make_async_copy(amps_ref.at[s], recv.at[0], own_sem)
    own.start()
    for part in range(2):
        frame[part, HALF : HALF + NW, HALF : HALF + NW] = spec_ref[part].astype(bf16)
    pl.semaphore_wait(barrier, expected)

    def halo_copy(k, dt, ds):
        src = (slice(None), slice(*span(dt, (128, 256), (128, 384), (256, 384))), slice(*span(ds, (128, 256), (128, 384), (256, 384))))
        dst = (slice(None), slice(*span(dt, (384, 512), (128, 384), (0, 128))), slice(*span(ds, (384, 512), (128, 384), (0, 128))))
        return pltpu.make_async_remote_copy(
            src_ref=frame.at[src], dst_ref=frame.at[dst], send_sem=halo_send.at[k], recv_sem=halo_recv.at[k],
            device_id=(t + dt, s + ds), device_id_type=MESH,
        )

    def amp_copy(k, dy, dz):
        d = peer(dy, dz)
        return pltpu.make_async_remote_copy(
            src_ref=amps_ref.at[d], dst_ref=recv.at[k], send_sem=amp_send.at[k], recv_sem=amp_recv.at[k],
            device_id=(t, d), device_id_type=MESH,
        )

    for k, (dt, ds) in enumerate(SIDES):
        @pl.when(exists(dt, ds))
        def _():
            halo_copy(k, dt, ds).start()

    for part in range(2):
        acc[part] = jnp.zeros((2 * NW, 2 * NW), f32)
        acc[part, HALF : HALF + NW, HALF : HALF + NW] = spec_ref[part] + 0.5 * noise_ref[part]
        for half in range(2):
            columns = probe_ref[part, :, half * HALF : (half + 1) * HALF]
            probe2[part, half, :NW, :] = columns
            probe2[part, half, NW:, :] = columns

    for k, (dt, ds) in enumerate(SIDES):
        here = exists(-dt, -ds)

        @pl.when(here)
        def _():
            halo_copy(k, dt, ds).wait_recv()

        @pl.when(jnp.logical_not(here))
        def _():
            at_row, at_col = span(dt, (384, 512), (128, 384), (0, 128)), span(ds, (384, 512), (128, 384), (0, 128))
            for part in range(2):
                frame[part, slice(*at_row), slice(*at_col)] = jnp.zeros((at_row[1] - at_row[0], at_col[1] - at_col[0]), bf16)

    square = lax.broadcasted_iota(jnp.int32, (128, 128), 0) == lax.broadcasted_iota(jnp.int32, (128, 128), 1)
    bias = jnp.sum(jnp.where(square, b1_ref[...], 0.0), axis=1, keepdims=True) * 0.5
    high = bias.astype(bf16).astype(f32)
    for v in range(3):
        column = lax.broadcasted_iota(jnp.int32, (128, 32), 1)
        at = 24 if v else 6
        weights = lax.dot_general(w1_ref[...], sel1_ref[v], (((0,), (0,)), ((), ())), preferred_element_type=f32)
        weights = (weights + jnp.where(column == at, high, 0.0) + jnp.where(column == at + 1, bias - high, 0.0)).astype(bf16)
        if v == 0:
            first_ref[...] = weights
        else:
            first_edge[(v - 1) * 128 : v * 128, :] = weights
    second_ref[...] = jnp.dot(sel2_ref[0], w2_ref[...], preferred_element_type=f32).astype(bf16)
    for side in range(2):
        for v in range(2):
            second_edge[side, :, v * 128 : (v + 1) * 128] = jnp.dot(
                sel2_ref[1 + 2 * side + v], w2_ref[...], preferred_element_type=f32
            ).astype(bf16)

    CH = 32
    lane = lax.broadcasted_iota(jnp.int32, (CH, NW), 1)
    sub = lax.broadcasted_iota(jnp.int32, (CH, NW), 0)

    def steps_of(k):
        dy, dz = jnp.int32(0), jnp.int32(0)
        for i, (a, b) in enumerate(order):
            dy = jnp.where(k == i + 1, a, dy)
            dz = jnp.where(k == i + 1, b, dz)
        return dy, dz

    def corners(k):
        dy, dz = steps_of(k)
        h = peer(-dy, -dz)
        return h, [(rows_ref[c, h], cols_ref[c, h]) for c in range(CAP)]

    def both(left_ref, right_ref, result):
        for c in range(CAP):
            mid = jnp.dot(left_ref[...], wave_in[:, c * NW : (c + 1) * NW], preferred_element_type=f32)
            for p in range(2):
                mid_ref[c * NW : (c + 1) * NW, p * NW : (p + 1) * NW] = mid[p * NW : (p + 1) * NW].astype(bf16)
        for p in range(2):
            result[:, p * NW : (p + 1) * NW] = jnp.dot(mid_ref[...], right_ref[:, p * NW : (p + 1) * NW], preferred_element_type=f32)

    for k in issue:
        amp_copy(k + 1, *order[k]).start()

    def outward(k, carry):
        h, corner = corners(k)

        def exits(i, carry):
            base = pl.multiple_of(i * CH, CH)
            for c in range(CAP):
                r, q = corner[c]
                low_row = sub + base < r
                low_col = lane < q
                shift = lax.rem(q, NW)
                cell, prb = [], []
                for part in range(2):
                    tile = [[frame[part, pl.ds(base + a * NW, CH), b * NW : (b + 1) * NW].astype(f32) for b in range(2)] for a in range(2)]
                    cell.append(jnp.where(low_row, jnp.where(low_col, tile[1][1], tile[1][0]), jnp.where(low_col, tile[0][1], tile[0][0])))
                    turned = pltpu.roll(jnp.concatenate([probe2[part, half, pl.ds(base + NW - r, CH), :] for half in range(2)], 1), shift, 1)
                    rolled[k, c, part, pl.ds(base, CH), :] = turned
                    prb.append(turned)
                wave_in[pl.ds(base, CH), c * NW : (c + 1) * NW] = (prb[0] * cell[0] - prb[1] * cell[1]).astype(bf16)
                wave_in[pl.ds(base + NW, CH), c * NW : (c + 1) * NW] = (prb[0] * cell[1] + prb[1] * cell[0]).astype(bf16)
            return carry

        lax.fori_loop(0, NW // CH, exits, 0, unroll=True)
        both(fwd_ref, inv_ref, far_ref.at[k])
        return carry

    lax.fori_loop(0, len(order) + 1, outward, 0, unroll=2)
    own.wait()

    def inward(k, carry):
        h, corner = corners(k)
        dy, dz = steps_of(k)
        scale = [jnp.where(counts_ref[h] > c, f32(-0.25), f32(0.0)) for c in range(CAP)]

        @pl.when(k > 0)
        def _():
            pltpu.make_async_remote_copy(
                src_ref=recv.at[k], dst_ref=recv.at[k], send_sem=amp_send.at[k], recv_sem=amp_recv.at[k],
                device_id=(t, peer(dy, dz)), device_id_type=MESH,
            ).wait_recv()

        def correct(i, carry):
            base = pl.multiple_of(i * CH, CH)
            for c in range(CAP):
                fr = far_ref[k, pl.ds(base + c * NW, CH), :NW]
                fi = far_ref[k, pl.ds(base + c * NW, CH), NW:]
                amp = recv[k, c, pl.ds(base, CH), :].astype(f32)
                keep = 1.0 - amp * lax.rsqrt(jnp.maximum(fr * fr + fi * fi, 1.0))
                wave_in[pl.ds(base, CH), c * NW : (c + 1) * NW] = (fr * keep).astype(bf16)
                wave_in[pl.ds(base + NW, CH), c * NW : (c + 1) * NW] = (fi * keep).astype(bf16)
            return carry

        lax.fori_loop(0, NW // CH, correct, 0, unroll=True)
        both(inv_ref, fwd_ref, wave_ref)

        def gather(i, carry):
            base = pl.multiple_of(i * CH, CH)
            grads = []
            for c in range(CAP):
                wr = wave_ref[pl.ds(base + c * NW, CH), :NW]
                wi = wave_ref[pl.ds(base + c * NW, CH), NW:]
                pr = rolled[k, c, 0, pl.ds(base, CH), :] * scale[c]
                pi = rolled[k, c, 1, pl.ds(base, CH), :] * scale[c]
                grads.append((pr * wr + pi * wi, pr * wi - pi * wr))
            for a in range(2):
                for b in range(2):
                    masks = []
                    for c in range(CAP):
                        r, q = corner[c]
                        row_ok = sub + base < r if a else sub + base >= r
                        col_ok = lane < q if b else lane >= q
                        masks.append(jnp.logical_and(row_ok, col_ok))
                    for part in range(2):
                        total = acc[part, pl.ds(base + a * NW, CH), b * NW : (b + 1) * NW]
                        for c in range(CAP):
                            total = total + jnp.where(masks[c], grads[c][part], 0.0)
                        acc[part, pl.ds(base + a * NW, CH), b * NW : (b + 1) * NW] = total
            return carry

        lax.fori_loop(0, NW // CH, gather, 0, unroll=True)
        return carry

    lax.fori_loop(0, len(order) + 1, inward, 0, unroll=2)

    for part in range(2):
        for lo, hi in ((0, HALF), (HALF + NW, 2 * NW)):
            rim[part, lo:hi, :] = acc[part, lo:hi, :].astype(bf16)
            rim[part, HALF : HALF + NW, lo:hi] = acc[part, HALF : HALF + NW, lo:hi].astype(bf16)

    def rim_copy(k, dt, ds):
        where = (slice(None), slice(*span(dt, (0, 128), (128, 384), (384, 512))), slice(*span(ds, (0, 128), (128, 384), (384, 512))))
        return pltpu.make_async_remote_copy(
            src_ref=rim.at[where], dst_ref=rim_in.at[where], send_sem=rim_send.at[k], recv_sem=rim_recv.at[k],
            device_id=(t + dt, s + ds), device_id_type=MESH,
        )

    for k, (dt, ds) in enumerate(SIDES):
        @pl.when(exists(dt, ds))
        def _():
            rim_copy(k, dt, ds).start()
    for part in range(2):
        out_ref[part] = acc[part, HALF : HALF + NW, HALF : HALF + NW]
    for k, (dt, ds) in enumerate(SIDES):
        @pl.when(exists(-dt, -ds))
        def _():
            rim_copy(k, dt, ds).wait_recv()
            src_r, dst_r = span(dt, ((0, 128), (128, 256)), ((128, 384), (0, 256)), ((384, 512), (0, 128)))
            src_c, dst_c = span(ds, ((0, 128), (128, 256)), ((128, 384), (0, 256)), ((384, 512), (0, 128)))
            for part in range(2):
                out_ref[part, slice(*dst_r), slice(*dst_c)] += rim_in[part, slice(*src_r), slice(*src_c)].astype(f32)
    for part in range(2):
        cells_ref[part, EDGE : EDGE + NW, HALF : HALF + NW] = out_ref[part].astype(bf16)

    def ring_copy(k, dt, ds):
        src = (slice(None), slice(*span(dt, (16, 32), (16, 272), (256, 272))), slice(*span(ds, (128, 256), (128, 384), (256, 384))))
        dst = (slice(None), slice(*span(dt, (272, 288), (16, 272), (0, 16))), slice(*span(ds, (384, 512), (128, 384), (0, 128))))
        return pltpu.make_async_remote_copy(
            src_ref=cells_ref.at[src], dst_ref=cells_ref.at[dst], send_sem=ring_send.at[k], recv_sem=ring_recv.at[k],
            device_id=(t + dt, s + ds), device_id_type=MESH,
        )

    for k, (dt, ds) in enumerate(SIDES):
        @pl.when(exists(dt, ds))
        def _():
            ring_copy(k, dt, ds).start()
    def moved(rows256, dx):
        return rows256 if dx == 1 else pltpu.roll(rows256, 1 if dx == 0 else NW - 1, 1)

    for part in range(2):
        for dx in range(3):
            shifted = moved(out_ref[part], dx)
            for v in range(2):
                taps[v, pl.ds(16 + 3 * part + dx, NW, stride=8), :] = shifted[:, v * 128 : (v + 1) * 128]
    for v in range(2):
        for k in (6, 7):
            taps[v, pl.ds(k, NW + 4, stride=8), :] = jnp.ones((NW + 4, 128), f32)

    mlane = lax.broadcasted_iota(jnp.int32, (24, 128), 1)
    inner = (mlane > 0, mlane < 127)

    def hidden_of(weights, window):
        pre = jnp.dot(weights, window, preferred_element_type=f32)
        return pre + pre * jnp.tanh(pre)

    def mixed_rows(starts):
        window = jnp.concatenate([taps[v, pl.ds(start, 24), :].astype(bf16) for start in starts for v in range(2)], 1)
        return jnp.dot(second_ref[...], hidden_of(first_ref[:, :24], window).astype(bf16), preferred_element_type=f32)

    def group(g, carry):
        older, old = carry
        mixed_all = mixed_rows([pl.multiple_of((g * GROUP + j) * 8, 8) for j in range(GROUP)])
        for j in range(GROUP):
            index = g * GROUP + j
            here = jnp.logical_and(index > 1, index < NW)
            mixed = [jnp.where(jnp.logical_and(inner[v], here), mixed_all[:, (2 * j + v) * 128 : (2 * j + v + 1) * 128], 0.0) for v in range(2)]
            for v in range(2):
                mixed_sum[v, pl.ds(pl.multiple_of(index * 8, 8), 8), :] = older[v] + mixed[v][16:24]
            older = [old[v] + mixed[v][8:16] for v in range(2)]
            old = [mixed[v][0:8] for v in range(2)]
        return older, old

    zero = [jnp.zeros((8, 128), f32)] * 2
    lax.fori_loop(0, PRIOR_ROWS // GROUP, group, (zero, zero))

    for k, (dt, ds) in enumerate(SIDES):
        here = exists(-dt, -ds)

        @pl.when(here)
        def _():
            ring_copy(k, dt, ds).wait_recv()

        @pl.when(jnp.logical_not(here))
        def _():
            at_row, at_col = span(dt, (272, 288), (16, 272), (0, 16)), span(ds, (384, 512), (128, 384), (0, 128))
            for part in range(2):
                cells_ref[part, slice(*at_row), slice(*at_col)] = jnp.zeros((at_row[1] - at_row[0], at_col[1] - at_col[0]), bf16)

    for part in range(2):
        for at, first_row, take in ((0, 0, 14), (NW + 2, EDGE + NW, 0)):
            strip = cells_ref[part, first_row : first_row + EDGE, HALF : HALF + NW].astype(f32)
            for dx in range(3):
                shifted = moved(strip, dx)
                for v in range(2):
                    for i in range(2):
                        taps[v, (at + i) * 8 + 3 * part + dx : (at + i) * 8 + 3 * part + dx + 1, :] = shifted[take + i : take + i + 1, v * 128 : (v + 1) * 128]
    border = (0, 1, NW, NW + 1)
    mixed_all = mixed_rows([8 * index for index in border])
    for j, index in enumerate(border):
        here = {0: t > 0, NW + 1: t < tiles - 1}.get(index, t >= 0)
        for v in range(2):
            mixed = jnp.where(jnp.logical_and(inner[v], here), mixed_all[:, (2 * j + v) * 128 : (2 * j + v + 1) * 128], 0.0)
            for dy in range(3):
                row = index + 2 - dy
                if 2 <= row < NW + 2:
                    mixed_sum[v, row * 8 : row * 8 + 8, :] += mixed[8 * dy : 8 * dy + 8]

    WIDE = 384
    strip_lane = lax.broadcasted_iota(jnp.int32, (NW + 2 * EDGE, 128), 1)
    row_lane = lax.broadcasted_iota(jnp.int32, (8, WIDE), 1)
    constant = jnp.where(lax.broadcasted_iota(jnp.int32, (8, WIDE), 0) < 2, 1.0, 0.0)
    edge_sum = None
    for side in range(2):
        planes = [cells_ref[part, :, side * NW : (side + 1) * NW].astype(f32) for part in range(2)]
        strips = [pltpu.roll(planes[part], NW - 126 + 4 * part, 1)[:, :128] for part in range(2)]
        strip = jnp.where(strip_lane < 4, strips[0], strips[1])
        strip = jnp.concatenate([strip, jnp.zeros((WIDE - NW - 2 * EDGE, 128), f32)], 0).T[:8]
        window = jnp.concatenate([pltpu.roll(strip, 1, 1), strip, pltpu.roll(strip, WIDE - 1, 1), constant], 0).astype(bf16)
        hidden = hidden_of(first_edge[...], window)
        outer = lax.broadcasted_iota(jnp.int32, (NW, WIDE), 0) < 128 if side == 0 else lax.broadcasted_iota(jnp.int32, (NW, WIDE), 0) >= 128
        gone = s == 0 if side == 0 else s == peers - 1
        hidden = jnp.where(jnp.logical_and(outer, gone), 0.0, hidden).astype(bf16)
        mixed = jnp.dot(second_edge[side], hidden, preferred_element_type=f32)
        edge_sum = mixed if edge_sum is None else edge_sum + mixed
    by_dy = []
    for dy in range(3):
        piece = edge_sum[8 * dy : 8 * dy + 8]
        piece = jnp.where(jnp.logical_and(row_lane == EDGE - 1, t == 0), 0.0, piece)
        piece = jnp.where(jnp.logical_and(row_lane == EDGE + NW, t == tiles - 1), 0.0, piece)
        by_dy.append(piece if dy == 1 else pltpu.roll(piece, 1 if dy == 0 else WIDE - 1, 1))
    columns = by_dy[0] + by_dy[1] + by_dy[2]
    columns = jnp.concatenate([columns, jnp.zeros((120, WIDE), f32)], 0).T[EDGE : EDGE + NW]
    out_lane = lax.broadcasted_iota(jnp.int32, (NW, 128), 1)
    for part in range(2):
        halves = [jnp.zeros((NW, 128), f32), jnp.zeros((NW, 128), f32)]
        for dx in range(3):
            sums = jnp.concatenate([mixed_sum[v, pl.ds(16 + 3 * part + dx, NW, stride=8), :] for v in range(2)], 1)
            sums = sums if dx == 1 else pltpu.roll(sums, 1 if dx == 0 else NW - 1, 1)
            halves = [halves[v] + sums[:, v * 128 : (v + 1) * 128] for v in range(2)]
        left = pltpu.roll(columns, (128 - 2 * part) % 128, 1) if part else columns
        right = pltpu.roll(columns, 126 - 4 - 2 * part, 1)
        halves[0] = halves[0] + jnp.where(out_lane < 2, left, 0.0)
        halves[1] = halves[1] + jnp.where(out_lane >= 126, right, 0.0)
        for v in range(2):
            at = slice(v * 128, (v + 1) * 128)
            out_ref[part, :, at] = out_ref[part, :, at] - (halves[v] + b2_ref[part])
    for k, (dt, ds) in enumerate(SIDES):
        @pl.when(exists(dt, ds))
        def _():
            ring_copy(k, dt, ds).wait_send()
            halo_copy(k, dt, ds).wait_send()
            rim_copy(k, dt, ds).wait_send()
    for k, (dy, dz) in enumerate(order):
        amp_copy(k + 1, dy, dz).wait_send()


def sample(specimen, noise, probe, amps, rows, cols, counts, w1, b1, w2, b2):
    tiles, peers = lax.axis_size("tile"), lax.axis_size("scan")
    if peers == 16:
        order, issue, rows_y = ORDER_16, ISSUE_16, 4
    else:
        order, issue, rows_y = [(0, b) for b in range(1, peers)], list(range(peers - 1)), 1
    forward, inverse = dft_matrices()
    one, two = tap_selectors()
    f32, bf16 = jnp.float32, jnp.bfloat16
    smem = pl.BlockSpec(memory_space=pltpu.SMEM)
    vmem = pl.BlockSpec(memory_space=pltpu.VMEM)
    dma = pltpu.SemaphoreType.DMA
    return pl.pallas_call(
        functools.partial(patch_kernel, order, issue, rows_y, tiles, peers),
        out_shape=jax.ShapeDtypeStruct((2, NW, NW), f32),
        in_specs=[smem, smem, smem, pl.BlockSpec(memory_space=pl.ANY)] + [vmem] * 5 + [vmem, vmem, vmem, smem, vmem, vmem],
        out_specs=vmem,
        scratch_shapes=[
            pltpu.VMEM((2, NW + 2 * EDGE, 2 * NW), bf16),
            pltpu.VMEM((2, 8 * (PRIOR_ROWS + 2), 128), f32),
            pltpu.VMEM((2, 8 * PRIOR_ROWS, 128), f32),
            pltpu.VMEM((128, 32), bf16),
            pltpu.VMEM((NW, 32), bf16),
            pltpu.VMEM((24, 128), bf16),
            pltpu.VMEM((2, 24, NW), bf16),
            pltpu.VMEM((peers, CAP, NW, NW), bf16),
            pltpu.VMEM((2, 2 * NW, 2 * NW), bf16),
            pltpu.VMEM((2, 2 * NW, 2 * NW), f32),
            pltpu.VMEM((2, 2 * NW, 2 * NW), bf16),
            pltpu.VMEM((2, 2 * NW, 2 * NW), bf16),
            pltpu.VMEM((2, 2, 2 * NW, HALF), f32),
            pltpu.VMEM((peers, CAP, 2, NW, NW), f32),
            pltpu.VMEM((2 * NW, 2 * NW), bf16),
            pltpu.VMEM((2 * NW, 2 * NW), bf16),
            pltpu.VMEM((peers, 2 * NW, 2 * NW), f32),
            pltpu.VMEM((2 * NW, 2 * NW), f32),
            dma((peers,)), dma((peers,)), dma, dma((8,)), dma((8,)), dma((8,)), dma((8,)), dma((8,)), dma((8,)),
        ],
        compiler_params=pltpu.CompilerParams(collective_id=0, has_side_effects=True, vmem_limit_bytes=60 << 20),
        name="step",
    )(rows, cols, counts, amps, specimen, noise, probe, jnp.asarray(forward), jnp.asarray(inverse),
      w1, b1, w2, b2, jnp.asarray(one), jnp.asarray(two))


def tap_selectors():
    first = np.zeros((3, 18, 32), np.float32)
    second = np.zeros((5, 24, 18), np.float32)
    for c in range(2):
        for dy in range(3):
            for dx in range(3):
                tap = 9 * c + 3 * dy + dx
                first[0, tap, 8 * dy + 3 * c + dx] = 0.5
                first[1, tap, 8 * dy + 4 * c + dx] = 0.5
                first[2, tap, 8 * dy + 4 * c + dx + 1] = 0.5
                second[0, 8 * dy + 3 * c + dx, tap] = 1.0
            for side, half, dx, at in ((0, 0, 0, 0), (0, 1, 1, 0), (0, 1, 0, 1), (1, 0, 2, 0), (1, 0, 1, 1), (1, 1, 2, 1)):
                second[1 + 2 * side + half, 8 * dy + 4 * side + 2 * c + at, 9 * c + 3 * dy + dx] = 1.0
    return first.astype(jnp.bfloat16), second.astype(jnp.bfloat16)


def shards(
    specimen, sampler_noise, probe_field, amplitudes, corner_rows, corner_cols, slot_counts,
    first_weight, first_bias, second_weight, second_bias,
):
    return sample(
        specimen, sampler_noise, probe_field, amplitudes[0, 0],
        corner_rows[0, 0].T, corner_cols[0, 0].T, slot_counts[0, 0],
        first_weight.T, first_bias.reshape(1, -1), second_weight, second_bias,
    )


def solution(mesh):
    return jax.shard_map(
        shards,
        mesh=mesh,
        in_specs=(
            P(None, "tile", "scan"),
            P(None, "tile", "scan"),
            P(),
            P("tile", "scan", None, None, None, None),
            P("tile", "scan", None, None),
            P("tile", "scan", None, None),
            P("tile", "scan", None),
            P(),
            P(),
            P(),
            P(),
        ),
        out_specs=P(None, "tile", "scan"),
        check_vma=False,
    )
```

```python
import functools

import jax
import jax.numpy as jnp
import numpy as np
from jax import lax
from jax.experimental import pallas as pl
from jax.experimental.pallas import tpu as pltpu
from jax.sharding import PartitionSpec as P

MESH = pl.DeviceIdType.MESH
NW = 256
HALF = 128
EDGE = 16
GROUP = 24
PRIOR_ROWS = 264
CAP = 2

ORDER_16 = [(3, 1), (1, 3), (2, 3), (1, 1), (3, 0), (2, 0), (3, 3), (1, 2), (0, 1), (0, 3), (2, 1), (3, 2), (1, 0), (0, 2), (2, 2)]
ISSUE_16 = [0, 2, 1, 4, 6, 8, 3, 13, 5, 11, 7, 9, 10, 14, 12]
SIDES = [(a, b) for a in (-1, 0, 1) for b in (-1, 0, 1) if (a, b) != (0, 0)]


def dft_matrices():
    index = np.arange(NW)
    angle = (index[:, None] * index[None, :] % NW) * (2.0 * np.pi / NW)
    cosine = (np.cos(angle) / 16.0).astype(jnp.bfloat16)
    sine = (np.sin(angle) / 16.0).astype(jnp.bfloat16)
    forward = np.concatenate([np.concatenate([cosine, sine], 1), np.concatenate([-sine, cosine], 1)], 0)
    return forward, np.ascontiguousarray(forward.T)


def span(step, low, mid, high):
    return {-1: low, 0: mid, 1: high}[step]


def patch_kernel(
    order, issue, rows_y, tiles, peers,
    rows_ref, cols_ref, counts_ref, amps_ref, spec_hbm, noise_hbm, probe_hbm, fwd_hbm, inv_hbm,
    w1_ref, b1_ref, w2_ref, b2_ref, sel1_ref, sel2_ref,
    out_ref,
    spec_ref, noise_ref, probe_ref, fwd_ref, inv_ref, load_sem,
    cells_ref, taps, mixed_sum, first_ref, first_edge, second_ref, second_edge,
    recv, frame, acc, rim, rim_in, probe2, rolled, wave_in, mid_ref, far_ref, wave_ref,
    amp_send, amp_recv, own_sem, halo_send, halo_recv, rim_send, rim_recv, ring_send, ring_recv,
):
    f32, bf16 = jnp.float32, jnp.bfloat16
    t = lax.axis_index("tile")
    s = lax.axis_index("scan")
    rows_z = peers // rows_y
    y, z = s // rows_z, lax.rem(s, rows_z)

    mirror = 1 - 2 * lax.rem(t, 2)

    def peer(dy, dz):
        return lax.rem(y + mirror * dy + rows_y, rows_y) * rows_z + lax.rem(z + mirror * dz + rows_z, rows_z)

    def exists(dt, ds):
        ok_t = {-1: t > 0, 0: t >= 0, 1: t < tiles - 1}[dt]
        ok_s = {-1: s > 0, 0: s >= 0, 1: s < peers - 1}[ds]
        return jnp.logical_and(ok_t, ok_s)

    barrier = pltpu.get_barrier_semaphore()
    expected = jnp.int32(len(order))
    for dy, dz in order:
        pl.semaphore_signal(barrier, inc=1, device_id=(t, peer(-dy, -dz)), device_id_type=MESH)
    for dt, ds in SIDES:
        if dt != 0:
            here = exists(dt, ds)
            expected = expected + here.astype(jnp.int32)

            @pl.when(here)
            def _():
                pl.semaphore_signal(barrier, inc=1, device_id=(t + dt, s + ds), device_id_type=MESH)

    loads = [
        pltpu.make_async_copy(source, place, load_sem.at[i])
        for i, (source, place) in enumerate(
            ((spec_hbm, spec_ref), (noise_hbm, noise_ref), (probe_hbm, probe_ref), (fwd_hbm, fwd_ref), (inv_hbm, inv_ref))
        )
    ]
    for load in loads:
        load.start()
    own = pltpu.make_async_copy(amps_ref.at[s], recv.at[0], own_sem)
    own.start()
    loads[0].wait()
    for part in range(2):
        frame[part, HALF : HALF + NW, HALF : HALF + NW] = spec_ref[part].astype(bf16)
    pl.semaphore_wait(barrier, expected)

    def halo_copy(k, dt, ds):
        src = (slice(None), slice(*span(dt, (128, 256), (128, 384), (256, 384))), slice(*span(ds, (128, 256), (128, 384), (256, 384))))
        dst = (slice(None), slice(*span(dt, (384, 512), (128, 384), (0, 128))), slice(*span(ds, (384, 512), (128, 384), (0, 128))))
        return pltpu.make_async_remote_copy(
            src_ref=frame.at[src], dst_ref=frame.at[dst], send_sem=halo_send.at[k], recv_sem=halo_recv.at[k],
            device_id=(t + dt, s + ds), device_id_type=MESH,
        )

    def relay_copy(k, dt, ds):
        columns = span(ds, slice(384, 512), None, slice(0, 128))
        return pltpu.make_async_remote_copy(
            src_ref=frame.at[:, span(dt, slice(128, 256), None, slice(256, 384)), columns],
            dst_ref=frame.at[:, span(dt, slice(384, 512), None, slice(0, 128)), columns],
            send_sem=halo_send.at[k], recv_sem=halo_recv.at[k], device_id=(t + dt, s), device_id_type=MESH,
        )

    def amp_copy(k, dy, dz):
        d = peer(dy, dz)
        return pltpu.make_async_remote_copy(
            src_ref=amps_ref.at[d], dst_ref=recv.at[k], send_sem=amp_send.at[k], recv_sem=amp_recv.at[k],
            device_id=(t, d), device_id_type=MESH,
        )

    straight = [(k, dt, ds) for k, (dt, ds) in enumerate(SIDES) if dt * ds == 0]
    diagonal = [(k, dt, ds) for k, (dt, ds) in enumerate(SIDES) if dt * ds != 0]
    for k, dt, ds in straight:
        @pl.when(exists(dt, ds))
        def _():
            halo_copy(k, dt, ds).start()

    for load in loads[1:]:
        load.wait()
    for part in range(2):
        acc[part] = jnp.zeros((2 * NW, 2 * NW), f32)
        acc[part, HALF : HALF + NW, HALF : HALF + NW] = spec_ref[part] + 0.5 * noise_ref[part]
        for half in range(2):
            columns = probe_ref[part, :, half * HALF : (half + 1) * HALF]
            probe2[part, half, :NW, :] = columns
            probe2[part, half, NW:, :] = columns

    def take_halo(k, dt, ds, copy):
        here = exists(-dt, -ds)

        @pl.when(here)
        def _():
            copy(k, dt, ds).wait_recv()

        @pl.when(jnp.logical_not(here))
        def _():
            at_row, at_col = span(dt, (384, 512), (128, 384), (0, 128)), span(ds, (384, 512), (128, 384), (0, 128))
            for part in range(2):
                frame[part, slice(*at_row), slice(*at_col)] = jnp.zeros((at_row[1] - at_row[0], at_col[1] - at_col[0]), bf16)

    for k, dt, ds in straight:
        take_halo(k, dt, ds, halo_copy)
    for k, dt, ds in diagonal:
        @pl.when(jnp.logical_and(exists(dt, 0), exists(0, -ds)))
        def _():
            relay_copy(k, dt, ds).start()
    for k in issue:
        amp_copy(k + 1, *order[k]).start()
    for k, dt, ds in diagonal:
        take_halo(k, dt, ds, relay_copy)

    square = lax.broadcasted_iota(jnp.int32, (128, 128), 0) == lax.broadcasted_iota(jnp.int32, (128, 128), 1)
    bias = jnp.sum(jnp.where(square, b1_ref[...], 0.0), axis=1, keepdims=True) * 0.5
    high = bias.astype(bf16).astype(f32)
    for v in range(3):
        column = lax.broadcasted_iota(jnp.int32, (128, 32), 1)
        at = 24 if v else 6
        weights = lax.dot_general(w1_ref[...], sel1_ref[v], (((0,), (0,)), ((), ())), preferred_element_type=f32)
        weights = (weights + jnp.where(column == at, high, 0.0) + jnp.where(column == at + 1, bias - high, 0.0)).astype(bf16)
        if v == 0:
            first_ref[...] = weights
        else:
            first_edge[(v - 1) * 128 : v * 128, :] = weights
    second_ref[...] = jnp.dot(sel2_ref[0], w2_ref[...], preferred_element_type=f32).astype(bf16)
    for side in range(2):
        for v in range(2):
            second_edge[side, :, v * 128 : (v + 1) * 128] = jnp.dot(
                sel2_ref[1 + 2 * side + v], w2_ref[...], preferred_element_type=f32
            ).astype(bf16)

    CH = 32
    lane = lax.broadcasted_iota(jnp.int32, (CH, NW), 1)
    sub = lax.broadcasted_iota(jnp.int32, (CH, NW), 0)

    def steps_of(k):
        dy, dz = jnp.int32(0), jnp.int32(0)
        for i, (a, b) in enumerate(order):
            dy = jnp.where(k == i + 1, a, dy)
            dz = jnp.where(k == i + 1, b, dz)
        return dy, dz

    def corners(k):
        dy, dz = steps_of(k)
        h = peer(-dy, -dz)
        return h, [(rows_ref[c, h], cols_ref[c, h]) for c in range(CAP)]

    def both(left_ref, right_ref, result):
        for c in range(CAP):
            mid = jnp.dot(left_ref[...], wave_in[:, c * NW : (c + 1) * NW], preferred_element_type=f32)
            for p in range(2):
                mid_ref[c * NW : (c + 1) * NW, p * NW : (p + 1) * NW] = mid[p * NW : (p + 1) * NW].astype(bf16)
        for p in range(2):
            result[:, p * NW : (p + 1) * NW] = jnp.dot(mid_ref[...], right_ref[:, p * NW : (p + 1) * NW], preferred_element_type=f32)


    def outward(k, carry):
        h, corner = corners(k)

        def exits(i, carry):
            base = pl.multiple_of(i * CH, CH)
            for c in range(CAP):
                r, q = corner[c]
                low_row = sub + base < r
                low_col = lane < q
                shift = lax.rem(q, NW)
                cell, prb = [], []
                for part in range(2):
                    tile = [[frame[part, pl.ds(base + a * NW, CH), b * NW : (b + 1) * NW].astype(f32) for b in range(2)] for a in range(2)]
                    cell.append(jnp.where(low_row, jnp.where(low_col, tile[1][1], tile[1][0]), jnp.where(low_col, tile[0][1], tile[0][0])))
                    turned = pltpu.roll(jnp.concatenate([probe2[part, half, pl.ds(base + NW - r, CH), :] for half in range(2)], 1), shift, 1)
                    rolled[k, c, part, pl.ds(base, CH), :] = turned
                    prb.append(turned)
                wave_in[pl.ds(base, CH), c * NW : (c + 1) * NW] = (prb[0] * cell[0] - prb[1] * cell[1]).astype(bf16)
                wave_in[pl.ds(base + NW, CH), c * NW : (c + 1) * NW] = (prb[0] * cell[1] + prb[1] * cell[0]).astype(bf16)
            return carry

        lax.fori_loop(0, NW // CH, exits, 0, unroll=True)
        both(fwd_ref, inv_ref, far_ref.at[k])
        return carry

    lax.fori_loop(0, len(order) + 1, outward, 0, unroll=2)
    own.wait()

    def inward(k, carry):
        h, corner = corners(k)
        dy, dz = steps_of(k)
        scale = [jnp.where(counts_ref[h] > c, f32(-0.25), f32(0.0)) for c in range(CAP)]

        @pl.when(k > 0)
        def _():
            pltpu.make_async_remote_copy(
                src_ref=recv.at[k], dst_ref=recv.at[k], send_sem=amp_send.at[k], recv_sem=amp_recv.at[k],
                device_id=(t, peer(dy, dz)), device_id_type=MESH,
            ).wait_recv()

        def correct(i, carry):
            base = pl.multiple_of(i * CH, CH)
            for c in range(CAP):
                fr = far_ref[k, pl.ds(base + c * NW, CH), :NW]
                fi = far_ref[k, pl.ds(base + c * NW, CH), NW:]
                amp = recv[k, c, pl.ds(base, CH), :].astype(f32)
                keep = 1.0 - amp * lax.rsqrt(jnp.maximum(fr * fr + fi * fi, 1.0))
                wave_in[pl.ds(base, CH), c * NW : (c + 1) * NW] = (fr * keep).astype(bf16)
                wave_in[pl.ds(base + NW, CH), c * NW : (c + 1) * NW] = (fi * keep).astype(bf16)
            return carry

        lax.fori_loop(0, NW // CH, correct, 0, unroll=True)
        both(inv_ref, fwd_ref, wave_ref)

        def gather(i, carry):
            base = pl.multiple_of(i * CH, CH)
            grads = []
            for c in range(CAP):
                wr = wave_ref[pl.ds(base + c * NW, CH), :NW]
                wi = wave_ref[pl.ds(base + c * NW, CH), NW:]
                pr = rolled[k, c, 0, pl.ds(base, CH), :] * scale[c]
                pi = rolled[k, c, 1, pl.ds(base, CH), :] * scale[c]
                grads.append((pr * wr + pi * wi, pr * wi - pi * wr))
            for a in range(2):
                for b in range(2):
                    masks = []
                    for c in range(CAP):
                        r, q = corner[c]
                        row_ok = sub + base < r if a else sub + base >= r
                        col_ok = lane < q if b else lane >= q
                        masks.append(jnp.logical_and(row_ok, col_ok))
                    for part in range(2):
                        total = acc[part, pl.ds(base + a * NW, CH), b * NW : (b + 1) * NW]
                        for c in range(CAP):
                            total = total + jnp.where(masks[c], grads[c][part], 0.0)
                        acc[part, pl.ds(base + a * NW, CH), b * NW : (b + 1) * NW] = total
            return carry

        lax.fori_loop(0, NW // CH, gather, 0, unroll=True)
        return carry

    lax.fori_loop(0, len(order) + 1, inward, 0, unroll=2)

    for part in range(2):
        for lo, hi in ((0, HALF), (HALF + NW, 2 * NW)):
            rim[part, lo:hi, :] = acc[part, lo:hi, :].astype(bf16)
            rim[part, HALF : HALF + NW, lo:hi] = acc[part, HALF : HALF + NW, lo:hi].astype(bf16)

    def rim_copy(k, dt, ds):
        where = (slice(None), slice(*span(dt, (0, 128), (128, 384), (384, 512))), slice(*span(ds, (0, 128), (128, 384), (384, 512))))
        return pltpu.make_async_remote_copy(
            src_ref=rim.at[where], dst_ref=rim_in.at[where], send_sem=rim_send.at[k], recv_sem=rim_recv.at[k],
            device_id=(t + dt, s + ds), device_id_type=MESH,
        )

    for k, (dt, ds) in enumerate(SIDES):
        @pl.when(exists(dt, ds))
        def _():
            rim_copy(k, dt, ds).start()
    for part in range(2):
        out_ref[part] = acc[part, HALF : HALF + NW, HALF : HALF + NW]
    for k, (dt, ds) in enumerate(SIDES):
        @pl.when(exists(-dt, -ds))
        def _():
            rim_copy(k, dt, ds).wait_recv()
            src_r, dst_r = span(dt, ((0, 128), (128, 256)), ((128, 384), (0, 256)), ((384, 512), (0, 128)))
            src_c, dst_c = span(ds, ((0, 128), (128, 256)), ((128, 384), (0, 256)), ((384, 512), (0, 128)))
            for part in range(2):
                out_ref[part, slice(*dst_r), slice(*dst_c)] += rim_in[part, slice(*src_r), slice(*src_c)].astype(f32)
    for part in range(2):
        cells_ref[part, EDGE : EDGE + NW, HALF : HALF + NW] = out_ref[part].astype(bf16)

    def ring_copy(k, dt, ds):
        src = (slice(None), slice(*span(dt, (16, 32), (16, 272), (256, 272))), slice(*span(ds, (128, 256), (128, 384), (256, 384))))
        dst = (slice(None), slice(*span(dt, (272, 288), (16, 272), (0, 16))), slice(*span(ds, (384, 512), (128, 384), (0, 128))))
        return pltpu.make_async_remote_copy(
            src_ref=cells_ref.at[src], dst_ref=cells_ref.at[dst], send_sem=ring_send.at[k], recv_sem=ring_recv.at[k],
            device_id=(t + dt, s + ds), device_id_type=MESH,
        )

    for k, (dt, ds) in enumerate(SIDES):
        @pl.when(exists(dt, ds))
        def _():
            ring_copy(k, dt, ds).start()
    def moved(rows256, dx):
        return rows256 if dx == 1 else pltpu.roll(rows256, 1 if dx == 0 else NW - 1, 1)

    for part in range(2):
        for dx in range(3):
            shifted = moved(out_ref[part], dx)
            for v in range(2):
                taps[v, pl.ds(16 + 3 * part + dx, NW, stride=8), :] = shifted[:, v * 128 : (v + 1) * 128]
    for v in range(2):
        for k in (6, 7):
            taps[v, pl.ds(k, NW + 4, stride=8), :] = jnp.ones((NW + 4, 128), f32)

    mlane = lax.broadcasted_iota(jnp.int32, (24, 128), 1)
    inner = (mlane > 0, mlane < 127)

    def hidden_of(weights, window):
        pre = jnp.dot(weights, window, preferred_element_type=f32)
        return pre + pre * jnp.tanh(pre)

    def mixed_rows(starts):
        window = jnp.concatenate([taps[v, pl.ds(start, 24), :].astype(bf16) for start in starts for v in range(2)], 1)
        return jnp.dot(second_ref[...], hidden_of(first_ref[:, :24], window).astype(bf16), preferred_element_type=f32)

    def group(g, carry):
        older, old = carry
        mixed_all = mixed_rows([pl.multiple_of((g * GROUP + j) * 8, 8) for j in range(GROUP)])
        for j in range(GROUP):
            index = g * GROUP + j
            here = jnp.logical_and(index > 1, index < NW)
            mixed = [jnp.where(jnp.logical_and(inner[v], here), mixed_all[:, (2 * j + v) * 128 : (2 * j + v + 1) * 128], 0.0) for v in range(2)]
            for v in range(2):
                mixed_sum[v, pl.ds(pl.multiple_of(index * 8, 8), 8), :] = older[v] + mixed[v][16:24]
            older = [old[v] + mixed[v][8:16] for v in range(2)]
            old = [mixed[v][0:8] for v in range(2)]
        return older, old

    zero = [jnp.zeros((8, 128), f32)] * 2
    lax.fori_loop(0, PRIOR_ROWS // GROUP, group, (zero, zero))

    for k, (dt, ds) in enumerate(SIDES):
        here = exists(-dt, -ds)

        @pl.when(here)
        def _():
            ring_copy(k, dt, ds).wait_recv()

        @pl.when(jnp.logical_not(here))
        def _():
            at_row, at_col = span(dt, (272, 288), (16, 272), (0, 16)), span(ds, (384, 512), (128, 384), (0, 128))
            for part in range(2):
                cells_ref[part, slice(*at_row), slice(*at_col)] = jnp.zeros((at_row[1] - at_row[0], at_col[1] - at_col[0]), bf16)

    for part in range(2):
        for at, first_row, take in ((0, 0, 14), (NW + 2, EDGE + NW, 0)):
            strip = cells_ref[part, first_row : first_row + EDGE, HALF : HALF + NW].astype(f32)
            for dx in range(3):
                shifted = moved(strip, dx)
                for v in range(2):
                    for i in range(2):
                        taps[v, (at + i) * 8 + 3 * part + dx : (at + i) * 8 + 3 * part + dx + 1, :] = shifted[take + i : take + i + 1, v * 128 : (v + 1) * 128]
    border = (0, 1, NW, NW + 1)
    mixed_all = mixed_rows([8 * index for index in border])
    for j, index in enumerate(border):
        here = {0: t > 0, NW + 1: t < tiles - 1}.get(index, t >= 0)
        for v in range(2):
            mixed = jnp.where(jnp.logical_and(inner[v], here), mixed_all[:, (2 * j + v) * 128 : (2 * j + v + 1) * 128], 0.0)
            for dy in range(3):
                row = index + 2 - dy
                if 2 <= row < NW + 2:
                    mixed_sum[v, row * 8 : row * 8 + 8, :] += mixed[8 * dy : 8 * dy + 8]

    WIDE = 384
    strip_lane = lax.broadcasted_iota(jnp.int32, (NW + 2 * EDGE, 128), 1)
    row_lane = lax.broadcasted_iota(jnp.int32, (8, WIDE), 1)
    constant = jnp.where(lax.broadcasted_iota(jnp.int32, (8, WIDE), 0) < 2, 1.0, 0.0)
    edge_sum = None
    for side in range(2):
        planes = [cells_ref[part, :, side * NW : (side + 1) * NW].astype(f32) for part in range(2)]
        strips = [pltpu.roll(planes[part], NW - 126 + 4 * part, 1)[:, :128] for part in range(2)]
        strip = jnp.where(strip_lane < 4, strips[0], strips[1])
        strip = jnp.concatenate([strip, jnp.zeros((WIDE - NW - 2 * EDGE, 128), f32)], 0).T[:8]
        window = jnp.concatenate([pltpu.roll(strip, 1, 1), strip, pltpu.roll(strip, WIDE - 1, 1), constant], 0).astype(bf16)
        hidden = hidden_of(first_edge[...], window)
        outer = lax.broadcasted_iota(jnp.int32, (NW, WIDE), 0) < 128 if side == 0 else lax.broadcasted_iota(jnp.int32, (NW, WIDE), 0) >= 128
        gone = s == 0 if side == 0 else s == peers - 1
        hidden = jnp.where(jnp.logical_and(outer, gone), 0.0, hidden).astype(bf16)
        mixed = jnp.dot(second_edge[side], hidden, preferred_element_type=f32)
        edge_sum = mixed if edge_sum is None else edge_sum + mixed
    by_dy = []
    for dy in range(3):
        piece = edge_sum[8 * dy : 8 * dy + 8]
        piece = jnp.where(jnp.logical_and(row_lane == EDGE - 1, t == 0), 0.0, piece)
        piece = jnp.where(jnp.logical_and(row_lane == EDGE + NW, t == tiles - 1), 0.0, piece)
        by_dy.append(piece if dy == 1 else pltpu.roll(piece, 1 if dy == 0 else WIDE - 1, 1))
    columns = by_dy[0] + by_dy[1] + by_dy[2]
    columns = jnp.concatenate([columns, jnp.zeros((120, WIDE), f32)], 0).T[EDGE : EDGE + NW]
    out_lane = lax.broadcasted_iota(jnp.int32, (NW, 128), 1)
    for part in range(2):
        halves = [jnp.zeros((NW, 128), f32), jnp.zeros((NW, 128), f32)]
        for dx in range(3):
            sums = jnp.concatenate([mixed_sum[v, pl.ds(16 + 3 * part + dx, NW, stride=8), :] for v in range(2)], 1)
            sums = sums if dx == 1 else pltpu.roll(sums, 1 if dx == 0 else NW - 1, 1)
            halves = [halves[v] + sums[:, v * 128 : (v + 1) * 128] for v in range(2)]
        left = pltpu.roll(columns, (128 - 2 * part) % 128, 1) if part else columns
        right = pltpu.roll(columns, 126 - 4 - 2 * part, 1)
        halves[0] = halves[0] + jnp.where(out_lane < 2, left, 0.0)
        halves[1] = halves[1] + jnp.where(out_lane >= 126, right, 0.0)
        for v in range(2):
            at = slice(v * 128, (v + 1) * 128)
            out_ref[part, :, at] = out_ref[part, :, at] - (halves[v] + b2_ref[part])
    for k, (dt, ds) in enumerate(SIDES):
        @pl.when(exists(dt, ds))
        def _():
            ring_copy(k, dt, ds).wait_send()
            rim_copy(k, dt, ds).wait_send()
    for k, dt, ds in straight:
        @pl.when(exists(dt, ds))
        def _():
            halo_copy(k, dt, ds).wait_send()
    for k, dt, ds in diagonal:
        @pl.when(jnp.logical_and(exists(dt, 0), exists(0, -ds)))
        def _():
            relay_copy(k, dt, ds).wait_send()
    for k, (dy, dz) in enumerate(order):
        amp_copy(k + 1, dy, dz).wait_send()


def sample(specimen, noise, probe, amps, rows, cols, counts, w1, b1, w2, b2):
    tiles, peers = lax.axis_size("tile"), lax.axis_size("scan")
    if peers == 16:
        order, issue, rows_y = ORDER_16, ISSUE_16, 4
    else:
        order, issue, rows_y = [(0, b) for b in range(1, peers)], list(range(peers - 1)), 1
    forward, inverse = dft_matrices()
    one, two = tap_selectors()
    f32, bf16 = jnp.float32, jnp.bfloat16
    smem = pl.BlockSpec(memory_space=pltpu.SMEM)
    vmem = pl.BlockSpec(memory_space=pltpu.VMEM)
    dma = pltpu.SemaphoreType.DMA
    return pl.pallas_call(
        functools.partial(patch_kernel, order, issue, rows_y, tiles, peers),
        out_shape=pltpu.VMEM((2, NW, NW), f32),
        in_specs=[smem, smem, smem, pl.BlockSpec(memory_space=pl.ANY)] + [pl.BlockSpec(memory_space=pl.ANY)] * 5 + [vmem, vmem, vmem, smem, vmem, vmem],
        out_specs=vmem,
        scratch_shapes=[
            pltpu.VMEM((2, NW, NW), f32),
            pltpu.VMEM((2, NW, NW), f32),
            pltpu.VMEM((2, NW, NW), f32),
            pltpu.VMEM((2 * NW, 2 * NW), bf16),
            pltpu.VMEM((2 * NW, 2 * NW), bf16),
            dma((5,)),
            pltpu.VMEM((2, NW + 2 * EDGE, 2 * NW), bf16),
            pltpu.VMEM((2, 8 * (PRIOR_ROWS + 2), 128), f32),
            pltpu.VMEM((2, 8 * PRIOR_ROWS, 128), f32),
            pltpu.VMEM((128, 32), bf16),
            pltpu.VMEM((NW, 32), bf16),
            pltpu.VMEM((24, 128), bf16),
            pltpu.VMEM((2, 24, NW), bf16),
            pltpu.VMEM((peers, CAP, NW, NW), bf16),
            pltpu.VMEM((2, 2 * NW, 2 * NW), bf16),
            pltpu.VMEM((2, 2 * NW, 2 * NW), f32),
            pltpu.VMEM((2, 2 * NW, 2 * NW), bf16),
            pltpu.VMEM((2, 2 * NW, 2 * NW), bf16),
            pltpu.VMEM((2, 2, 2 * NW, HALF), f32),
            pltpu.VMEM((peers, CAP, 2, NW, NW), f32),
            pltpu.VMEM((2 * NW, 2 * NW), bf16),
            pltpu.VMEM((2 * NW, 2 * NW), bf16),
            pltpu.VMEM((peers, 2 * NW, 2 * NW), f32),
            pltpu.VMEM((2 * NW, 2 * NW), f32),
            dma((peers,)), dma((peers,)), dma, dma((8,)), dma((8,)), dma((8,)), dma((8,)), dma((8,)), dma((8,)),
        ],
        compiler_params=pltpu.CompilerParams(collective_id=0, has_side_effects=True, vmem_limit_bytes=60 << 20),
        name="step",
    )(rows, cols, counts, amps, specimen, noise, probe, jnp.asarray(forward), jnp.asarray(inverse),
      w1, b1, w2, b2, jnp.asarray(one), jnp.asarray(two))


def tap_selectors():
    first = np.zeros((3, 18, 32), np.float32)
    second = np.zeros((5, 24, 18), np.float32)
    for c in range(2):
        for dy in range(3):
            for dx in range(3):
                tap = 9 * c + 3 * dy + dx
                first[0, tap, 8 * dy + 3 * c + dx] = 0.5
                first[1, tap, 8 * dy + 4 * c + dx] = 0.5
                first[2, tap, 8 * dy + 4 * c + dx + 1] = 0.5
                second[0, 8 * dy + 3 * c + dx, tap] = 1.0
            for side, half, dx, at in ((0, 0, 0, 0), (0, 1, 1, 0), (0, 1, 0, 1), (1, 0, 2, 0), (1, 0, 1, 1), (1, 1, 2, 1)):
                second[1 + 2 * side + half, 8 * dy + 4 * side + 2 * c + at, 9 * c + 3 * dy + dx] = 1.0
    return first.astype(jnp.bfloat16), second.astype(jnp.bfloat16)


def shards(
    specimen, sampler_noise, probe_field, amplitudes, corner_rows, corner_cols, slot_counts,
    first_weight, first_bias, second_weight, second_bias,
):
    return sample(
        specimen, sampler_noise, probe_field, amplitudes[0, 0],
        corner_rows[0, 0].T, corner_cols[0, 0].T, slot_counts[0, 0],
        first_weight.T, first_bias.reshape(1, -1), second_weight, second_bias,
    )


def solution(mesh):
    return jax.shard_map(
        shards,
        mesh=mesh,
        in_specs=(
            P(None, "tile", "scan"),
            P(None, "tile", "scan"),
            P(),
            P("tile", "scan", None, None, None, None),
            P("tile", "scan", None, None),
            P("tile", "scan", None, None),
            P("tile", "scan", None),
            P(),
            P(),
            P(),
            P(),
        ),
        out_specs=P(None, "tile", "scan"),
        check_vma=False,
    )
```

```python
import functools

import jax
import jax.numpy as jnp
import numpy as np
from jax import lax
from jax.experimental import pallas as pl
from jax.experimental.pallas import tpu as pltpu
from jax.sharding import PartitionSpec as P

MESH = pl.DeviceIdType.MESH
NW = 256
HALF = 128
EDGE = 16
GROUP = 44
PRIOR_ROWS = 264
CAP = 2

ORDER_16 = [(3, 1), (1, 3), (2, 3), (1, 1), (3, 0), (2, 0), (3, 3), (1, 2), (0, 1), (0, 3), (2, 1), (3, 2), (1, 0), (0, 2), (2, 2)]
ISSUE_16 = [0, 2, 1, 4, 6, 8, 3, 13, 5, 11, 7, 9, 10, 14, 12]
SIDES = [(a, b) for a in (-1, 0, 1) for b in (-1, 0, 1) if (a, b) != (0, 0)]


def dft_matrices():
    index = np.arange(NW)
    angle = (index[:, None] * index[None, :] % NW) * (2.0 * np.pi / NW)
    cosine = (np.cos(angle) / 16.0).astype(jnp.bfloat16)
    sine = (np.sin(angle) / 16.0).astype(jnp.bfloat16)
    forward = np.concatenate([np.concatenate([cosine, sine], 1), np.concatenate([-sine, cosine], 1)], 0)
    return forward, np.ascontiguousarray(forward.T)


def span(step, low, mid, high):
    return {-1: low, 0: mid, 1: high}[step]


def patch_kernel(
    order, issue, rows_y, tiles, peers,
    rows_ref, cols_ref, counts_ref, amps_ref, spec_hbm, noise_hbm, probe_hbm, fwd_hbm, inv_hbm,
    w1_ref, b1_ref, w2_ref, b2_ref, sel1_ref, sel2_ref,
    out_ref,
    spec_ref, noise_ref, probe_ref, fwd_ref, inv_ref, load_sem,
    cells_ref, taps, mixed_sum, first_ref, first_edge, second_ref, second_edge,
    recv, frame, acc, rim, rim_in, probe2, rolled, wave_in, mid_ref, far_ref, wave_ref,
    amp_send, amp_recv, own_sem, halo_send, halo_recv, rim_send, rim_recv, ring_send, ring_recv,
):
    f32, bf16 = jnp.float32, jnp.bfloat16
    t = lax.axis_index("tile")
    s = lax.axis_index("scan")
    rows_z = peers // rows_y
    y, z = s // rows_z, lax.rem(s, rows_z)

    mirror = 1 - 2 * lax.rem(t, 2)

    def peer(dy, dz):
        return lax.rem(y + mirror * dy + rows_y, rows_y) * rows_z + lax.rem(z + mirror * dz + rows_z, rows_z)

    def exists(dt, ds):
        ok_t = {-1: t > 0, 0: t >= 0, 1: t < tiles - 1}[dt]
        ok_s = {-1: s > 0, 0: s >= 0, 1: s < peers - 1}[ds]
        return jnp.logical_and(ok_t, ok_s)

    barrier = pltpu.get_barrier_semaphore()
    expected = jnp.int32(len(order))
    for dy, dz in order:
        pl.semaphore_signal(barrier, inc=1, device_id=(t, peer(-dy, -dz)), device_id_type=MESH)
    for dt, ds in SIDES:
        if dt != 0:
            here = exists(dt, ds)
            expected = expected + here.astype(jnp.int32)

            @pl.when(here)
            def _():
                pl.semaphore_signal(barrier, inc=1, device_id=(t + dt, s + ds), device_id_type=MESH)

    loads = [
        pltpu.make_async_copy(source, place, load_sem.at[i])
        for i, (source, place) in enumerate(
            ((spec_hbm, spec_ref), (noise_hbm, noise_ref), (probe_hbm, probe_ref), (fwd_hbm, fwd_ref), (inv_hbm, inv_ref))
        )
    ]
    for load in loads:
        load.start()
    own = pltpu.make_async_copy(amps_ref.at[s], recv.at[0], own_sem)
    own.start()
    loads[0].wait()
    for part in range(2):
        frame[part, HALF : HALF + NW, HALF : HALF + NW] = spec_ref[part].astype(bf16)
    pl.semaphore_wait(barrier, expected)

    def halo_copy(k, dt, ds):
        src = (slice(None), slice(*span(dt, (128, 256), (128, 384), (256, 384))), slice(*span(ds, (128, 256), (128, 384), (256, 384))))
        dst = (slice(None), slice(*span(dt, (384, 512), (128, 384), (0, 128))), slice(*span(ds, (384, 512), (128, 384), (0, 128))))
        return pltpu.make_async_remote_copy(
            src_ref=frame.at[src], dst_ref=frame.at[dst], send_sem=halo_send.at[k], recv_sem=halo_recv.at[k],
            device_id=(t + dt, s + ds), device_id_type=MESH,
        )

    def relay_copy(k, dt, ds):
        columns = span(ds, slice(384, 512), None, slice(0, 128))
        return pltpu.make_async_remote_copy(
            src_ref=frame.at[:, span(dt, slice(128, 256), None, slice(256, 384)), columns],
            dst_ref=frame.at[:, span(dt, slice(384, 512), None, slice(0, 128)), columns],
            send_sem=halo_send.at[k], recv_sem=halo_recv.at[k], device_id=(t + dt, s), device_id_type=MESH,
        )

    def amp_copy(k, dy, dz):
        d = peer(dy, dz)
        return pltpu.make_async_remote_copy(
            src_ref=amps_ref.at[d], dst_ref=recv.at[k], send_sem=amp_send.at[k], recv_sem=amp_recv.at[k],
            device_id=(t, d), device_id_type=MESH,
        )

    straight = [(k, dt, ds) for k, (dt, ds) in enumerate(SIDES) if dt * ds == 0]
    diagonal = [(k, dt, ds) for k, (dt, ds) in enumerate(SIDES) if dt * ds != 0]
    for k, dt, ds in straight:
        @pl.when(exists(dt, ds))
        def _():
            halo_copy(k, dt, ds).start()

    for load in loads[1:]:
        load.wait()
    for part in range(2):
        acc[part] = jnp.zeros((2 * NW, 2 * NW), f32)
        acc[part, HALF : HALF + NW, HALF : HALF + NW] = spec_ref[part] + 0.5 * noise_ref[part]
        for half in range(2):
            columns = probe_ref[part, :, half * HALF : (half + 1) * HALF]
            probe2[part, half, :NW, :] = columns
            probe2[part, half, NW:, :] = columns

    def take_halo(k, dt, ds, copy):
        here = exists(-dt, -ds)

        @pl.when(here)
        def _():
            copy(k, dt, ds).wait_recv()

        @pl.when(jnp.logical_not(here))
        def _():
            at_row, at_col = span(dt, (384, 512), (128, 384), (0, 128)), span(ds, (384, 512), (128, 384), (0, 128))
            for part in range(2):
                frame[part, slice(*at_row), slice(*at_col)] = jnp.zeros((at_row[1] - at_row[0], at_col[1] - at_col[0]), bf16)

    for k, dt, ds in straight:
        take_halo(k, dt, ds, halo_copy)
    for k, dt, ds in diagonal:
        @pl.when(jnp.logical_and(exists(dt, 0), exists(0, -ds)))
        def _():
            relay_copy(k, dt, ds).start()
    for k in issue:
        amp_copy(k + 1, *order[k]).start()
    for k, dt, ds in diagonal:
        take_halo(k, dt, ds, relay_copy)

    square = lax.broadcasted_iota(jnp.int32, (128, 128), 0) == lax.broadcasted_iota(jnp.int32, (128, 128), 1)
    bias = jnp.sum(jnp.where(square, b1_ref[...], 0.0), axis=1, keepdims=True) * 0.5
    high = bias.astype(bf16).astype(f32)
    for v in range(3):
        column = lax.broadcasted_iota(jnp.int32, (128, 32), 1)
        at = 24 if v else 6
        weights = lax.dot_general(w1_ref[...], sel1_ref[v], (((0,), (0,)), ((), ())), preferred_element_type=f32)
        weights = (weights + jnp.where(column == at, high, 0.0) + jnp.where(column == at + 1, bias - high, 0.0)).astype(bf16)
        if v == 0:
            first_ref[...] = weights
        else:
            first_edge[(v - 1) * 128 : v * 128, :] = weights
    second_ref[...] = jnp.dot(sel2_ref[0], w2_ref[...], preferred_element_type=f32).astype(bf16)
    for side in range(2):
        for v in range(2):
            second_edge[side, :, v * 128 : (v + 1) * 128] = jnp.dot(
                sel2_ref[1 + 2 * side + v], w2_ref[...], preferred_element_type=f32
            ).astype(bf16)

    CH = 32
    lane = lax.broadcasted_iota(jnp.int32, (CH, NW), 1)
    sub = lax.broadcasted_iota(jnp.int32, (CH, NW), 0)

    def steps_of(k):
        dy, dz = jnp.int32(0), jnp.int32(0)
        for i, (a, b) in enumerate(order):
            dy = jnp.where(k == i + 1, a, dy)
            dz = jnp.where(k == i + 1, b, dz)
        return dy, dz

    def corners(k):
        dy, dz = steps_of(k)
        h = peer(-dy, -dz)
        return h, [(rows_ref[c, h], cols_ref[c, h]) for c in range(CAP)]

    def both(left_ref, right_ref, result):
        for c in range(CAP):
            mid = jnp.dot(left_ref[...], wave_in[:, c * NW : (c + 1) * NW], preferred_element_type=f32)
            for p in range(2):
                mid_ref[c * NW : (c + 1) * NW, p * NW : (p + 1) * NW] = mid[p * NW : (p + 1) * NW].astype(bf16)
        for p in range(2):
            result[:, p * NW : (p + 1) * NW] = jnp.dot(mid_ref[...], right_ref[:, p * NW : (p + 1) * NW], preferred_element_type=f32)


    def outward(k, carry):
        h, corner = corners(k)

        def exits(i, carry):
            base = pl.multiple_of(i * CH, CH)
            for c in range(CAP):
                r, q = corner[c]
                low_row = sub + base < r
                low_col = lane < q
                shift = lax.rem(q, NW)
                cell, prb = [], []
                for part in range(2):
                    tile = [[frame[part, pl.ds(base + a * NW, CH), b * NW : (b + 1) * NW].astype(f32) for b in range(2)] for a in range(2)]
                    cell.append(jnp.where(low_row, jnp.where(low_col, tile[1][1], tile[1][0]), jnp.where(low_col, tile[0][1], tile[0][0])))
                    turned = pltpu.roll(jnp.concatenate([probe2[part, half, pl.ds(base + NW - r, CH), :] for half in range(2)], 1), shift, 1)
                    rolled[k, c, part, pl.ds(base, CH), :] = turned
                    prb.append(turned)
                wave_in[pl.ds(base, CH), c * NW : (c + 1) * NW] = (prb[0] * cell[0] - prb[1] * cell[1]).astype(bf16)
                wave_in[pl.ds(base + NW, CH), c * NW : (c + 1) * NW] = (prb[0] * cell[1] + prb[1] * cell[0]).astype(bf16)
            return carry

        lax.fori_loop(0, NW // CH, exits, 0, unroll=True)
        both(fwd_ref, inv_ref, far_ref.at[k])
        return carry

    lax.fori_loop(0, len(order) + 1, outward, 0, unroll=2)
    own.wait()

    def inward(k, carry):
        h, corner = corners(k)
        dy, dz = steps_of(k)
        scale = [jnp.where(counts_ref[h] > c, f32(-0.25), f32(0.0)) for c in range(CAP)]

        @pl.when(k > 0)
        def _():
            pltpu.make_async_remote_copy(
                src_ref=recv.at[k], dst_ref=recv.at[k], send_sem=amp_send.at[k], recv_sem=amp_recv.at[k],
                device_id=(t, peer(dy, dz)), device_id_type=MESH,
            ).wait_recv()

        def correct(i, carry):
            base = pl.multiple_of(i * CH, CH)
            for c in range(CAP):
                fr = far_ref[k, pl.ds(base + c * NW, CH), :NW]
                fi = far_ref[k, pl.ds(base + c * NW, CH), NW:]
                amp = recv[k, c, pl.ds(base, CH), :].astype(f32)
                keep = 1.0 - amp * lax.rsqrt(jnp.maximum(fr * fr + fi * fi, 1.0))
                wave_in[pl.ds(base, CH), c * NW : (c + 1) * NW] = (fr * keep).astype(bf16)
                wave_in[pl.ds(base + NW, CH), c * NW : (c + 1) * NW] = (fi * keep).astype(bf16)
            return carry

        lax.fori_loop(0, NW // CH, correct, 0, unroll=True)
        both(inv_ref, fwd_ref, wave_ref)

        def gather(i, carry):
            base = pl.multiple_of(i * CH, CH)
            grads = []
            for c in range(CAP):
                wr = wave_ref[pl.ds(base + c * NW, CH), :NW]
                wi = wave_ref[pl.ds(base + c * NW, CH), NW:]
                pr = rolled[k, c, 0, pl.ds(base, CH), :] * scale[c]
                pi = rolled[k, c, 1, pl.ds(base, CH), :] * scale[c]
                grads.append((pr * wr + pi * wi, pr * wi - pi * wr))
            for a in range(2):
                for b in range(2):
                    masks = []
                    for c in range(CAP):
                        r, q = corner[c]
                        row_ok = sub + base < r if a else sub + base >= r
                        col_ok = lane < q if b else lane >= q
                        masks.append(jnp.logical_and(row_ok, col_ok))
                    for part in range(2):
                        total = acc[part, pl.ds(base + a * NW, CH), b * NW : (b + 1) * NW]
                        for c in range(CAP):
                            total = total + jnp.where(masks[c], grads[c][part], 0.0)
                        acc[part, pl.ds(base + a * NW, CH), b * NW : (b + 1) * NW] = total
            return carry

        lax.fori_loop(0, NW // CH, gather, 0, unroll=True)
        return carry

    lax.fori_loop(0, len(order) + 1, inward, 0, unroll=2)

    for part in range(2):
        for lo, hi in ((0, HALF), (HALF + NW, 2 * NW)):
            rim[part, lo:hi, :] = acc[part, lo:hi, :].astype(bf16)
            rim[part, HALF : HALF + NW, lo:hi] = acc[part, HALF : HALF + NW, lo:hi].astype(bf16)

    def rim_copy(k, dt, ds):
        where = (slice(None), slice(*span(dt, (0, 128), (128, 384), (384, 512))), slice(*span(ds, (0, 128), (128, 384), (384, 512))))
        return pltpu.make_async_remote_copy(
            src_ref=rim.at[where], dst_ref=rim_in.at[where], send_sem=rim_send.at[k], recv_sem=rim_recv.at[k],
            device_id=(t + dt, s + ds), device_id_type=MESH,
        )

    for k, (dt, ds) in enumerate(SIDES):
        @pl.when(exists(dt, ds))
        def _():
            rim_copy(k, dt, ds).start()
    for part in range(2):
        out_ref[part] = acc[part, HALF : HALF + NW, HALF : HALF + NW]
    for k, (dt, ds) in enumerate(SIDES):
        @pl.when(exists(-dt, -ds))
        def _():
            rim_copy(k, dt, ds).wait_recv()
            src_r, dst_r = span(dt, ((0, 128), (128, 256)), ((128, 384), (0, 256)), ((384, 512), (0, 128)))
            src_c, dst_c = span(ds, ((0, 128), (128, 256)), ((128, 384), (0, 256)), ((384, 512), (0, 128)))
            for part in range(2):
                out_ref[part, slice(*dst_r), slice(*dst_c)] += rim_in[part, slice(*src_r), slice(*src_c)].astype(f32)
    for part in range(2):
        cells_ref[part, EDGE : EDGE + NW, HALF : HALF + NW] = out_ref[part].astype(bf16)

    def ring_copy(k, dt, ds):
        src = (slice(None), slice(*span(dt, (16, 32), (16, 272), (256, 272))), slice(*span(ds, (128, 256), (128, 384), (256, 384))))
        dst = (slice(None), slice(*span(dt, (272, 288), (16, 272), (0, 16))), slice(*span(ds, (384, 512), (128, 384), (0, 128))))
        return pltpu.make_async_remote_copy(
            src_ref=cells_ref.at[src], dst_ref=cells_ref.at[dst], send_sem=ring_send.at[k], recv_sem=ring_recv.at[k],
            device_id=(t + dt, s + ds), device_id_type=MESH,
        )

    for k, (dt, ds) in enumerate(SIDES):
        @pl.when(exists(dt, ds))
        def _():
            ring_copy(k, dt, ds).start()
    def moved(rows256, dx):
        return rows256 if dx == 1 else pltpu.roll(rows256, 1 if dx == 0 else NW - 1, 1)

    for part in range(2):
        for dx in range(3):
            shifted = moved(out_ref[part], dx)
            for v in range(2):
                taps[v, pl.ds(16 + 3 * part + dx, NW, stride=8), :] = shifted[:, v * 128 : (v + 1) * 128]
    for v in range(2):
        for k in (6, 7):
            taps[v, pl.ds(k, NW + 4, stride=8), :] = jnp.ones((NW + 4, 128), f32)

    mlane = lax.broadcasted_iota(jnp.int32, (24, 128), 1)
    inner = (mlane > 0, mlane < 127)

    def hidden_of(weights, window):
        pre = jnp.dot(weights, window, preferred_element_type=f32)
        return pre + pre * jnp.tanh(pre)

    def mixed_rows(starts):
        window = jnp.concatenate([taps[v, pl.ds(start, 24), :].astype(bf16) for start in starts for v in range(2)], 1)
        return jnp.dot(second_ref[...], hidden_of(first_ref[:, :24], window).astype(bf16), preferred_element_type=f32)

    def group(g, carry):
        older, old = carry
        mixed_all = mixed_rows([pl.multiple_of((g * GROUP + j) * 8, 8) for j in range(GROUP)])
        for j in range(GROUP):
            index = g * GROUP + j
            here = jnp.logical_and(index > 1, index < NW)
            mixed = [jnp.where(jnp.logical_and(inner[v], here), mixed_all[:, (2 * j + v) * 128 : (2 * j + v + 1) * 128], 0.0) for v in range(2)]
            for v in range(2):
                mixed_sum[v, pl.ds(pl.multiple_of(index * 8, 8), 8), :] = older[v] + mixed[v][16:24]
            older = [old[v] + mixed[v][8:16] for v in range(2)]
            old = [mixed[v][0:8] for v in range(2)]
        return older, old

    zero = [jnp.zeros((8, 128), f32)] * 2
    lax.fori_loop(0, PRIOR_ROWS // GROUP, group, (zero, zero))

    for k, (dt, ds) in enumerate(SIDES):
        here = exists(-dt, -ds)

        @pl.when(here)
        def _():
            ring_copy(k, dt, ds).wait_recv()

        @pl.when(jnp.logical_not(here))
        def _():
            at_row, at_col = span(dt, (272, 288), (16, 272), (0, 16)), span(ds, (384, 512), (128, 384), (0, 128))
            for part in range(2):
                cells_ref[part, slice(*at_row), slice(*at_col)] = jnp.zeros((at_row[1] - at_row[0], at_col[1] - at_col[0]), bf16)

    for part in range(2):
        for at, first_row, take in ((0, 0, 14), (NW + 2, EDGE + NW, 0)):
            strip = cells_ref[part, first_row : first_row + EDGE, HALF : HALF + NW].astype(f32)
            for dx in range(3):
                shifted = moved(strip, dx)
                for v in range(2):
                    for i in range(2):
                        taps[v, (at + i) * 8 + 3 * part + dx : (at + i) * 8 + 3 * part + dx + 1, :] = shifted[take + i : take + i + 1, v * 128 : (v + 1) * 128]
    border = (0, 1, NW, NW + 1)
    mixed_all = mixed_rows([8 * index for index in border])
    for j, index in enumerate(border):
        here = {0: t > 0, NW + 1: t < tiles - 1}.get(index, t >= 0)
        for v in range(2):
            mixed = jnp.where(jnp.logical_and(inner[v], here), mixed_all[:, (2 * j + v) * 128 : (2 * j + v + 1) * 128], 0.0)
            for dy in range(3):
                row = index + 2 - dy
                if 2 <= row < NW + 2:
                    mixed_sum[v, row * 8 : row * 8 + 8, :] += mixed[8 * dy : 8 * dy + 8]

    WIDE = 384
    strip_lane = lax.broadcasted_iota(jnp.int32, (NW + 2 * EDGE, 128), 1)
    row_lane = lax.broadcasted_iota(jnp.int32, (8, WIDE), 1)
    constant = jnp.where(lax.broadcasted_iota(jnp.int32, (8, WIDE), 0) < 2, 1.0, 0.0)
    edge_sum = None
    for side in range(2):
        planes = [cells_ref[part, :, side * NW : (side + 1) * NW].astype(f32) for part in range(2)]
        strips = [pltpu.roll(planes[part], NW - 126 + 4 * part, 1)[:, :128] for part in range(2)]
        strip = jnp.where(strip_lane < 4, strips[0], strips[1])
        strip = jnp.concatenate([strip, jnp.zeros((WIDE - NW - 2 * EDGE, 128), f32)], 0).T[:8]
        window = jnp.concatenate([pltpu.roll(strip, 1, 1), strip, pltpu.roll(strip, WIDE - 1, 1), constant], 0).astype(bf16)
        hidden = hidden_of(first_edge[...], window)
        outer = lax.broadcasted_iota(jnp.int32, (NW, WIDE), 0) < 128 if side == 0 else lax.broadcasted_iota(jnp.int32, (NW, WIDE), 0) >= 128
        gone = s == 0 if side == 0 else s == peers - 1
        hidden = jnp.where(jnp.logical_and(outer, gone), 0.0, hidden).astype(bf16)
        mixed = jnp.dot(second_edge[side], hidden, preferred_element_type=f32)
        edge_sum = mixed if edge_sum is None else edge_sum + mixed
    by_dy = []
    for dy in range(3):
        piece = edge_sum[8 * dy : 8 * dy + 8]
        piece = jnp.where(jnp.logical_and(row_lane == EDGE - 1, t == 0), 0.0, piece)
        piece = jnp.where(jnp.logical_and(row_lane == EDGE + NW, t == tiles - 1), 0.0, piece)
        by_dy.append(piece if dy == 1 else pltpu.roll(piece, 1 if dy == 0 else WIDE - 1, 1))
    columns = by_dy[0] + by_dy[1] + by_dy[2]
    columns = jnp.concatenate([columns, jnp.zeros((120, WIDE), f32)], 0).T[EDGE : EDGE + NW]
    out_lane = lax.broadcasted_iota(jnp.int32, (NW, 128), 1)
    for part in range(2):
        halves = [jnp.zeros((NW, 128), f32), jnp.zeros((NW, 128), f32)]
        for dx in range(3):
            sums = jnp.concatenate([mixed_sum[v, pl.ds(16 + 3 * part + dx, NW, stride=8), :] for v in range(2)], 1)
            sums = sums if dx == 1 else pltpu.roll(sums, 1 if dx == 0 else NW - 1, 1)
            halves = [halves[v] + sums[:, v * 128 : (v + 1) * 128] for v in range(2)]
        left = pltpu.roll(columns, (128 - 2 * part) % 128, 1) if part else columns
        right = pltpu.roll(columns, 126 - 4 - 2 * part, 1)
        halves[0] = halves[0] + jnp.where(out_lane < 2, left, 0.0)
        halves[1] = halves[1] + jnp.where(out_lane >= 126, right, 0.0)
        for v in range(2):
            at = slice(v * 128, (v + 1) * 128)
            out_ref[part, :, at] = out_ref[part, :, at] - (halves[v] + b2_ref[part])
    for k, (dt, ds) in enumerate(SIDES):
        @pl.when(exists(dt, ds))
        def _():
            ring_copy(k, dt, ds).wait_send()
            rim_copy(k, dt, ds).wait_send()
    for k, dt, ds in straight:
        @pl.when(exists(dt, ds))
        def _():
            halo_copy(k, dt, ds).wait_send()
    for k, dt, ds in diagonal:
        @pl.when(jnp.logical_and(exists(dt, 0), exists(0, -ds)))
        def _():
            relay_copy(k, dt, ds).wait_send()
    for k, (dy, dz) in enumerate(order):
        amp_copy(k + 1, dy, dz).wait_send()


def sample(specimen, noise, probe, amps, rows, cols, counts, w1, b1, w2, b2):
    tiles, peers = lax.axis_size("tile"), lax.axis_size("scan")
    if peers == 16:
        order, issue, rows_y = ORDER_16, ISSUE_16, 4
    else:
        order, issue, rows_y = [(0, b) for b in range(1, peers)], list(range(peers - 1)), 1
    forward, inverse = dft_matrices()
    one, two = tap_selectors()
    f32, bf16 = jnp.float32, jnp.bfloat16
    smem = pl.BlockSpec(memory_space=pltpu.SMEM)
    vmem = pl.BlockSpec(memory_space=pltpu.VMEM)
    dma = pltpu.SemaphoreType.DMA
    return pl.pallas_call(
        functools.partial(patch_kernel, order, issue, rows_y, tiles, peers),
        out_shape=pltpu.VMEM((2, NW, NW), f32),
        in_specs=[smem, smem, smem, pl.BlockSpec(memory_space=pl.ANY)] + [pl.BlockSpec(memory_space=pl.ANY)] * 5 + [vmem, vmem, vmem, smem, vmem, vmem],
        out_specs=vmem,
        scratch_shapes=[
            pltpu.VMEM((2, NW, NW), f32),
            pltpu.VMEM((2, NW, NW), f32),
            pltpu.VMEM((2, NW, NW), f32),
            pltpu.VMEM((2 * NW, 2 * NW), bf16),
            pltpu.VMEM((2 * NW, 2 * NW), bf16),
            dma((5,)),
            pltpu.VMEM((2, NW + 2 * EDGE, 2 * NW), bf16),
            pltpu.VMEM((2, 8 * (PRIOR_ROWS + 2), 128), f32),
            pltpu.VMEM((2, 8 * PRIOR_ROWS, 128), f32),
            pltpu.VMEM((128, 32), bf16),
            pltpu.VMEM((NW, 32), bf16),
            pltpu.VMEM((24, 128), bf16),
            pltpu.VMEM((2, 24, NW), bf16),
            pltpu.VMEM((peers, CAP, NW, NW), bf16),
            pltpu.VMEM((2, 2 * NW, 2 * NW), bf16),
            pltpu.VMEM((2, 2 * NW, 2 * NW), f32),
            pltpu.VMEM((2, 2 * NW, 2 * NW), bf16),
            pltpu.VMEM((2, 2 * NW, 2 * NW), bf16),
            pltpu.VMEM((2, 2, 2 * NW, HALF), f32),
            pltpu.VMEM((peers, CAP, 2, NW, NW), f32),
            pltpu.VMEM((2 * NW, 2 * NW), bf16),
            pltpu.VMEM((2 * NW, 2 * NW), bf16),
            pltpu.VMEM((peers, 2 * NW, 2 * NW), f32),
            pltpu.VMEM((2 * NW, 2 * NW), f32),
            dma((peers,)), dma((peers,)), dma, dma((8,)), dma((8,)), dma((8,)), dma((8,)), dma((8,)), dma((8,)),
        ],
        compiler_params=pltpu.CompilerParams(collective_id=0, has_side_effects=True, vmem_limit_bytes=62 << 20),
        name="step",
    )(rows, cols, counts, amps, specimen, noise, probe, jnp.asarray(forward), jnp.asarray(inverse),
      w1, b1, w2, b2, jnp.asarray(one), jnp.asarray(two))


def tap_selectors():
    first = np.zeros((3, 18, 32), np.float32)
    second = np.zeros((5, 24, 18), np.float32)
    for c in range(2):
        for dy in range(3):
            for dx in range(3):
                tap = 9 * c + 3 * dy + dx
                first[0, tap, 8 * dy + 3 * c + dx] = 0.5
                first[1, tap, 8 * dy + 4 * c + dx] = 0.5
                first[2, tap, 8 * dy + 4 * c + dx + 1] = 0.5
                second[0, 8 * dy + 3 * c + dx, tap] = 1.0
            for side, half, dx, at in ((0, 0, 0, 0), (0, 1, 1, 0), (0, 1, 0, 1), (1, 0, 2, 0), (1, 0, 1, 1), (1, 1, 2, 1)):
                second[1 + 2 * side + half, 8 * dy + 4 * side + 2 * c + at, 9 * c + 3 * dy + dx] = 1.0
    return first.astype(jnp.bfloat16), second.astype(jnp.bfloat16)


def shards(
    specimen, sampler_noise, probe_field, amplitudes, corner_rows, corner_cols, slot_counts,
    first_weight, first_bias, second_weight, second_bias,
):
    return sample(
        specimen, sampler_noise, probe_field, amplitudes[0, 0],
        corner_rows[0, 0].T, corner_cols[0, 0].T, slot_counts[0, 0],
        first_weight.T, first_bias.reshape(1, -1), second_weight, second_bias,
    )


def solution(mesh):
    return jax.shard_map(
        shards,
        mesh=mesh,
        in_specs=(
            P(None, "tile", "scan"),
            P(None, "tile", "scan"),
            P(),
            P("tile", "scan", None, None, None, None),
            P("tile", "scan", None, None),
            P("tile", "scan", None, None),
            P("tile", "scan", None),
            P(),
            P(),
            P(),
            P(),
        ),
        out_specs=P(None, "tile", "scan"),
        check_vma=False,
    )
```

```python
import functools

import jax
import jax.numpy as jnp
import numpy as np
from jax import lax
from jax.experimental import pallas as pl
from jax.experimental.pallas import tpu as pltpu
from jax.sharding import PartitionSpec as P

MESH = pl.DeviceIdType.MESH
NW = 256
HALF = 128
EDGE = 16
GROUP = 44
PRIOR_ROWS = 264
CAP = 2

ORDER_16 = [(3, 1), (1, 3), (2, 3), (1, 1), (3, 0), (2, 0), (3, 3), (1, 2), (0, 1), (0, 3), (2, 1), (3, 2), (1, 0), (0, 2), (2, 2)]
ISSUE_16 = [0, 2, 1, 4, 6, 8, 3, 13, 5, 11, 7, 9, 10, 14, 12]
SIDES = [(a, b) for a in (-1, 0, 1) for b in (-1, 0, 1) if (a, b) != (0, 0)]


def dft_matrices():
    index = np.arange(NW)
    angle = (index[:, None] * index[None, :] % NW) * (2.0 * np.pi / NW)
    cosine = (np.cos(angle) / 16.0).astype(jnp.bfloat16)
    sine = (np.sin(angle) / 16.0).astype(jnp.bfloat16)
    forward = np.concatenate([np.concatenate([cosine, sine], 1), np.concatenate([-sine, cosine], 1)], 0)
    return forward, np.ascontiguousarray(forward.T)


def span(step, low, mid, high):
    return {-1: low, 0: mid, 1: high}[step]


def patch_kernel(
    order, issue, rows_y, tiles, peers,
    rows_ref, cols_ref, counts_ref, amps_ref, spec_hbm, noise_hbm, probe_hbm, fwd_hbm, inv_hbm,
    w1_ref, b1_ref, w2_ref, b2_ref, sel1_ref, sel2_ref,
    out_ref,
    spec_ref, noise_ref, probe_ref, fwd_ref, inv_ref, load_sem,
    cells_ref, taps, mixed_sum, first_ref, first_edge, second_ref, second_edge,
    recv, frame, acc, rim, rim_in, probe2, rolled, wave_in, mid_ref, far_ref, wave_ref,
    amp_send, amp_recv, own_sem, halo_send, halo_recv, rim_send, rim_recv, ring_send, ring_recv,
):
    f32, bf16 = jnp.float32, jnp.bfloat16
    t = lax.axis_index("tile")
    s = lax.axis_index("scan")
    rows_z = peers // rows_y
    y, z = s // rows_z, lax.rem(s, rows_z)

    mirror = 1 - 2 * lax.rem(t, 2)

    def peer(dy, dz):
        return lax.rem(y + mirror * dy + rows_y, rows_y) * rows_z + lax.rem(z + mirror * dz + rows_z, rows_z)

    def exists(dt, ds):
        ok_t = {-1: t > 0, 0: t >= 0, 1: t < tiles - 1}[dt]
        ok_s = {-1: s > 0, 0: s >= 0, 1: s < peers - 1}[ds]
        return jnp.logical_and(ok_t, ok_s)

    barrier = pltpu.get_barrier_semaphore()
    expected = jnp.int32(len(order))
    for dy, dz in order:
        pl.semaphore_signal(barrier, inc=1, device_id=(t, peer(-dy, -dz)), device_id_type=MESH)
    for dt, ds in SIDES:
        if dt != 0:
            here = exists(dt, ds)
            expected = expected + here.astype(jnp.int32)

            @pl.when(here)
            def _():
                pl.semaphore_signal(barrier, inc=1, device_id=(t + dt, s + ds), device_id_type=MESH)

    loads = [
        pltpu.make_async_copy(source, place, load_sem.at[i])
        for i, (source, place) in enumerate(
            ((spec_hbm, spec_ref), (noise_hbm, noise_ref), (probe_hbm, probe_ref), (fwd_hbm, fwd_ref), (inv_hbm, inv_ref))
        )
    ]
    for load in loads:
        load.start()
    own = pltpu.make_async_copy(amps_ref.at[s], recv.at[0], own_sem)
    own.start()
    loads[0].wait()
    for part in range(2):
        frame[part, HALF : HALF + NW, HALF : HALF + NW] = spec_ref[part].astype(bf16)
    pl.semaphore_wait(barrier, expected)

    def halo_copy(k, dt, ds):
        src = (slice(None), slice(*span(dt, (128, 256), (128, 384), (256, 384))), slice(*span(ds, (128, 256), (128, 384), (256, 384))))
        dst = (slice(None), slice(*span(dt, (384, 512), (128, 384), (0, 128))), slice(*span(ds, (384, 512), (128, 384), (0, 128))))
        return pltpu.make_async_remote_copy(
            src_ref=frame.at[src], dst_ref=frame.at[dst], send_sem=halo_send.at[k], recv_sem=halo_recv.at[k],
            device_id=(t + dt, s + ds), device_id_type=MESH,
        )

    def relay_copy(k, dt, ds):
        columns = span(ds, slice(384, 512), None, slice(0, 128))
        return pltpu.make_async_remote_copy(
            src_ref=frame.at[:, span(dt, slice(128, 256), None, slice(256, 384)), columns],
            dst_ref=frame.at[:, span(dt, slice(384, 512), None, slice(0, 128)), columns],
            send_sem=halo_send.at[k], recv_sem=halo_recv.at[k], device_id=(t + dt, s), device_id_type=MESH,
        )

    def amp_copy(k, dy, dz):
        d = peer(dy, dz)
        return pltpu.make_async_remote_copy(
            src_ref=amps_ref.at[d], dst_ref=recv.at[k], send_sem=amp_send.at[k], recv_sem=amp_recv.at[k],
            device_id=(t, d), device_id_type=MESH,
        )

    straight = [(k, dt, ds) for k, (dt, ds) in enumerate(SIDES) if dt * ds == 0]
    diagonal = [(k, dt, ds) for k, (dt, ds) in enumerate(SIDES) if dt * ds != 0]
    for k, dt, ds in straight:
        @pl.when(exists(dt, ds))
        def _():
            halo_copy(k, dt, ds).start()

    for load in loads[1:]:
        load.wait()
    for part in range(2):
        acc[part] = jnp.zeros((2 * NW, 2 * NW), f32)
        acc[part, HALF : HALF + NW, HALF : HALF + NW] = spec_ref[part] + 0.5 * noise_ref[part]
        for half in range(2):
            columns = probe_ref[part, :, half * HALF : (half + 1) * HALF]
            probe2[part, half, :NW, :] = columns
            probe2[part, half, NW:, :] = columns

    def take_halo(k, dt, ds, copy):
        here = exists(-dt, -ds)

        @pl.when(here)
        def _():
            copy(k, dt, ds).wait_recv()

        @pl.when(jnp.logical_not(here))
        def _():
            at_row, at_col = span(dt, (384, 512), (128, 384), (0, 128)), span(ds, (384, 512), (128, 384), (0, 128))
            for part in range(2):
                frame[part, slice(*at_row), slice(*at_col)] = jnp.zeros((at_row[1] - at_row[0], at_col[1] - at_col[0]), bf16)

    for k, dt, ds in straight:
        take_halo(k, dt, ds, halo_copy)
    for k, dt, ds in diagonal:
        @pl.when(jnp.logical_and(exists(dt, 0), exists(0, -ds)))
        def _():
            relay_copy(k, dt, ds).start()
    for k in issue:
        amp_copy(k + 1, *order[k]).start()
    for k, dt, ds in diagonal:
        take_halo(k, dt, ds, relay_copy)

    square = lax.broadcasted_iota(jnp.int32, (128, 128), 0) == lax.broadcasted_iota(jnp.int32, (128, 128), 1)
    bias = jnp.sum(jnp.where(square, b1_ref[...], 0.0), axis=1, keepdims=True) * 0.5
    high = bias.astype(bf16).astype(f32)
    for v in range(3):
        column = lax.broadcasted_iota(jnp.int32, (128, 32), 1)
        at = 24 if v else 6
        weights = lax.dot_general(w1_ref[...], sel1_ref[v], (((0,), (0,)), ((), ())), preferred_element_type=f32)
        weights = (weights + jnp.where(column == at, high, 0.0) + jnp.where(column == at + 1, bias - high, 0.0)).astype(bf16)
        if v == 0:
            first_ref[...] = weights
        else:
            first_edge[(v - 1) * 128 : v * 128, :] = weights
    second_ref[...] = jnp.dot(sel2_ref[0], w2_ref[...], preferred_element_type=f32).astype(bf16)
    for side in range(2):
        for v in range(2):
            second_edge[side, :, v * 128 : (v + 1) * 128] = jnp.dot(
                sel2_ref[1 + 2 * side + v], w2_ref[...], preferred_element_type=f32
            ).astype(bf16)

    CH = 32
    lane = lax.broadcasted_iota(jnp.int32, (CH, NW), 1)
    sub = lax.broadcasted_iota(jnp.int32, (CH, NW), 0)

    def steps_of(k):
        dy, dz = jnp.int32(0), jnp.int32(0)
        for i, (a, b) in enumerate(order):
            dy = jnp.where(k == i + 1, a, dy)
            dz = jnp.where(k == i + 1, b, dz)
        return dy, dz

    def corners(k):
        dy, dz = steps_of(k)
        h = peer(-dy, -dz)
        return h, [(rows_ref[c, h], cols_ref[c, h]) for c in range(CAP)]

    def both(left_ref, right_ref, result):
        for c in range(CAP):
            mid = jnp.dot(left_ref[...], wave_in[:, c * NW : (c + 1) * NW], preferred_element_type=f32)
            for p in range(2):
                mid_ref[c * NW : (c + 1) * NW, p * NW : (p + 1) * NW] = mid[p * NW : (p + 1) * NW].astype(bf16)
        for p in range(2):
            result[:, p * NW : (p + 1) * NW] = jnp.dot(mid_ref[...], right_ref[:, p * NW : (p + 1) * NW], preferred_element_type=f32)


    def outward(k, carry):
        h, corner = corners(k)

        def exits(i, carry):
            base = pl.multiple_of(i * CH, CH)
            for c in range(CAP):
                r, q = corner[c]
                low_row = sub + base < r
                low_col = lane < q
                shift = lax.rem(q, NW)
                cell, prb = [], []
                for part in range(2):
                    tile = [[frame[part, pl.ds(base + a * NW, CH), b * NW : (b + 1) * NW].astype(f32) for b in range(2)] for a in range(2)]
                    cell.append(jnp.where(low_row, jnp.where(low_col, tile[1][1], tile[1][0]), jnp.where(low_col, tile[0][1], tile[0][0])))
                    turned = pltpu.roll(jnp.concatenate([probe2[part, half, pl.ds(base + NW - r, CH), :] for half in range(2)], 1), shift, 1)
                    rolled[k, c, part, pl.ds(base, CH), :] = turned
                    prb.append(turned)
                wave_in[pl.ds(base, CH), c * NW : (c + 1) * NW] = (prb[0] * cell[0] - prb[1] * cell[1]).astype(bf16)
                wave_in[pl.ds(base + NW, CH), c * NW : (c + 1) * NW] = (prb[0] * cell[1] + prb[1] * cell[0]).astype(bf16)
            return carry

        lax.fori_loop(0, NW // CH, exits, 0, unroll=True)
        both(fwd_ref, inv_ref, far_ref.at[k])
        return carry

    lax.fori_loop(0, len(order) + 1, outward, 0, unroll=2)
    own.wait()

    def inward(k, carry):
        h, corner = corners(k)
        dy, dz = steps_of(k)
        scale = [jnp.where(counts_ref[h] > c, f32(-0.25), f32(0.0)) for c in range(CAP)]

        @pl.when(k > 0)
        def _():
            pltpu.make_async_remote_copy(
                src_ref=recv.at[k], dst_ref=recv.at[k], send_sem=amp_send.at[k], recv_sem=amp_recv.at[k],
                device_id=(t, peer(dy, dz)), device_id_type=MESH,
            ).wait_recv()

        def correct(i, carry):
            base = pl.multiple_of(i * CH, CH)
            for c in range(CAP):
                fr = far_ref[k, pl.ds(base + c * NW, CH), :NW]
                fi = far_ref[k, pl.ds(base + c * NW, CH), NW:]
                amp = recv[k, c, pl.ds(base, CH), :].astype(f32)
                keep = 1.0 - amp * lax.rsqrt(jnp.maximum(fr * fr + fi * fi, 1.0))
                wave_in[pl.ds(base, CH), c * NW : (c + 1) * NW] = (fr * keep).astype(bf16)
                wave_in[pl.ds(base + NW, CH), c * NW : (c + 1) * NW] = (fi * keep).astype(bf16)
            return carry

        lax.fori_loop(0, NW // CH, correct, 0, unroll=True)
        both(inv_ref, fwd_ref, wave_ref)

        def gather(i, carry):
            base = pl.multiple_of(i * CH, CH)
            grads = []
            for c in range(CAP):
                wr = wave_ref[pl.ds(base + c * NW, CH), :NW]
                wi = wave_ref[pl.ds(base + c * NW, CH), NW:]
                pr = rolled[k, c, 0, pl.ds(base, CH), :] * scale[c]
                pi = rolled[k, c, 1, pl.ds(base, CH), :] * scale[c]
                grads.append((pr * wr + pi * wi, pr * wi - pi * wr))
            for a in range(2):
                for b in range(2):
                    masks = []
                    for c in range(CAP):
                        r, q = corner[c]
                        row_ok = sub + base < r if a else sub + base >= r
                        col_ok = lane < q if b else lane >= q
                        masks.append(jnp.logical_and(row_ok, col_ok))
                    for part in range(2):
                        total = acc[part, pl.ds(base + a * NW, CH), b * NW : (b + 1) * NW]
                        for c in range(CAP):
                            total = total + jnp.where(masks[c], grads[c][part], 0.0)
                        acc[part, pl.ds(base + a * NW, CH), b * NW : (b + 1) * NW] = total
            return carry

        lax.fori_loop(0, NW // CH, gather, 0, unroll=True)
        return carry

    lax.fori_loop(0, len(order) + 1, inward, 0, unroll=2)

    for part in range(2):
        for lo, hi in ((0, HALF), (HALF + NW, 2 * NW)):
            rim[part, :, lo:hi] = acc[part, :, lo:hi].astype(bf16)

    def rim_copy(k, dt, ds):
        where = (slice(None), slice(*span(dt, (0, 128), (128, 384), (384, 512))), slice(*span(ds, (0, 128), (128, 384), (384, 512))))
        return pltpu.make_async_remote_copy(
            src_ref=rim.at[where], dst_ref=rim_in.at[where], send_sem=rim_send.at[k], recv_sem=rim_recv.at[k],
            device_id=(t + dt, s + ds), device_id_type=MESH,
        )

    for k, dt, ds in [side for side in straight if side[2] != 0] + diagonal:
        @pl.when(exists(dt, ds))
        def _():
            rim_copy(k, dt, ds).start()
    for part in range(2):
        for lo, hi in ((0, HALF), (HALF + NW, 2 * NW)):
            rim[part, lo:hi, HALF : HALF + NW] = acc[part, lo:hi, HALF : HALF + NW].astype(bf16)
    for k, dt, ds in straight:
        if ds == 0:
            @pl.when(exists(dt, ds))
            def _():
                rim_copy(k, dt, ds).start()
    for part in range(2):
        out_ref[part] = acc[part, HALF : HALF + NW, HALF : HALF + NW]
    for k, dt, ds in sorted(straight, key=lambda side: side[2] != 0) + diagonal:
        @pl.when(exists(-dt, -ds))
        def _():
            rim_copy(k, dt, ds).wait_recv()
            src_r, dst_r = span(dt, ((0, 128), (128, 256)), ((128, 384), (0, 256)), ((384, 512), (0, 128)))
            src_c, dst_c = span(ds, ((0, 128), (128, 256)), ((128, 384), (0, 256)), ((384, 512), (0, 128)))
            for part in range(2):
                out_ref[part, slice(*dst_r), slice(*dst_c)] += rim_in[part, slice(*src_r), slice(*src_c)].astype(f32)
    for part in range(2):
        cells_ref[part, EDGE : EDGE + NW, HALF : HALF + NW] = out_ref[part].astype(bf16)

    def ring_copy(k, dt, ds):
        src = (slice(None), slice(*span(dt, (16, 32), (16, 272), (256, 272))), slice(*span(ds, (128, 256), (128, 384), (256, 384))))
        dst = (slice(None), slice(*span(dt, (272, 288), (16, 272), (0, 16))), slice(*span(ds, (384, 512), (128, 384), (0, 128))))
        return pltpu.make_async_remote_copy(
            src_ref=cells_ref.at[src], dst_ref=cells_ref.at[dst], send_sem=ring_send.at[k], recv_sem=ring_recv.at[k],
            device_id=(t + dt, s + ds), device_id_type=MESH,
        )

    for k, (dt, ds) in enumerate(SIDES):
        @pl.when(exists(dt, ds))
        def _():
            ring_copy(k, dt, ds).start()
    def moved(rows256, dx):
        return rows256 if dx == 1 else pltpu.roll(rows256, 1 if dx == 0 else NW - 1, 1)

    for part in range(2):
        for dx in range(3):
            shifted = moved(out_ref[part], dx)
            for v in range(2):
                taps[v, pl.ds(16 + 3 * part + dx, NW, stride=8), :] = shifted[:, v * 128 : (v + 1) * 128]
    for v in range(2):
        for k in (6, 7):
            taps[v, pl.ds(k, NW + 4, stride=8), :] = jnp.ones((NW + 4, 128), f32)

    mlane = lax.broadcasted_iota(jnp.int32, (24, 128), 1)
    inner = (mlane > 0, mlane < 127)

    def hidden_of(weights, window):
        pre = jnp.dot(weights, window, preferred_element_type=f32)
        return pre + pre * jnp.tanh(pre)

    def mixed_rows(starts):
        window = jnp.concatenate([taps[v, pl.ds(start, 24), :].astype(bf16) for start in starts for v in range(2)], 1)
        return jnp.dot(second_ref[...], hidden_of(first_ref[:, :24], window).astype(bf16), preferred_element_type=f32)

    def group(g, carry):
        older, old = carry
        mixed_all = mixed_rows([pl.multiple_of((g * GROUP + j) * 8, 8) for j in range(GROUP)])
        for j in range(GROUP):
            index = g * GROUP + j
            here = jnp.logical_and(index > 1, index < NW)
            mixed = [jnp.where(jnp.logical_and(inner[v], here), mixed_all[:, (2 * j + v) * 128 : (2 * j + v + 1) * 128], 0.0) for v in range(2)]
            for v in range(2):
                mixed_sum[v, pl.ds(pl.multiple_of(index * 8, 8), 8), :] = older[v] + mixed[v][16:24]
            older = [old[v] + mixed[v][8:16] for v in range(2)]
            old = [mixed[v][0:8] for v in range(2)]
        return older, old

    zero = [jnp.zeros((8, 128), f32)] * 2
    lax.fori_loop(0, PRIOR_ROWS // GROUP, group, (zero, zero))

    for k, (dt, ds) in enumerate(SIDES):
        here = exists(-dt, -ds)

        @pl.when(here)
        def _():
            ring_copy(k, dt, ds).wait_recv()

        @pl.when(jnp.logical_not(here))
        def _():
            at_row, at_col = span(dt, (272, 288), (16, 272), (0, 16)), span(ds, (384, 512), (128, 384), (0, 128))
            for part in range(2):
                cells_ref[part, slice(*at_row), slice(*at_col)] = jnp.zeros((at_row[1] - at_row[0], at_col[1] - at_col[0]), bf16)

    for part in range(2):
        for at, first_row, take in ((0, 0, 14), (NW + 2, EDGE + NW, 0)):
            strip = cells_ref[part, first_row : first_row + EDGE, HALF : HALF + NW].astype(f32)
            for dx in range(3):
                shifted = moved(strip, dx)
                for v in range(2):
                    for i in range(2):
                        taps[v, (at + i) * 8 + 3 * part + dx : (at + i) * 8 + 3 * part + dx + 1, :] = shifted[take + i : take + i + 1, v * 128 : (v + 1) * 128]
    border = (0, 1, NW, NW + 1)
    mixed_all = mixed_rows([8 * index for index in border])
    for j, index in enumerate(border):
        here = {0: t > 0, NW + 1: t < tiles - 1}.get(index, t >= 0)
        for v in range(2):
            mixed = jnp.where(jnp.logical_and(inner[v], here), mixed_all[:, (2 * j + v) * 128 : (2 * j + v + 1) * 128], 0.0)
            for dy in range(3):
                row = index + 2 - dy
                if 2 <= row < NW + 2:
                    mixed_sum[v, row * 8 : row * 8 + 8, :] += mixed[8 * dy : 8 * dy + 8]

    WIDE = 384
    strip_lane = lax.broadcasted_iota(jnp.int32, (NW + 2 * EDGE, 128), 1)
    row_lane = lax.broadcasted_iota(jnp.int32, (8, WIDE), 1)
    constant = jnp.where(lax.broadcasted_iota(jnp.int32, (8, WIDE), 0) < 2, 1.0, 0.0)
    edge_sum = None
    for side in range(2):
        planes = [cells_ref[part, :, side * NW : (side + 1) * NW].astype(f32) for part in range(2)]
        strips = [pltpu.roll(planes[part], NW - 126 + 4 * part, 1)[:, :128] for part in range(2)]
        strip = jnp.where(strip_lane < 4, strips[0], strips[1])
        strip = jnp.concatenate([strip, jnp.zeros((WIDE - NW - 2 * EDGE, 128), f32)], 0).T[:8]
        window = jnp.concatenate([pltpu.roll(strip, 1, 1), strip, pltpu.roll(strip, WIDE - 1, 1), constant], 0).astype(bf16)
        hidden = hidden_of(first_edge[...], window)
        outer = lax.broadcasted_iota(jnp.int32, (NW, WIDE), 0) < 128 if side == 0 else lax.broadcasted_iota(jnp.int32, (NW, WIDE), 0) >= 128
        gone = s == 0 if side == 0 else s == peers - 1
        hidden = jnp.where(jnp.logical_and(outer, gone), 0.0, hidden).astype(bf16)
        mixed = jnp.dot(second_edge[side], hidden, preferred_element_type=f32)
        edge_sum = mixed if edge_sum is None else edge_sum + mixed
    by_dy = []
    for dy in range(3):
        piece = edge_sum[8 * dy : 8 * dy + 8]
        piece = jnp.where(jnp.logical_and(row_lane == EDGE - 1, t == 0), 0.0, piece)
        piece = jnp.where(jnp.logical_and(row_lane == EDGE + NW, t == tiles - 1), 0.0, piece)
        by_dy.append(piece if dy == 1 else pltpu.roll(piece, 1 if dy == 0 else WIDE - 1, 1))
    columns = by_dy[0] + by_dy[1] + by_dy[2]
    columns = jnp.concatenate([columns, jnp.zeros((120, WIDE), f32)], 0).T[EDGE : EDGE + NW]
    out_lane = lax.broadcasted_iota(jnp.int32, (NW, 128), 1)
    for part in range(2):
        halves = [jnp.zeros((NW, 128), f32), jnp.zeros((NW, 128), f32)]
        for dx in range(3):
            sums = jnp.concatenate([mixed_sum[v, pl.ds(16 + 3 * part + dx, NW, stride=8), :] for v in range(2)], 1)
            sums = sums if dx == 1 else pltpu.roll(sums, 1 if dx == 0 else NW - 1, 1)
            halves = [halves[v] + sums[:, v * 128 : (v + 1) * 128] for v in range(2)]
        left = pltpu.roll(columns, (128 - 2 * part) % 128, 1) if part else columns
        right = pltpu.roll(columns, 126 - 4 - 2 * part, 1)
        halves[0] = halves[0] + jnp.where(out_lane < 2, left, 0.0)
        halves[1] = halves[1] + jnp.where(out_lane >= 126, right, 0.0)
        for v in range(2):
            at = slice(v * 128, (v + 1) * 128)
            out_ref[part, :, at] = out_ref[part, :, at] - (halves[v] + b2_ref[part])
    for k, (dt, ds) in enumerate(SIDES):
        @pl.when(exists(dt, ds))
        def _():
            ring_copy(k, dt, ds).wait_send()
            rim_copy(k, dt, ds).wait_send()
    for k, dt, ds in straight:
        @pl.when(exists(dt, ds))
        def _():
            halo_copy(k, dt, ds).wait_send()
    for k, dt, ds in diagonal:
        @pl.when(jnp.logical_and(exists(dt, 0), exists(0, -ds)))
        def _():
            relay_copy(k, dt, ds).wait_send()
    for k, (dy, dz) in enumerate(order):
        amp_copy(k + 1, dy, dz).wait_send()


def sample(specimen, noise, probe, amps, rows, cols, counts, w1, b1, w2, b2):
    tiles, peers = lax.axis_size("tile"), lax.axis_size("scan")
    if peers == 16:
        order, issue, rows_y = ORDER_16, ISSUE_16, 4
    else:
        order, issue, rows_y = [(0, b) for b in range(1, peers)], list(range(peers - 1)), 1
    forward, inverse = dft_matrices()
    one, two = tap_selectors()
    f32, bf16 = jnp.float32, jnp.bfloat16
    smem = pl.BlockSpec(memory_space=pltpu.SMEM)
    vmem = pl.BlockSpec(memory_space=pltpu.VMEM)
    dma = pltpu.SemaphoreType.DMA
    return pl.pallas_call(
        functools.partial(patch_kernel, order, issue, rows_y, tiles, peers),
        out_shape=pltpu.VMEM((2, NW, NW), f32),
        in_specs=[smem, smem, smem, pl.BlockSpec(memory_space=pl.ANY)] + [pl.BlockSpec(memory_space=pl.ANY)] * 5 + [vmem, vmem, vmem, smem, vmem, vmem],
        out_specs=vmem,
        scratch_shapes=[
            pltpu.VMEM((2, NW, NW), f32),
            pltpu.VMEM((2, NW, NW), f32),
            pltpu.VMEM((2, NW, NW), f32),
            pltpu.VMEM((2 * NW, 2 * NW), bf16),
            pltpu.VMEM((2 * NW, 2 * NW), bf16),
            dma((5,)),
            pltpu.VMEM((2, NW + 2 * EDGE, 2 * NW), bf16),
            pltpu.VMEM((2, 8 * (PRIOR_ROWS + 2), 128), f32),
            pltpu.VMEM((2, 8 * PRIOR_ROWS, 128), f32),
            pltpu.VMEM((128, 32), bf16),
            pltpu.VMEM((NW, 32), bf16),
            pltpu.VMEM((24, 128), bf16),
            pltpu.VMEM((2, 24, NW), bf16),
            pltpu.VMEM((peers, CAP, NW, NW), bf16),
            pltpu.VMEM((2, 2 * NW, 2 * NW), bf16),
            pltpu.VMEM((2, 2 * NW, 2 * NW), f32),
            pltpu.VMEM((2, 2 * NW, 2 * NW), bf16),
            pltpu.VMEM((2, 2 * NW, 2 * NW), bf16),
            pltpu.VMEM((2, 2, 2 * NW, HALF), f32),
            pltpu.VMEM((peers, CAP, 2, NW, NW), f32),
            pltpu.VMEM((2 * NW, 2 * NW), bf16),
            pltpu.VMEM((2 * NW, 2 * NW), bf16),
            pltpu.VMEM((peers, 2 * NW, 2 * NW), f32),
            pltpu.VMEM((2 * NW, 2 * NW), f32),
            dma((peers,)), dma((peers,)), dma, dma((8,)), dma((8,)), dma((8,)), dma((8,)), dma((8,)), dma((8,)),
        ],
        compiler_params=pltpu.CompilerParams(collective_id=0, has_side_effects=True, vmem_limit_bytes=62 << 20),
        name="step",
    )(rows, cols, counts, amps, specimen, noise, probe, jnp.asarray(forward), jnp.asarray(inverse),
      w1, b1, w2, b2, jnp.asarray(one), jnp.asarray(two))


def tap_selectors():
    first = np.zeros((3, 18, 32), np.float32)
    second = np.zeros((5, 24, 18), np.float32)
    for c in range(2):
        for dy in range(3):
            for dx in range(3):
                tap = 9 * c + 3 * dy + dx
                first[0, tap, 8 * dy + 3 * c + dx] = 0.5
                first[1, tap, 8 * dy + 4 * c + dx] = 0.5
                first[2, tap, 8 * dy + 4 * c + dx + 1] = 0.5
                second[0, 8 * dy + 3 * c + dx, tap] = 1.0
            for side, half, dx, at in ((0, 0, 0, 0), (0, 1, 1, 0), (0, 1, 0, 1), (1, 0, 2, 0), (1, 0, 1, 1), (1, 1, 2, 1)):
                second[1 + 2 * side + half, 8 * dy + 4 * side + 2 * c + at, 9 * c + 3 * dy + dx] = 1.0
    return first.astype(jnp.bfloat16), second.astype(jnp.bfloat16)


def shards(
    specimen, sampler_noise, probe_field, amplitudes, corner_rows, corner_cols, slot_counts,
    first_weight, first_bias, second_weight, second_bias,
):
    return sample(
        specimen, sampler_noise, probe_field, amplitudes[0, 0],
        corner_rows[0, 0].T, corner_cols[0, 0].T, slot_counts[0, 0],
        first_weight.T, first_bias.reshape(1, -1), second_weight, second_bias,
    )


def solution(mesh):
    return jax.shard_map(
        shards,
        mesh=mesh,
        in_specs=(
            P(None, "tile", "scan"),
            P(None, "tile", "scan"),
            P(),
            P("tile", "scan", None, None, None, None),
            P("tile", "scan", None, None),
            P("tile", "scan", None, None),
            P("tile", "scan", None),
            P(),
            P(),
            P(),
            P(),
        ),
        out_specs=P(None, "tile", "scan"),
        check_vma=False,
    )
```

```python
import functools

import jax
import jax.numpy as jnp
import numpy as np
from jax import lax
from jax.experimental import pallas as pl
from jax.experimental.pallas import tpu as pltpu
from jax.sharding import PartitionSpec as P

MESH = pl.DeviceIdType.MESH
NW = 256
HALF = 128
EDGE = 16
GROUP = 44
PRIOR_ROWS = 264
CAP = 2

ORDER_16 = [(3, 1), (1, 3), (2, 3), (1, 1), (3, 0), (2, 0), (3, 3), (1, 2), (0, 1), (0, 3), (2, 1), (3, 2), (1, 0), (0, 2), (2, 2)]
ISSUE_16 = [0, 2, 1, 4, 6, 8, 3, 13, 5, 11, 7, 9, 10, 14, 12]
SIDES = [(a, b) for a in (-1, 0, 1) for b in (-1, 0, 1) if (a, b) != (0, 0)]


def dft_matrices():
    index = np.arange(NW)
    angle = (index[:, None] * index[None, :] % NW) * (2.0 * np.pi / NW)
    cosine = (np.cos(angle) / 16.0).astype(jnp.bfloat16)
    sine = (np.sin(angle) / 16.0).astype(jnp.bfloat16)
    forward = np.concatenate([np.concatenate([cosine, sine], 1), np.concatenate([-sine, cosine], 1)], 0)
    return forward, np.ascontiguousarray(forward.T)


def span(step, low, mid, high):
    return {-1: low, 0: mid, 1: high}[step]


def patch_kernel(
    order, issue, rows_y, tiles, peers,
    rows_ref, cols_ref, counts_ref, amps_ref, spec_hbm, noise_hbm, probe_hbm, fwd_hbm, inv_hbm,
    w1_ref, b1_ref, w2_ref, b2_ref, sel1_ref, sel2_ref,
    out_ref,
    spec_ref, noise_ref, probe_ref, fwd_ref, inv_ref, load_sem,
    cells_ref, taps, mixed_sum, first_ref, first_edge, second_ref, second_edge,
    recv, frame, acc, rim, rim_in, probe2, rolled, wave_in, mid_ref, far_ref, wave_ref,
    amp_send, amp_recv, own_sem, halo_send, halo_recv, rim_send, rim_recv, ring_send, ring_recv,
):
    f32, bf16 = jnp.float32, jnp.bfloat16
    t = lax.axis_index("tile")
    s = lax.axis_index("scan")
    rows_z = peers // rows_y
    y, z = s // rows_z, lax.rem(s, rows_z)

    mirror = 1 - 2 * lax.rem(t, 2)

    def peer(dy, dz):
        return lax.rem(y + mirror * dy + rows_y, rows_y) * rows_z + lax.rem(z + mirror * dz + rows_z, rows_z)

    def exists(dt, ds):
        ok_t = {-1: t > 0, 0: t >= 0, 1: t < tiles - 1}[dt]
        ok_s = {-1: s > 0, 0: s >= 0, 1: s < peers - 1}[ds]
        return jnp.logical_and(ok_t, ok_s)

    barrier = pltpu.get_barrier_semaphore()
    expected = jnp.int32(len(order))
    for dy, dz in order:
        pl.semaphore_signal(barrier, inc=1, device_id=(t, peer(-dy, -dz)), device_id_type=MESH)
    for dt, ds in SIDES:
        if dt != 0:
            here = exists(dt, ds)
            expected = expected + here.astype(jnp.int32)

            @pl.when(here)
            def _():
                pl.semaphore_signal(barrier, inc=1, device_id=(t + dt, s + ds), device_id_type=MESH)

    loads = [
        pltpu.make_async_copy(source, place, load_sem.at[i])
        for i, (source, place) in enumerate(
            ((spec_hbm, spec_ref), (noise_hbm, noise_ref), (probe_hbm, probe_ref), (fwd_hbm, fwd_ref), (inv_hbm, inv_ref))
        )
    ]
    for load in loads:
        load.start()
    own = pltpu.make_async_copy(amps_ref.at[s], recv.at[0], own_sem)
    own.start()
    loads[0].wait()
    for part in range(2):
        frame[part, HALF : HALF + NW, HALF : HALF + NW] = spec_ref[part].astype(bf16)
    pl.semaphore_wait(barrier, expected)

    def halo_copy(k, dt, ds):
        src = (slice(None), slice(*span(dt, (128, 256), (128, 384), (256, 384))), slice(*span(ds, (128, 256), (128, 384), (256, 384))))
        dst = (slice(None), slice(*span(dt, (384, 512), (128, 384), (0, 128))), slice(*span(ds, (384, 512), (128, 384), (0, 128))))
        return pltpu.make_async_remote_copy(
            src_ref=frame.at[src], dst_ref=frame.at[dst], send_sem=halo_send.at[k], recv_sem=halo_recv.at[k],
            device_id=(t + dt, s + ds), device_id_type=MESH,
        )

    def relay_copy(k, dt, ds):
        columns = span(ds, slice(384, 512), None, slice(0, 128))
        return pltpu.make_async_remote_copy(
            src_ref=frame.at[:, span(dt, slice(128, 256), None, slice(256, 384)), columns],
            dst_ref=frame.at[:, span(dt, slice(384, 512), None, slice(0, 128)), columns],
            send_sem=halo_send.at[k], recv_sem=halo_recv.at[k], device_id=(t + dt, s), device_id_type=MESH,
        )

    def amp_copy(k, dy, dz):
        d = peer(dy, dz)
        return pltpu.make_async_remote_copy(
            src_ref=amps_ref.at[d], dst_ref=recv.at[k], send_sem=amp_send.at[k], recv_sem=amp_recv.at[k],
            device_id=(t, d), device_id_type=MESH,
        )

    straight = [(k, dt, ds) for k, (dt, ds) in enumerate(SIDES) if dt * ds == 0]
    diagonal = [(k, dt, ds) for k, (dt, ds) in enumerate(SIDES) if dt * ds != 0]
    for k, dt, ds in straight:
        @pl.when(exists(dt, ds))
        def _():
            halo_copy(k, dt, ds).start()

    for load in loads[1:]:
        load.wait()
    for part in range(2):
        acc[part] = jnp.zeros((2 * NW, 2 * NW), f32)
        acc[part, HALF : HALF + NW, HALF : HALF + NW] = spec_ref[part] + 0.5 * noise_ref[part]
        for half in range(2):
            columns = probe_ref[part, :, half * HALF : (half + 1) * HALF]
            probe2[part, half, :NW, :] = columns
            probe2[part, half, NW:, :] = columns

    def take_halo(k, dt, ds, copy):
        here = exists(-dt, -ds)

        @pl.when(here)
        def _():
            copy(k, dt, ds).wait_recv()

        @pl.when(jnp.logical_not(here))
        def _():
            at_row, at_col = span(dt, (384, 512), (128, 384), (0, 128)), span(ds, (384, 512), (128, 384), (0, 128))
            for part in range(2):
                frame[part, slice(*at_row), slice(*at_col)] = jnp.zeros((at_row[1] - at_row[0], at_col[1] - at_col[0]), bf16)

    for k, dt, ds in straight:
        take_halo(k, dt, ds, halo_copy)
    for k, dt, ds in diagonal:
        @pl.when(jnp.logical_and(exists(dt, 0), exists(0, -ds)))
        def _():
            relay_copy(k, dt, ds).start()
    for k in issue:
        amp_copy(k + 1, *order[k]).start()
    for k, dt, ds in diagonal:
        take_halo(k, dt, ds, relay_copy)

    square = lax.broadcasted_iota(jnp.int32, (128, 128), 0) == lax.broadcasted_iota(jnp.int32, (128, 128), 1)
    bias = jnp.sum(jnp.where(square, b1_ref[...], 0.0), axis=1, keepdims=True) * 0.5
    high = bias.astype(bf16).astype(f32)
    for v in range(3):
        column = lax.broadcasted_iota(jnp.int32, (128, 32), 1)
        at = 24 if v else 6
        weights = lax.dot_general(w1_ref[...], sel1_ref[v], (((0,), (0,)), ((), ())), preferred_element_type=f32)
        weights = (weights + jnp.where(column == at, high, 0.0) + jnp.where(column == at + 1, bias - high, 0.0)).astype(bf16)
        if v == 0:
            first_ref[...] = weights
        else:
            first_edge[(v - 1) * 128 : v * 128, :] = weights
    second_ref[...] = jnp.dot(sel2_ref[0], w2_ref[...], preferred_element_type=f32).astype(bf16)
    for side in range(2):
        for v in range(2):
            second_edge[side, :, v * 128 : (v + 1) * 128] = jnp.dot(
                sel2_ref[1 + 2 * side + v], w2_ref[...], preferred_element_type=f32
            ).astype(bf16)

    CH = 32
    lane = lax.broadcasted_iota(jnp.int32, (CH, NW), 1)
    sub = lax.broadcasted_iota(jnp.int32, (CH, NW), 0)

    def steps_of(k):
        dy, dz = jnp.int32(0), jnp.int32(0)
        for i, (a, b) in enumerate(order):
            dy = jnp.where(k == i + 1, a, dy)
            dz = jnp.where(k == i + 1, b, dz)
        return dy, dz

    def corners(k):
        dy, dz = steps_of(k)
        h = peer(-dy, -dz)
        return h, [(rows_ref[c, h], cols_ref[c, h]) for c in range(CAP)]

    def both(left_ref, right_ref, result):
        for c in range(CAP):
            mid = jnp.dot(left_ref[...], wave_in[:, c * NW : (c + 1) * NW], preferred_element_type=f32)
            for p in range(2):
                mid_ref[c * NW : (c + 1) * NW, p * NW : (p + 1) * NW] = mid[p * NW : (p + 1) * NW].astype(bf16)
        for p in range(2):
            result[:, p * NW : (p + 1) * NW] = jnp.dot(mid_ref[...], right_ref[:, p * NW : (p + 1) * NW], preferred_element_type=f32)


    def outward(k, carry):
        h, corner = corners(k)

        def exits(i, carry):
            base = pl.multiple_of(i * CH, CH)
            for c in range(CAP):
                r, q = corner[c]
                low_row = sub + base < r
                low_col = lane < q
                shift = lax.rem(q, NW)
                cell, prb = [], []
                for part in range(2):
                    tile = [[frame[part, pl.ds(base + a * NW, CH), b * NW : (b + 1) * NW].astype(f32) for b in range(2)] for a in range(2)]
                    cell.append(jnp.where(low_row, jnp.where(low_col, tile[1][1], tile[1][0]), jnp.where(low_col, tile[0][1], tile[0][0])))
                    turned = pltpu.roll(jnp.concatenate([probe2[part, half, pl.ds(base + NW - r, CH), :] for half in range(2)], 1), shift, 1)
                    rolled[k, c, part, pl.ds(base, CH), :] = turned
                    prb.append(turned)
                wave_in[pl.ds(base, CH), c * NW : (c + 1) * NW] = (prb[0] * cell[0] - prb[1] * cell[1]).astype(bf16)
                wave_in[pl.ds(base + NW, CH), c * NW : (c + 1) * NW] = (prb[0] * cell[1] + prb[1] * cell[0]).astype(bf16)
            return carry

        lax.fori_loop(0, NW // CH, exits, 0, unroll=True)
        both(fwd_ref, inv_ref, far_ref.at[k])
        return carry

    lax.fori_loop(0, len(order) + 1, outward, 0, unroll=2)
    own.wait()

    def inward(k, carry):
        h, corner = corners(k)
        dy, dz = steps_of(k)
        scale = [jnp.where(counts_ref[h] > c, f32(-0.25), f32(0.0)) for c in range(CAP)]

        @pl.when(k > 0)
        def _():
            pltpu.make_async_remote_copy(
                src_ref=recv.at[k], dst_ref=recv.at[k], send_sem=amp_send.at[k], recv_sem=amp_recv.at[k],
                device_id=(t, peer(dy, dz)), device_id_type=MESH,
            ).wait_recv()

        def correct(i, carry):
            base = pl.multiple_of(i * CH, CH)
            for c in range(CAP):
                fr = far_ref[k, pl.ds(base + c * NW, CH), :NW]
                fi = far_ref[k, pl.ds(base + c * NW, CH), NW:]
                amp = recv[k, c, pl.ds(base, CH), :].astype(f32)
                keep = 1.0 - amp * lax.rsqrt(jnp.maximum(fr * fr + fi * fi, 1.0))
                wave_in[pl.ds(base, CH), c * NW : (c + 1) * NW] = (fr * keep).astype(bf16)
                wave_in[pl.ds(base + NW, CH), c * NW : (c + 1) * NW] = (fi * keep).astype(bf16)
            return carry

        lax.fori_loop(0, NW // CH, correct, 0, unroll=True)
        both(inv_ref, fwd_ref, wave_ref)

        def gather(i, carry):
            base = pl.multiple_of(i * CH, CH)
            grads = []
            for c in range(CAP):
                wr = wave_ref[pl.ds(base + c * NW, CH), :NW]
                wi = wave_ref[pl.ds(base + c * NW, CH), NW:]
                pr = rolled[k, c, 0, pl.ds(base, CH), :] * scale[c]
                pi = rolled[k, c, 1, pl.ds(base, CH), :] * scale[c]
                grads.append((pr * wr + pi * wi, pr * wi - pi * wr))
            for a in range(2):
                for b in range(2):
                    masks = []
                    for c in range(CAP):
                        r, q = corner[c]
                        row_ok = sub + base < r if a else sub + base >= r
                        col_ok = lane < q if b else lane >= q
                        masks.append(jnp.logical_and(row_ok, col_ok))
                    for part in range(2):
                        total = acc[part, pl.ds(base + a * NW, CH), b * NW : (b + 1) * NW]
                        for c in range(CAP):
                            total = total + jnp.where(masks[c], grads[c][part], 0.0)
                        acc[part, pl.ds(base + a * NW, CH), b * NW : (b + 1) * NW] = total
            return carry

        lax.fori_loop(0, NW // CH, gather, 0, unroll=True)
        return carry

    lax.fori_loop(0, len(order) + 1, inward, 0, unroll=2)

    for part in range(2):
        for lo, hi in ((0, HALF), (HALF + NW, 2 * NW)):
            rim[part, :, lo:hi] = acc[part, :, lo:hi].astype(bf16)

    def rim_copy(k, dt, ds):
        where = (slice(None), slice(*span(dt, (0, 128), (128, 384), (384, 512))), slice(*span(ds, (0, 128), (128, 384), (384, 512))))
        return pltpu.make_async_remote_copy(
            src_ref=rim.at[where], dst_ref=rim_in.at[where], send_sem=rim_send.at[k], recv_sem=rim_recv.at[k],
            device_id=(t + dt, s + ds), device_id_type=MESH,
        )

    for k, dt, ds in [side for side in straight if side[2] != 0] + diagonal:
        @pl.when(exists(dt, ds))
        def _():
            rim_copy(k, dt, ds).start()
    for part in range(2):
        for lo, hi in ((0, HALF), (HALF + NW, 2 * NW)):
            rim[part, lo:hi, HALF : HALF + NW] = acc[part, lo:hi, HALF : HALF + NW].astype(bf16)
    for k, dt, ds in straight:
        if ds == 0:
            @pl.when(exists(dt, ds))
            def _():
                rim_copy(k, dt, ds).start()
    for part in range(2):
        out_ref[part] = acc[part, HALF : HALF + NW, HALF : HALF + NW]
    for k, dt, ds in sorted(straight, key=lambda side: side[2] != 0) + diagonal:
        @pl.when(exists(-dt, -ds))
        def _():
            rim_copy(k, dt, ds).wait_recv()
            src_r, dst_r = span(dt, ((0, 128), (128, 256)), ((128, 384), (0, 256)), ((384, 512), (0, 128)))
            src_c, dst_c = span(ds, ((0, 128), (128, 256)), ((128, 384), (0, 256)), ((384, 512), (0, 128)))
            for part in range(2):
                out_ref[part, slice(*dst_r), slice(*dst_c)] += rim_in[part, slice(*src_r), slice(*src_c)].astype(f32)
    for part in range(2):
        cells_ref[part, EDGE : EDGE + NW, HALF : HALF + NW] = out_ref[part].astype(bf16)

    def ring_copy(k, dt, ds):
        src = (slice(None), slice(*span(dt, (16, 32), (16, 272), (256, 272))), slice(*span(ds, (128, 256), (128, 384), (256, 384))))
        dst = (slice(None), slice(*span(dt, (272, 288), (16, 272), (0, 16))), slice(*span(ds, (384, 512), (128, 384), (0, 128))))
        return pltpu.make_async_remote_copy(
            src_ref=cells_ref.at[src], dst_ref=cells_ref.at[dst], send_sem=ring_send.at[k], recv_sem=ring_recv.at[k],
            device_id=(t + dt, s + ds), device_id_type=MESH,
        )

    for k, dt, ds in sorted(straight, key=lambda side: side[2] == 0) + diagonal:
        @pl.when(exists(dt, ds))
        def _():
            ring_copy(k, dt, ds).start()
    def moved(rows256, dx):
        return rows256 if dx == 1 else pltpu.roll(rows256, 1 if dx == 0 else NW - 1, 1)

    for part in range(2):
        for dx in range(3):
            shifted = moved(out_ref[part], dx)
            for v in range(2):
                taps[v, pl.ds(16 + 3 * part + dx, NW, stride=8), :] = shifted[:, v * 128 : (v + 1) * 128]
    for v in range(2):
        for k in (6, 7):
            taps[v, pl.ds(k, NW + 4, stride=8), :] = jnp.ones((NW + 4, 128), f32)

    mlane = lax.broadcasted_iota(jnp.int32, (24, 128), 1)
    inner = (mlane > 0, mlane < 127)

    def hidden_of(weights, window):
        pre = jnp.dot(weights, window, preferred_element_type=f32)
        return pre + pre * jnp.tanh(pre)

    def mixed_rows(starts):
        window = jnp.concatenate([taps[v, pl.ds(start, 24), :].astype(bf16) for start in starts for v in range(2)], 1)
        return jnp.dot(second_ref[...], hidden_of(first_ref[:, :24], window).astype(bf16), preferred_element_type=f32)

    def group(g, carry):
        older, old = carry
        mixed_all = mixed_rows([pl.multiple_of((g * GROUP + j) * 8, 8) for j in range(GROUP)])
        for j in range(GROUP):
            index = g * GROUP + j
            here = jnp.logical_and(index > 1, index < NW)
            mixed = [jnp.where(jnp.logical_and(inner[v], here), mixed_all[:, (2 * j + v) * 128 : (2 * j + v + 1) * 128], 0.0) for v in range(2)]
            for v in range(2):
                mixed_sum[v, pl.ds(pl.multiple_of(index * 8, 8), 8), :] = older[v] + mixed[v][16:24]
            older = [old[v] + mixed[v][8:16] for v in range(2)]
            old = [mixed[v][0:8] for v in range(2)]
        return older, old

    zero = [jnp.zeros((8, 128), f32)] * 2
    lax.fori_loop(0, PRIOR_ROWS // GROUP, group, (zero, zero))

    for k, (dt, ds) in enumerate(SIDES):
        here = exists(-dt, -ds)

        @pl.when(here)
        def _():
            ring_copy(k, dt, ds).wait_recv()

        @pl.when(jnp.logical_not(here))
        def _():
            at_row, at_col = span(dt, (272, 288), (16, 272), (0, 16)), span(ds, (384, 512), (128, 384), (0, 128))
            for part in range(2):
                cells_ref[part, slice(*at_row), slice(*at_col)] = jnp.zeros((at_row[1] - at_row[0], at_col[1] - at_col[0]), bf16)

    for part in range(2):
        for at, first_row, take in ((0, 0, 14), (NW + 2, EDGE + NW, 0)):
            strip = cells_ref[part, first_row : first_row + EDGE, HALF : HALF + NW].astype(f32)
            for dx in range(3):
                shifted = moved(strip, dx)
                for v in range(2):
                    for i in range(2):
                        taps[v, (at + i) * 8 + 3 * part + dx : (at + i) * 8 + 3 * part + dx + 1, :] = shifted[take + i : take + i + 1, v * 128 : (v + 1) * 128]
    border = (0, 1, NW, NW + 1)
    mixed_all = mixed_rows([8 * index for index in border])
    for j, index in enumerate(border):
        here = {0: t > 0, NW + 1: t < tiles - 1}.get(index, t >= 0)
        for v in range(2):
            mixed = jnp.where(jnp.logical_and(inner[v], here), mixed_all[:, (2 * j + v) * 128 : (2 * j + v + 1) * 128], 0.0)
            for dy in range(3):
                row = index + 2 - dy
                if 2 <= row < NW + 2:
                    mixed_sum[v, row * 8 : row * 8 + 8, :] += mixed[8 * dy : 8 * dy + 8]

    WIDE = 384
    strip_lane = lax.broadcasted_iota(jnp.int32, (NW + 2 * EDGE, 128), 1)
    row_lane = lax.broadcasted_iota(jnp.int32, (8, WIDE), 1)
    constant = jnp.where(lax.broadcasted_iota(jnp.int32, (8, WIDE), 0) < 2, 1.0, 0.0)
    edge_sum = None
    for side in range(2):
        planes = [cells_ref[part, :, side * NW : (side + 1) * NW].astype(f32) for part in range(2)]
        strips = [pltpu.roll(planes[part], NW - 126 + 4 * part, 1)[:, :128] for part in range(2)]
        strip = jnp.where(strip_lane < 4, strips[0], strips[1])
        strip = jnp.concatenate([strip, jnp.zeros((WIDE - NW - 2 * EDGE, 128), f32)], 0).T[:8]
        window = jnp.concatenate([pltpu.roll(strip, 1, 1), strip, pltpu.roll(strip, WIDE - 1, 1), constant], 0).astype(bf16)
        hidden = hidden_of(first_edge[...], window)
        outer = lax.broadcasted_iota(jnp.int32, (NW, WIDE), 0) < 128 if side == 0 else lax.broadcasted_iota(jnp.int32, (NW, WIDE), 0) >= 128
        gone = s == 0 if side == 0 else s == peers - 1
        hidden = jnp.where(jnp.logical_and(outer, gone), 0.0, hidden).astype(bf16)
        mixed = jnp.dot(second_edge[side], hidden, preferred_element_type=f32)
        edge_sum = mixed if edge_sum is None else edge_sum + mixed
    by_dy = []
    for dy in range(3):
        piece = edge_sum[8 * dy : 8 * dy + 8]
        piece = jnp.where(jnp.logical_and(row_lane == EDGE - 1, t == 0), 0.0, piece)
        piece = jnp.where(jnp.logical_and(row_lane == EDGE + NW, t == tiles - 1), 0.0, piece)
        by_dy.append(piece if dy == 1 else pltpu.roll(piece, 1 if dy == 0 else WIDE - 1, 1))
    columns = by_dy[0] + by_dy[1] + by_dy[2]
    columns = jnp.concatenate([columns, jnp.zeros((120, WIDE), f32)], 0).T[EDGE : EDGE + NW]
    out_lane = lax.broadcasted_iota(jnp.int32, (NW, 128), 1)
    for part in range(2):
        halves = [jnp.zeros((NW, 128), f32), jnp.zeros((NW, 128), f32)]
        for dx in range(3):
            sums = jnp.concatenate([mixed_sum[v, pl.ds(16 + 3 * part + dx, NW, stride=8), :] for v in range(2)], 1)
            sums = sums if dx == 1 else pltpu.roll(sums, 1 if dx == 0 else NW - 1, 1)
            halves = [halves[v] + sums[:, v * 128 : (v + 1) * 128] for v in range(2)]
        left = pltpu.roll(columns, (128 - 2 * part) % 128, 1) if part else columns
        right = pltpu.roll(columns, 126 - 4 - 2 * part, 1)
        halves[0] = halves[0] + jnp.where(out_lane < 2, left, 0.0)
        halves[1] = halves[1] + jnp.where(out_lane >= 126, right, 0.0)
        for v in range(2):
            at = slice(v * 128, (v + 1) * 128)
            out_ref[part, :, at] = out_ref[part, :, at] - (halves[v] + b2_ref[part])
    for k, (dt, ds) in enumerate(SIDES):
        @pl.when(exists(dt, ds))
        def _():
            ring_copy(k, dt, ds).wait_send()
            rim_copy(k, dt, ds).wait_send()
    for k, dt, ds in straight:
        @pl.when(exists(dt, ds))
        def _():
            halo_copy(k, dt, ds).wait_send()
    for k, dt, ds in diagonal:
        @pl.when(jnp.logical_and(exists(dt, 0), exists(0, -ds)))
        def _():
            relay_copy(k, dt, ds).wait_send()
    for k, (dy, dz) in enumerate(order):
        amp_copy(k + 1, dy, dz).wait_send()


def sample(specimen, noise, probe, amps, rows, cols, counts, w1, b1, w2, b2):
    tiles, peers = lax.axis_size("tile"), lax.axis_size("scan")
    if peers == 16:
        order, issue, rows_y = ORDER_16, ISSUE_16, 4
    else:
        order, issue, rows_y = [(0, b) for b in range(1, peers)], list(range(peers - 1)), 1
    forward, inverse = dft_matrices()
    one, two = tap_selectors()
    f32, bf16 = jnp.float32, jnp.bfloat16
    smem = pl.BlockSpec(memory_space=pltpu.SMEM)
    vmem = pl.BlockSpec(memory_space=pltpu.VMEM)
    dma = pltpu.SemaphoreType.DMA
    return pl.pallas_call(
        functools.partial(patch_kernel, order, issue, rows_y, tiles, peers),
        out_shape=pltpu.VMEM((2, NW, NW), f32),
        in_specs=[smem, smem, smem, pl.BlockSpec(memory_space=pl.ANY)] + [pl.BlockSpec(memory_space=pl.ANY)] * 5 + [vmem, vmem, vmem, smem, vmem, vmem],
        out_specs=vmem,
        scratch_shapes=[
            pltpu.VMEM((2, NW, NW), f32),
            pltpu.VMEM((2, NW, NW), f32),
            pltpu.VMEM((2, NW, NW), f32),
            pltpu.VMEM((2 * NW, 2 * NW), bf16),
            pltpu.VMEM((2 * NW, 2 * NW), bf16),
            dma((5,)),
            pltpu.VMEM((2, NW + 2 * EDGE, 2 * NW), bf16),
            pltpu.VMEM((2, 8 * (PRIOR_ROWS + 2), 128), f32),
            pltpu.VMEM((2, 8 * PRIOR_ROWS, 128), f32),
            pltpu.VMEM((128, 32), bf16),
            pltpu.VMEM((NW, 32), bf16),
            pltpu.VMEM((24, 128), bf16),
            pltpu.VMEM((2, 24, NW), bf16),
            pltpu.VMEM((peers, CAP, NW, NW), bf16),
            pltpu.VMEM((2, 2 * NW, 2 * NW), bf16),
            pltpu.VMEM((2, 2 * NW, 2 * NW), f32),
            pltpu.VMEM((2, 2 * NW, 2 * NW), bf16),
            pltpu.VMEM((2, 2 * NW, 2 * NW), bf16),
            pltpu.VMEM((2, 2, 2 * NW, HALF), f32),
            pltpu.VMEM((peers, CAP, 2, NW, NW), f32),
            pltpu.VMEM((2 * NW, 2 * NW), bf16),
            pltpu.VMEM((2 * NW, 2 * NW), bf16),
            pltpu.VMEM((peers, 2 * NW, 2 * NW), f32),
            pltpu.VMEM((2 * NW, 2 * NW), f32),
            dma((peers,)), dma((peers,)), dma, dma((8,)), dma((8,)), dma((8,)), dma((8,)), dma((8,)), dma((8,)),
        ],
        compiler_params=pltpu.CompilerParams(collective_id=0, has_side_effects=True, vmem_limit_bytes=62 << 20),
        name="step",
    )(rows, cols, counts, amps, specimen, noise, probe, jnp.asarray(forward), jnp.asarray(inverse),
      w1, b1, w2, b2, jnp.asarray(one), jnp.asarray(two))


def tap_selectors():
    first = np.zeros((3, 18, 32), np.float32)
    second = np.zeros((5, 24, 18), np.float32)
    for c in range(2):
        for dy in range(3):
            for dx in range(3):
                tap = 9 * c + 3 * dy + dx
                first[0, tap, 8 * dy + 3 * c + dx] = 0.5
                first[1, tap, 8 * dy + 4 * c + dx] = 0.5
                first[2, tap, 8 * dy + 4 * c + dx + 1] = 0.5
                second[0, 8 * dy + 3 * c + dx, tap] = 1.0
            for side, half, dx, at in ((0, 0, 0, 0), (0, 1, 1, 0), (0, 1, 0, 1), (1, 0, 2, 0), (1, 0, 1, 1), (1, 1, 2, 1)):
                second[1 + 2 * side + half, 8 * dy + 4 * side + 2 * c + at, 9 * c + 3 * dy + dx] = 1.0
    return first.astype(jnp.bfloat16), second.astype(jnp.bfloat16)


def shards(
    specimen, sampler_noise, probe_field, amplitudes, corner_rows, corner_cols, slot_counts,
    first_weight, first_bias, second_weight, second_bias,
):
    return sample(
        specimen, sampler_noise, probe_field, amplitudes[0, 0],
        corner_rows[0, 0].T, corner_cols[0, 0].T, slot_counts[0, 0],
        first_weight.T, first_bias.reshape(1, -1), second_weight, second_bias,
    )


def solution(mesh):
    return jax.shard_map(
        shards,
        mesh=mesh,
        in_specs=(
            P(None, "tile", "scan"),
            P(None, "tile", "scan"),
            P(),
            P("tile", "scan", None, None, None, None),
            P("tile", "scan", None, None),
            P("tile", "scan", None, None),
            P("tile", "scan", None),
            P(),
            P(),
            P(),
            P(),
        ),
        out_specs=P(None, "tile", "scan"),
        check_vma=False,
    )
```
